512 devices in a mesh: dp: 16 (over z_lo, core), mp: 32 (over x, y, z_hi).
Axes of the slice: x: 4, y: 4, z: 16 (z_hi: 2, z_lo: 8; z = z_hi * 8 + z_lo), core: 2. Of those that a mesh axis runs over, the one named last changes fastest.
Arguments:
- inputs: bfloat16 [8192, 4608], P(('dp', 'mp')), may hold values from -6 to 6
- out_grad: bfloat16 [8192, 4608], P(('dp', 'mp')), may hold values from -6 to 6
- gate_pre: bfloat16 [8192, 36864], P('dp', 'mp'), may hold values from -6 to 6
- up_pre: bfloat16 [8192, 36864], P('dp', 'mp'), may hold values from -6 to 6
- hidden_grad: bfloat16 [8192, 36864], P('dp', 'mp'), may hold values from -4 to 4
- q_start: float32 [36864, 96], P('mp'), may hold values from -0.03125 to 0.03125
Outputs:
- p_factors: float32 [4608, 96], replicated
- q_factors: float32 [36864, 96], P('mp')
The draws below stay inside these ranges and needn't reach their ends.
All inputs are finite; a program needn't handle non-finite values.
Results may differ from the reference program's by a relative error of at most 0.0003.
Values sent between devices are 32-bit elements; how exact they have to be, the bound alone decides.
A program may use at most 64 MiB of HBM per device.

```python
import math
import jax
import jax.numpy as jnp
from jax import lax

D = 4608
FF = 36864
R = 32
TOK = 512
ROWS = 8192
N_DP = 16


def block_levels(key, dims, shards, least, top_value):
    gain = 1.0
    for axis_at, parts in shards:
        steps = jax.random.uniform(jax.random.fold_in(jax.random.fold_in(key, 6), axis_at), (parts,), jnp.float32, least / len(shards), top_value / len(shards))
        gain = gain * jnp.repeat(jnp.exp(steps), dims[axis_at] // parts).reshape((-1,) + (1,) * (len(dims) - 1 - axis_at))
    return gain


def noise(key, extent, deviation, limit, split=(), kind=jnp.bfloat16):
    level = block_levels(key, extent, split, -0.22, 0.18) if split else 1.0
    entries = jax.random.normal(key, extent, jnp.float32) * deviation * level
    return jnp.minimum(jnp.maximum(entries, -limit), limit).astype(kind)


def setup_inputs(seed: int = 0) -> dict:
    key_list = jax.random.split(jax.random.key(seed), 7)
    return {
        "inputs": noise(key_list[0], (ROWS, D), 1.0, 6.0, ((0, 512),)),
        "out_grad": noise(key_list[1], (ROWS, D), 1.0, 6.0, ((0, 512),)),
        "gate_pre": noise(key_list[2], (ROWS, FF), 1.5, 6.0, ((0, 16), (1, 32))),
        "up_pre": noise(key_list[3], (ROWS, FF), 1.0, 6.0, ((0, 16), (1, 32))),
        "hidden_grad": noise(key_list[4], (ROWS, FF), 0.25, 4.0, ((0, 16), (1, 32))),
        "q_start": noise(key_list[5], (FF, 3 * R), FF ** -0.5, 0.03125, ((0, 32),), jnp.float32),
    }


precise = lax.Precision.HIGHEST

def activations(gate_pre, up_pre, hidden_grad):
    gate = gate_pre.astype(jnp.float32)
    upper = up_pre.astype(jnp.float32)
    cotan = hidden_grad.astype(jnp.float32)
    sigmoid = 1.0 / (1.0 + jnp.exp(-gate))
    silu_value = gate * sigmoid
    hidden = silu_value * upper
    gate_grad = cotan * upper * sigmoid * (1.0 + gate * (1.0 - sigmoid))
    up_grad = cotan * silu_value
    return (gate_grad, up_grad, hidden)

def lower_inverse(lower):
    columns = lower.shape[-1]
    identity = jnp.eye(columns, dtype=jnp.float32)
    done_rows = []
    for index in range(columns):
        next_row = jnp.broadcast_to(identity[index], (lower.shape[0], columns))
        if index > 0:
            earlier = jnp.stack(done_rows, axis=1)
            next_row = next_row - jnp.einsum('kj,kjc->kc', lower[:, index, :index], earlier, precision=precise)
        done_rows.append(next_row / lower[:, index, index:index + 1])
    return jnp.stack(done_rows, axis=1)

def gram_blocks(factor, columns):
    blocks = factor.reshape(factor.shape[0], 3, columns)
    return jnp.einsum('dkc,dke->kce', blocks, blocks, precision=precise)

def orthonormal(factor, grams, columns):
    lower = jnp.linalg.cholesky(grams)
    inverse = lower_inverse(lower)
    blocks = factor.reshape(factor.shape[0], 3, columns)
    basis = jnp.einsum('dkc,kjc->dkj', blocks, inverse, precision=precise)
    return basis.reshape(factor.shape[0], 3 * columns)

def three_products(left_one, left_two, right_blocks, columns, form):
    return jnp.concatenate([jnp.einsum(form, left_one[0], right_blocks[:, :columns], precision=precise), jnp.einsum(form, left_one[1], right_blocks[:, columns:2 * columns], precision=precise), jnp.einsum(form, left_two, right_blocks[:, 2 * columns:], precision=precise)], axis=1)

def reference(inputs, out_grad, gate_pre, up_pre, hidden_grad, q_start):
    items = (inputs.reshape(N_DP, TOK, D), out_grad.reshape(N_DP, TOK, D), gate_pre.reshape(N_DP, TOK, FF), up_pre.reshape(N_DP, TOK, FF), hidden_grad.reshape(N_DP, TOK, FF))

    def factor_step(running, replica):
        in_rows, grad_rows, gate_rows, up_rows, cotan_rows = replica
        gate_grad, up_grad, hidden = activations(gate_rows, up_rows, cotan_rows)
        mixture = three_products((gate_grad, up_grad), hidden, q_start, R, 'tf,fc->tc')
        in_float = in_rows.astype(jnp.float32)
        grad_float = grad_rows.astype(jnp.float32)
        term = three_products((in_float, in_float), grad_float, mixture, R, 'td,tc->dc')
        return (running + term, None)
    summed, _ = lax.scan(factor_step, jnp.zeros((D, 3 * R), jnp.float32), items)
    factor = summed / N_DP
    basis = orthonormal(factor, gram_blocks(factor, R), R)

    def basis_step(running, replica):
        in_rows, grad_rows, gate_rows, up_rows, cotan_rows = replica
        gate_grad, up_grad, hidden = activations(gate_rows, up_rows, cotan_rows)
        in_float = in_rows.astype(jnp.float32)
        grad_float = grad_rows.astype(jnp.float32)
        image = three_products((in_float, in_float), grad_float, basis, R, 'td,dc->tc')
        term = three_products((gate_grad, up_grad), hidden, image, R, 'tf,tc->fc')
        return (running + term, None)
    new_sum, _ = lax.scan(basis_step, jnp.zeros((FF, 3 * R), jnp.float32), items)
    return (basis * math.sqrt(D), new_sum / N_DP)
```

```python
import functools
import math

import jax
import jax.numpy as jnp
from jax import lax
from jax.experimental import pallas as pl
from jax.experimental.pallas import tpu as pltpu
from jax.sharding import PartitionSpec as P

MESH = pl.DeviceIdType.MESH
F32 = jnp.float32
BF16 = jnp.bfloat16
HIGH = lax.Precision.HIGHEST

D = 4608
TOK = 512
FFL = 1152
ROWS = 16
RANK = 32
W = 3 * RANK
LANES = 128
SIDE = 4
PLANE = SIDE * SIDE
ZLO = 8
DEPTH = 16
GROUPS = 16

PB = 224
PB_USED = 216
PS = PB // SIDE
ZROWS = 64
QB = 448
QB_USED = 432
QS = QB // ZLO


def split(value):
    high = value.astype(BF16)
    low = (value - high.astype(F32)).astype(BF16)
    return high, low


def mm(left, right):
    return lax.dot_general(
        left, right, (((1,), (0,)), ((), ())), preferred_element_type=F32
    )


def mm_t(left, right, precision=None):
    return lax.dot_general(
        left,
        right,
        (((1,), (1,)), ((), ())),
        preferred_element_type=F32,
        precision=precision,
    )


def pieces(start, count, used):
    out = []
    at = start
    while at < start + count:
        block, row = divmod(at, used)
        here = min(used - row, start + count - at)
        out.append((block, row, at - start, here))
        at += here
    return out


def kernel(
    in_ref,
    og_ref,
    gate_ref,
    up_ref,
    cot_ref,
    q_ref,
    p_out,
    q_out,
    acts,
    qs,
    mpart,
    mrecv,
    m32,
    mzrecv,
    pb,
    pcrecv,
    r1,
    s1,
    r2,
    s2,
    r3,
    s3,
    pf,
    ptf,
    xs,
    pfin,
    img,
    qb,
    qcrecv,
    qh,
    qr,
    qf,
    ms,
    mr,
    mzs,
    mzr,
    pcs,
    pcr,
    r1s,
    r1r,
    r2s,
    r2r,
    r3s,
    r3r,
    g3s,
    g3r,
    g2s,
    g2r,
    g1s,
    g1r,
    gcs,
    gcr,
    izs,
    izr,
    ixs,
    ixr,
    qcs,
    qcr,
    qrs,
    qrr,
    qgs,
    qgr,
    qds,
    qdr,
    outs,
):
    dp, mp = lax.axis_index("dp"), lax.axis_index("mp")
    core, zl = lax.rem(dp, 2), lax.div(dp, 2)
    zh, plane = lax.rem(mp, 2), lax.div(mp, 2)
    xx, yy = lax.div(plane, SIDE), lax.rem(plane, SIDE)
    z = zh * ZLO + zl
    sibling = (zl * 2 + 1 - core, mp)
    opposite = (dp, plane * 2 + 1 - zh)

    def plane_peer(index):
        return (dp, index * 2 + zh)

    def z_peer(index):
        return (lax.rem(index, ZLO) * 2 + core, plane * 2 + lax.div(index, ZLO))

    def side_peer(axis, index):
        along_x = (dp, (index * SIDE + yy) * 2 + zh)
        along_y = (dp, (xx * SIDE + index) * 2 + zh)
        return along_x if axis == 0 else along_y

    def side(axis):
        return xx if axis == 0 else yy

    def remote(src, dst, send, recv, to):
        return pltpu.make_async_remote_copy(
            src_ref=src,
            dst_ref=dst,
            send_sem=send,
            recv_sem=recv,
            device_id=to,
            device_id_type=MESH,
        )

    def around(count, body):
        def step(index, carry):
            body(index)
            return carry

        lax.fori_loop(1, count, step, 0)

    barrier = pltpu.get_barrier_semaphore()

    def greet(d):
        pl.semaphore_signal(
            barrier,
            inc=1,
            device_id=plane_peer(lax.rem(plane + d, PLANE)),
            device_id_type=MESH,
        )
        pl.semaphore_signal(
            barrier,
            inc=1,
            device_id=z_peer(lax.rem(z + d, DEPTH)),
            device_id_type=MESH,
        )

    around(DEPTH, greet)
    pl.semaphore_signal(barrier, inc=1, device_id=sibling, device_id_type=MESH)

    def activate(i, carry):
        rows = pl.ds(pl.multiple_of(i * 16, 16), 16)
        low_rows = pl.ds(pl.multiple_of(TOK + i * 16, 16), 16)
        g = gate_ref[rows, :].astype(F32)
        u = up_ref[rows, :].astype(F32)
        e = cot_ref[rows, :].astype(F32)
        s = 1.0 / (1.0 + jnp.exp(-g))
        silu = g * s
        values = (e * u * s * (1.0 + g * (1.0 - s)), e * silu, silu * u)
        for k, value in enumerate(values):
            high, low = split(value)
            acts[k, rows, :] = high
            acts[k, low_rows, :] = low
        return carry

    lax.fori_loop(0, TOK // 16, activate, 0)

    q_high, q_low = split(q_ref[...])
    qs[...] = jnp.zeros_like(qs)
    qs[:, 0:W] = q_high
    qs[:, LANES : LANES + W] = q_low

    lane = lax.broadcasted_iota(jnp.int32, (TOK, LANES), 1)
    for k in range(3):
        first = mm(acts[k, 0:TOK, :], qs[...])
        second = mm(acts[k, TOK : 2 * TOK, :], qs[:, 0:LANES])
        both = first[:, 0:LANES] + first[:, LANES:] + second
        if k == 0:
            mpart[...] = both
        else:
            mpart[...] = jnp.where(lane >= k * RANK, both, mpart[...])

    pl.semaphore_wait(barrier, 2 * (DEPTH - 1) + 1)

    def m_copy(d):
        to = lax.rem(plane + d, PLANE)
        return remote(
            mpart.at[pl.ds(pl.multiple_of(to * 32, 32), 32)],
            mrecv.at[d - 1],
            ms.at[d - 1],
            mr.at[d - 1],
            plane_peer(to),
        )

    around(PLANE, lambda d: m_copy(d).start())
    around(PLANE, lambda d: m_copy(d).wait_recv())
    m32[...] = mpart[pl.ds(pl.multiple_of(plane * 32, 32), 32), :] + jnp.sum(
        mrecv[...], axis=0
    )
    mz_copy = remote(
        m32.at[pl.ds(pl.multiple_of((1 - zh) * 16, 16), 16)],
        mzrecv,
        mzs.at[0],
        mzr.at[0],
        opposite,
    )
    mz_copy.start()
    mz_copy.wait_recv()
    mixture = m32[pl.ds(pl.multiple_of(zh * 16, 16), 16), :] + mzrecv[...]
    m_high, m_low = split(mixture * (1.0 / GROUPS))
    m_both = jnp.concatenate([m_high.astype(F32), m_low.astype(F32)], axis=0)
    m_turned = m_both.T.astype(BF16)

    def p_blocks(half, portion):
        columns = pl.ds(
            pl.multiple_of((half * 2 + portion) * (9 * LANES), LANES), 9 * LANES
        )
        b_in = in_ref[:, columns]
        b_out = og_ref[:, columns]
        top = mm(m_turned[0 : 2 * RANK], jnp.concatenate([b_in, b_in], axis=0))
        low = mm(m_turned[2 * RANK : W], jnp.concatenate([b_out, b_out], axis=0))
        base = (half * 2 + portion) * SIDE
        for tile in range(9):
            at = slice(tile * LANES, (tile + 1) * LANES)
            for part, start in ((top[:, at], 0), (low[:, at], 2 * RANK)):
                for block, row, first, count in pieces(
                    tile * W + start, part.shape[0], PB_USED
                ):
                    pb[base + block, row : row + count, :] = part[first : first + count]
        for block in range(SIDE):
            pb[base + block, PB_USED:PB, :] = jnp.zeros((PB - PB_USED, LANES), F32)

    def pc_copy(index):
        return remote(
            pb.at[(1 - core) * 8 + index],
            pcrecv.at[index],
            pcs.at[index],
            pcr.at[index],
            sibling,
        )

    for portion in range(2):
        p_blocks(1 - core, portion)
        for f in range(SIDE):
            pc_copy(portion * SIDE + f).start()
    for portion in range(2):
        p_blocks(core, portion)

    def r1_copy(portion, d):
        to = lax.rem(side(portion) + d, SIDE)
        index = portion * SIDE + to
        at = portion * 3 + d - 1
        return remote(
            pb.at[core * 8 + index],
            r1.at[at],
            r1s.at[at],
            r1r.at[at],
            side_peer(portion, to),
        )

    for d in (2, 1, 3, 0):
        for portion in range(2):
            index = portion * SIDE + lax.rem(side(portion) + d, SIDE)
            pc_copy(index).wait_recv()
            pb[core * 8 + index] = pb[core * 8 + index] + pcrecv[index]
            if d:
                r1_copy(portion, d).start()

    def r2_copy(portion, d):
        axis = 1 - portion
        to = lax.rem(side(axis) + d, SIDE)
        at = portion * 3 + d - 1
        return remote(
            s1.at[portion, pl.ds(pl.multiple_of(to * PS, 8), PS)],
            r2.at[at],
            r2s.at[at],
            r2r.at[at],
            side_peer(axis, to),
        )

    for portion in range(2):
        for d in (1, 3, 2):
            r1_copy(portion, d).wait_recv()
        s1[portion] = (
            pb[core * 8 + portion * SIDE + side(portion)]
            + r1[portion * 3]
            + r1[portion * 3 + 1]
            + r1[portion * 3 + 2]
        )
        for d in (2, 1, 3):
            r2_copy(portion, d).start()
    for portion in range(2):
        for d in (1, 3, 2):
            r2_copy(portion, d).wait_recv()
        own = pl.ds(pl.multiple_of(side(1 - portion) * PS, 8), PS)
        s2[portion * ZROWS : portion * ZROWS + PS, :] = (
            s1[portion, own, :]
            + r2[portion * 3]
            + r2[portion * 3 + 1]
            + r2[portion * 3 + 2]
        )
        s2[portion * ZROWS + PS : (portion + 1) * ZROWS, :] = jnp.zeros(
            (ZROWS - PS, LANES), F32
        )

    def r3_copy(d):
        to = lax.rem(z + d, DEPTH)
        return remote(
            s2.at[pl.ds(pl.multiple_of(to * 8, 8), 8)],
            r3.at[d - 1],
            r3s.at[d - 1],
            r3r.at[d - 1],
            z_peer(to),
        )

    around(DEPTH, lambda d: r3_copy(d).start())
    around(DEPTH, lambda d: r3_copy(d).wait_recv())
    z_own = pl.ds(pl.multiple_of(z * 8, 8), 8)
    s3[z_own, :] = s2[z_own, :] + jnp.sum(r3[...], axis=0)

    def g3_copy(d):
        return remote(
            s3.at[z_own],
            s3.at[z_own],
            g3s.at[d - 1],
            g3r.at[d - 1],
            z_peer(lax.rem(z + d, DEPTH)),
        )

    around(DEPTH, lambda d: g3_copy(d).start())
    around(DEPTH, lambda d: g3_copy(d).wait_recv())

    def own_block(portion):
        return (core * 2 + portion) * SIDE + side(portion)

    def g2_copy(portion, d):
        axis = 1 - portion
        at = portion * 3 + d - 1
        rows = pl.ds(pl.multiple_of(side(axis) * PS, 8), PS)
        return remote(
            pf.at[own_block(portion), rows],
            pf.at[own_block(portion), rows],
            g2s.at[at],
            g2r.at[at],
            side_peer(axis, lax.rem(side(axis) + d, SIDE)),
        )

    for portion in range(2):
        rows = pl.ds(pl.multiple_of(side(1 - portion) * PS, 8), PS)
        pf[own_block(portion), rows, :] = s3[
            portion * ZROWS : portion * ZROWS + PS, :
        ]
        for d in (2, 1, 3):
            g2_copy(portion, d).start()

    def g1_copy(portion, d):
        at = portion * 3 + d - 1
        return remote(
            pf.at[own_block(portion)],
            pf.at[own_block(portion)],
            g1s.at[at],
            g1r.at[at],
            side_peer(portion, lax.rem(side(portion) + d, SIDE)),
        )

    def gc_copy(portion, d):
        f = lax.rem(side(portion) + SIDE - d, SIDE)
        index = portion * SIDE + f
        block = core * 8 + index
        return remote(
            pf.at[block], pf.at[block], gcs.at[index], gcr.at[index], sibling
        )

    for portion in range(2):
        for d in (1, 3, 2):
            g2_copy(portion, d).wait_recv()
        for d in (2, 1, 3):
            g1_copy(portion, d).start()
        gc_copy(portion, 0).start()
    for d in (1, 3, 2):
        for portion in range(2):
            g1_copy(portion, d).wait_recv()
            gc_copy(portion, d).start()
    for d in range(SIDE):
        for portion in range(2):
            gc_copy(portion, d).wait_recv()

    for tile in range(D // LANES):
        at = slice(tile * LANES, (tile + 1) * LANES)
        parts = [
            pf[block, row : row + count, :]
            for block, row, _, count in pieces(tile * W, W, PB_USED)
        ]
        whole = parts[0] if len(parts) == 1 else jnp.concatenate(parts, axis=0)
        ptf[:, at] = whole
        high, low = split(whole)
        xs[0:W, at] = high
        xs[LANES : LANES + W, at] = low
    xs[W:LANES, :] = jnp.zeros((LANES - W, D), BF16)
    xs[LANES + W : LANES + W + ROWS, :] = in_ref[...]
    xs[LANES + W + ROWS :, :] = og_ref[...]
    products = mm_t(xs[...], xs[...])
    near, far = products[:, 0:LANES], products[:, LANES:]
    gram = near[0:LANES] + near[LANES:] + far[0:LANES] + far[LANES:]
    onto = near[LANES + W :] + far[LANES + W :]

    row_at = lax.broadcasted_iota(jnp.int32, (RANK, LANES), 0)
    lane_at = lax.broadcasted_iota(jnp.int32, (RANK, LANES), 1)
    inverse = []
    left = [gram[k * RANK : (k + 1) * RANK] for k in range(3)]
    right = [(lane_at == row_at + k * RANK).astype(F32) for k in range(3)]
    for j in range(RANK - 1):
        for k in range(3):
            at = k * RANK + j
            pivot = left[k][j : j + 1, at : at + 1]
            column = left[k][:, at : at + 1] / pivot
            factor = jnp.where(row_at > j, column, 0.0)
            left[k] = left[k] - factor * left[k][j : j + 1, :]
            right[k] = right[k] - factor * right[k][j : j + 1, :]
    for k in range(3):
        diagonal = jnp.sum(
            jnp.where(lane_at == row_at + k * RANK, left[k], 0.0), axis=1, keepdims=True
        )
        inverse.append(right[k] / jnp.sqrt(diagonal))
    inverse.append(jnp.zeros((RANK, LANES), F32))
    inverse = jnp.concatenate(inverse, axis=0)

    token_lane = lax.broadcasted_iota(jnp.int32, (ROWS, LANES), 1)
    onto = jnp.where(
        token_lane < 2 * RANK,
        onto[0:ROWS],
        jnp.where(token_lane < W, onto[ROWS:], 0.0),
    )
    image = mm_t(onto, inverse, HIGH) * (1.0 / GROUPS)

    img_own = pl.ds(pl.multiple_of(plane * 32 + zh * 16, 16), 16)
    img[img_own, :] = image
    iz_copy = remote(img.at[img_own], img.at[img_own], izs.at[0], izr.at[0], opposite)
    iz_copy.start()
    iz_copy.wait_recv()
    img_pair = pl.ds(pl.multiple_of(plane * 32, 32), 32)

    def ix_copy(d):
        return remote(
            img.at[img_pair],
            img.at[img_pair],
            ixs.at[d - 1],
            ixr.at[d - 1],
            plane_peer(lax.rem(plane + d, PLANE)),
        )

    around(PLANE, lambda d: ix_copy(d).start())

    def left_factor(tile, carry):
        at = pl.ds(pl.multiple_of(tile * LANES, LANES), LANES)
        turned = ptf[:, at].T
        pfin[at, :] = mm_t(turned, inverse[0:W, 0:W] * math.sqrt(D), HIGH)
        return carry

    lax.fori_loop(0, D // LANES, left_factor, 0)
    out_copy = pltpu.make_async_copy(pfin, p_out, outs.at[0])
    out_copy.start()

    around(PLANE, lambda d: ix_copy(d).wait_recv())

    img_high, img_low = split(img[...].T)
    for half in range(2):
        qb[half, QB_USED:QB, :] = jnp.zeros((QB - QB_USED, LANES), F32)
    for k in range(3):
        rows = slice(k * RANK, (k + 1) * RANK)
        both = jnp.concatenate([img_high[rows], img_low[rows]], axis=0)
        first = mm(both, acts[k, 0:TOK, :])
        second = mm(img_high[rows], acts[k, TOK : 2 * TOK, :])
        share = first[0:RANK] + first[RANK:] + second
        for tile in range(FFL // LANES):
            part = share[:, tile * LANES : (tile + 1) * LANES]
            for half, row, start, count in pieces(
                tile * W + k * RANK, RANK, QB_USED
            ):
                qb[half, row : row + count, :] = part[start : start + count]

    qc_copy = remote(qb.at[1 - core], qcrecv, qcs.at[0], qcr.at[0], sibling)
    qc_copy.start()
    qc_copy.wait_recv()
    qh[...] = qb[core] + qcrecv[...]

    def zl_peer(index):
        return (index * 2 + core, mp)

    def qr_copy(d):
        to = lax.rem(zl + d, ZLO)
        return remote(
            qh.at[pl.ds(pl.multiple_of(to * QS, 8), QS)],
            qr.at[d - 1],
            qrs.at[d - 1],
            qrr.at[d - 1],
            zl_peer(to),
        )

    around(ZLO, lambda d: qr_copy(d).start())
    around(ZLO, lambda d: qr_copy(d).wait_recv())
    q_own = pl.ds(pl.multiple_of(zl * QS, 8), QS)
    qf[core, q_own, :] = qh[q_own, :] + jnp.sum(qr[...], axis=0)

    def qg_copy(d):
        return remote(
            qf.at[core, q_own],
            qf.at[core, q_own],
            qgs.at[d - 1],
            qgr.at[d - 1],
            zl_peer(lax.rem(zl + d, ZLO)),
        )

    def qd_copy(d):
        rows = pl.ds(pl.multiple_of(lax.rem(zl + ZLO - d, ZLO) * QS, 8), QS)
        return remote(
            qf.at[core, rows], qf.at[core, rows], qds.at[d], qdr.at[d], sibling
        )

    around(ZLO, lambda d: qg_copy(d).start())
    qd_copy(0).start()

    def hand_on(d):
        qg_copy(d).wait_recv()
        qd_copy(d).start()

    around(ZLO, hand_on)
    qd_copy(0).wait_recv()
    around(ZLO, lambda d: qd_copy(d).wait_recv())

    for tile in range(FFL // LANES):
        parts = [
            qf[half, row : row + count, :]
            for half, row, _, count in pieces(tile * W, W, QB_USED)
        ]
        whole = parts[0] if len(parts) == 1 else jnp.concatenate(parts, axis=0)
        q_out[tile * LANES : (tile + 1) * LANES, :] = whole.T

    around(PLANE, lambda d: m_copy(d).wait_send())
    mz_copy.wait_send()
    for index in range(8):
        pc_copy(index).wait_send()
    for portion in range(2):
        for d in (1, 2, 3):
            r1_copy(portion, d).wait_send()
            r2_copy(portion, d).wait_send()
            g2_copy(portion, d).wait_send()
            g1_copy(portion, d).wait_send()
        for d in range(SIDE):
            gc_copy(portion, d).wait_send()
    around(DEPTH, lambda d: r3_copy(d).wait_send())
    around(DEPTH, lambda d: g3_copy(d).wait_send())
    iz_copy.wait_send()
    around(PLANE, lambda d: ix_copy(d).wait_send())
    qc_copy.wait_send()
    around(ZLO, lambda d: qr_copy(d).wait_send())
    around(ZLO, lambda d: qg_copy(d).wait_send())
    qd_copy(0).wait_send()
    around(ZLO, lambda d: qd_copy(d).wait_send())
    out_copy.wait()


def on_device(inputs, out_grad, gate_pre, up_pre, hidden_grad, q_start):
    vmem = pl.BlockSpec(memory_space=pltpu.VMEM)
    buffers = [
        pltpu.VMEM((3, 2 * TOK, FFL), BF16),
        pltpu.VMEM((FFL, 2 * LANES), BF16),
        pltpu.VMEM((TOK, LANES), F32),
        pltpu.VMEM((PLANE - 1, 32, LANES), F32),
        pltpu.VMEM((32, LANES), F32),
        pltpu.VMEM((16, LANES), F32),
        pltpu.VMEM((16, PB, LANES), F32),
        pltpu.VMEM((8, PB, LANES), F32),
        pltpu.VMEM((6, PB, LANES), F32),
        pltpu.VMEM((2, PB, LANES), F32),
        pltpu.VMEM((6, PS, LANES), F32),
        pltpu.VMEM((2 * ZROWS, LANES), F32),
        pltpu.VMEM((DEPTH - 1, 8, LANES), F32),
        pltpu.VMEM((2 * ZROWS, LANES), F32),
        pltpu.VMEM((16, PB, LANES), F32),
        pltpu.VMEM((W, D), F32),
        pltpu.VMEM((2 * LANES, D), BF16),
        pltpu.VMEM((D, W), F32),
        pltpu.VMEM((TOK, LANES), F32),
        pltpu.VMEM((2, QB, LANES), F32),
        pltpu.VMEM((QB, LANES), F32),
        pltpu.VMEM((QB, LANES), F32),
        pltpu.VMEM((ZLO - 1, QS, LANES), F32),
        pltpu.VMEM((2, QB, LANES), F32),
    ]
    counts = [15, 15, 1, 1, 8, 8, 6, 6, 6, 6, 15, 15, 15, 15, 6, 6, 6, 6, 8, 8]
    counts += [1, 1, 15, 15, 1, 1, 7, 7, 7, 7, 8, 8, 1]
    flags = [pltpu.SemaphoreType.DMA((count,)) for count in counts]
    return pl.pallas_call(
        kernel,
        out_shape=(
            jax.ShapeDtypeStruct((D, W), F32),
            jax.ShapeDtypeStruct((FFL, W), F32),
        ),
        in_specs=[vmem] * 6,
        out_specs=(pl.BlockSpec(memory_space=pl.ANY), vmem),
        scratch_shapes=buffers + flags,
        compiler_params=pltpu.CompilerParams(
            collective_id=0, has_side_effects=True, vmem_limit_bytes=56 * 2**20
        ),
        name="power_step",
    )(inputs, out_grad, gate_pre, up_pre, hidden_grad, q_start)


def solution(mesh):
    in_specs = (
        P(("dp", "mp"), None),
        P(("dp", "mp"), None),
        P("dp", "mp"),
        P("dp", "mp"),
        P("dp", "mp"),
        P("mp", None),
    )
    out_specs = (P(), P("mp", None))
    return jax.shard_map(
        on_device, mesh=mesh, in_specs=in_specs, out_specs=out_specs, check_vma=False
    )
```

```python
import functools
import math

import jax
import jax.numpy as jnp
from jax import lax
from jax.experimental import pallas as pl
from jax.experimental.pallas import tpu as pltpu
from jax.sharding import PartitionSpec as P

MESH = pl.DeviceIdType.MESH
F32 = jnp.float32
BF16 = jnp.bfloat16
HIGH = lax.Precision.HIGHEST

D = 4608
TOK = 512
FFL = 1152
ROWS = 16
RANK = 32
W = 3 * RANK
LANES = 128
SIDE = 4
PLANE = SIDE * SIDE
ZLO = 8
DEPTH = 16
GROUPS = 16

TILES = D // LANES
NEAR = 2 * PLANE
SHARE = 128
QB = 448
QB_USED = 432
QS = QB // ZLO


def split(value):
    high = value.astype(BF16)
    low = (value - high.astype(F32)).astype(BF16)
    return high, low


def mm(left, right, precision=None):
    return lax.dot_general(
        left,
        right,
        (((1,), (0,)), ((), ())),
        preferred_element_type=F32,
        precision=precision,
    )


def mm_t(left, right, precision=None):
    return lax.dot_general(
        left,
        right,
        (((1,), (1,)), ((), ())),
        preferred_element_type=F32,
        precision=precision,
    )


def tiles_of(core, plane):
    x, y = divmod(plane, SIDE)
    if x == y:
        first = 12 + 6 * x + 3 * core
        return (
            [(1, first + i) for i in range(3)],
            [(32 * i, 2, first + i) for i in range(3)],
        )
    at = plane - plane // (SIDE + 1) - 1
    if core == 0:
        return (
            [(0, 3 * at), (0, 3 * at + 1)],
            [
                (0, 0, 3 * at),
                (32, 1, 3 * at),
                (64, 0, 3 * at + 1),
                (96, 1, 3 * at + 1),
            ],
        )
    return (
        [(0, 3 * at + 2), (1, at)],
        [(0, 0, 3 * at + 2), (32, 1, 3 * at + 2), (64, 2, at)],
    )


def staged(core, plane):
    x, y = lax.div(plane, SIDE), lax.rem(plane, SIDE)
    at = plane - lax.div(plane, SIDE + 1) - 1
    return jnp.where(x == y, 48 + 6 * x + 3 * core, 4 * at + 2 * core)


def pieces(start, count, used):
    out = []
    at = start
    while at < start + count:
        block, row = divmod(at, used)
        here = min(used - row, start + count - at)
        out.append((block, row, at - start, here))
        at += here
    return out


def kernel(
    in_ref,
    og_ref,
    gate_ref,
    up_ref,
    cot_ref,
    q_ref,
    p_out,
    q_out,
    gate_in,
    up_in,
    cot_in,
    acts,
    qs,
    mpart,
    mrecv,
    m32,
    mzrecv,
    bst,
    bt,
    bs,
    mall,
    yb,
    s2,
    r3,
    s3,
    zb,
    zs,
    ub,
    urecv,
    gmine,
    gsib,
    gall,
    ghalf,
    pf,
    ptf,
    pfin,
    img,
    qb,
    qcrecv,
    qh,
    qr,
    qf,
    loads,
    ms,
    mr,
    mzs,
    mzr,
    bsend,
    brecv,
    mas,
    mar,
    r3s,
    r3r,
    g3s,
    g3r,
    us,
    ur,
    gss,
    gsr,
    gps,
    gpr,
    ghs,
    ghr,
    g2s,
    g2r,
    g1s,
    g1r,
    gcs,
    gcr,
    izs,
    izr,
    ixs,
    ixr,
    qcs,
    qcr,
    qrs,
    qrr,
    qgs,
    qgr,
    qds,
    qdr,
    outs,
):
    dp, mp = lax.axis_index("dp"), lax.axis_index("mp")
    core, zl = lax.rem(dp, 2), lax.div(dp, 2)
    zh, plane = lax.rem(mp, 2), lax.div(mp, 2)
    xx, yy = lax.div(plane, SIDE), lax.rem(plane, SIDE)
    z = zh * ZLO + zl
    on_diagonal = xx == yy
    sibling = (zl * 2 + 1 - core, mp)
    opposite = (dp, plane * 2 + 1 - zh)

    def plane_peer(index):
        return (dp, index * 2 + zh)

    def z_peer(index):
        return (lax.rem(index, ZLO) * 2 + core, plane * 2 + lax.div(index, ZLO))

    def side_peer(axis, index):
        along_x = (dp, (index * SIDE + yy) * 2 + zh)
        along_y = (dp, (xx * SIDE + index) * 2 + zh)
        return along_x if axis == 0 else along_y

    def side(axis):
        return xx if axis == 0 else yy

    def after(e):
        return (
            lax.rem(core + lax.div(e, PLANE), 2),
            lax.rem(plane + lax.rem(e, PLANE), PLANE),
        )

    def before(e):
        return (
            lax.rem(core + lax.div(e, PLANE), 2),
            lax.rem(plane + PLANE - lax.rem(e, PLANE), PLANE),
        )

    def near_peer(place):
        return (zl * 2 + place[0], place[1] * 2 + zh)

    def remote(src, dst, send, recv, to):
        return pltpu.make_async_remote_copy(
            src_ref=src,
            dst_ref=dst,
            send_sem=send,
            recv_sem=recv,
            device_id=to,
            device_id_type=MESH,
        )

    def around(count, body):
        def step(index, carry):
            body(index)
            return carry

        lax.fori_loop(1, count, step, 0)

    pending = []

    def send(make, count):
        around(count, lambda d: make(d).start())
        pending.append(lambda: around(count, lambda d: make(d).wait_send()))

    def send_one(copy):
        copy.start()
        pending.append(copy.wait_send)

    def receive(make, count):
        around(count, lambda d: make(d).wait_recv())

    def finish():
        for wait in pending:
            wait()

    barrier = pltpu.get_barrier_semaphore()

    def greet(to):
        pl.semaphore_signal(barrier, inc=1, device_id=to, device_id_type=MESH)

    around(DEPTH, lambda d: greet(z_peer(lax.rem(z + d, DEPTH))))
    around(NEAR, lambda e: greet(near_peer(after(e))))

    quarter = TOK // 4

    def load(part, which):
        rows = pl.ds(part * quarter, quarter)
        src, dst = (
            (gate_ref, gate_in),
            (up_ref, up_in),
            (cot_ref, cot_in),
        )[which]
        return pltpu.make_async_copy(
            src.at[rows], dst.at[rows], loads.at[part * 3 + which]
        )

    for part in range(4):
        for which in range(3):
            load(part, which).start()

    place = 0
    for chip_type in (False, True):
        for chip in range(PLANE):
            if (chip // SIDE == chip % SIDE) != chip_type:
                continue
            for of_core in range(2):
                for array, tile in tiles_of(of_core, chip)[0]:
                    source = (in_ref, og_ref)[array]
                    bst[place] = source[:, tile * LANES : (tile + 1) * LANES].astype(F32)
                    place += 1

    def activate(i, carry):
        rows = pl.ds(pl.multiple_of(i * 16, 16), 16)
        low_rows = pl.ds(pl.multiple_of(TOK + i * 16, 16), 16)
        g = gate_in[rows, :].astype(F32)
        u = up_in[rows, :].astype(F32)
        e = cot_in[rows, :].astype(F32)
        s = 1.0 / (1.0 + jnp.exp(-g))
        silu = g * s
        values = (e * u * s * (1.0 + g * (1.0 - s)), e * silu, silu * u)
        for k, value in enumerate(values):
            high, low = split(value)
            acts[k, rows, :] = high
            acts[k, low_rows, :] = low
        return carry

    def b_copy(e, count):
        to = after(e)
        return remote(
            bst.at[pl.ds(staged(*to), count)],
            bt.at[e, pl.ds(0, count)],
            bsend.at[e - 1],
            brecv.at[e - 1],
            near_peer(to),
        )

    def b_each(e, act, diagonal):
        @pl.when(diagonal)
        def _():
            act(b_copy(e, 3))

        @pl.when(jnp.logical_not(diagonal))
        def _():
            act(b_copy(e, 2))

    def to_diagonal(e):
        chip = after(e)[1]
        return lax.div(chip, SIDE) == lax.rem(chip, SIDE)

    steps = quarter // 16
    for part in range(4):
        for which in range(3):
            load(part, which).wait()
        lax.fori_loop(part * steps, (part + 1) * steps, activate, 0)
        if part == 1:
            pl.semaphore_wait(barrier, DEPTH - 1 + NEAR - 1)
            around(NEAR, lambda e: b_each(e, lambda c: c.start(), to_diagonal(e)))
            pending.append(
                lambda: around(
                    NEAR, lambda e: b_each(e, lambda c: c.wait_send(), to_diagonal(e))
                )
            )

    q_high, q_low = split(q_ref[...])
    qs[...] = jnp.zeros_like(qs)
    qs[0:W, :] = q_high
    qs[LANES : LANES + W, :] = q_low

    lane = lax.broadcasted_iota(jnp.int32, (TOK, LANES), 1)
    for k in range(3):
        first = mm_t(acts[k, 0:TOK, :], qs[...])
        second = mm_t(acts[k, TOK : 2 * TOK, :], qs[0:LANES, :])
        both = first[:, 0:LANES] + first[:, LANES:] + second
        if k == 0:
            mpart[...] = both
        else:
            mpart[...] = jnp.where(lane >= k * RANK, both, mpart[...])

    def m_copy(d):
        to = lax.rem(plane + d, PLANE)
        return remote(
            mpart.at[pl.ds(pl.multiple_of(to * 32, 32), 32)],
            mrecv.at[d - 1],
            ms.at[d - 1],
            mr.at[d - 1],
            plane_peer(to),
        )

    send(m_copy, PLANE)
    receive(m_copy, PLANE)
    m32[...] = mpart[pl.ds(pl.multiple_of(plane * 32, 32), 32), :] + jnp.sum(
        mrecv[...], axis=0
    )
    mz_copy = remote(
        m32.at[pl.ds(pl.multiple_of((1 - zh) * 16, 16), 16)],
        mzrecv,
        mzs.at[0],
        mzr.at[0],
        opposite,
    )
    send_one(mz_copy)
    mz_copy.wait_recv()
    mixture = m32[pl.ds(pl.multiple_of(zh * 16, 16), 16), :] + mzrecv[...]
    mall[0] = mixture * (1.0 / GROUPS)

    def ma_copy(e):
        return remote(
            mall.at[0], mall.at[e], mas.at[e - 1], mar.at[e - 1], near_peer(after(e))
        )

    send(ma_copy, NEAR)

    own_tiles = staged(core, plane)
    for tile in range(2):
        bt[0, tile] = bst[own_tiles + tile]

    @pl.when(on_diagonal)
    def _():
        bt[0, 2] = bst[own_tiles + 2]

    around(NEAR, lambda e: b_each(e, lambda c: c.wait_recv(), on_diagonal))

    def round_rows(e, carry):
        rows = pl.ds(pl.multiple_of(e * ROWS, ROWS), ROWS)
        for tile in range(2):
            bs[rows, tile * LANES : (tile + 1) * LANES] = bt[e, tile].astype(BF16)

        @pl.when(on_diagonal)
        def _():
            bs[rows, 2 * LANES :] = bt[e, 2].astype(BF16)

        @pl.when(jnp.logical_not(on_diagonal))
        def _():
            bs[rows, 2 * LANES :] = jnp.zeros((ROWS, LANES), BF16)

        return carry

    lax.fori_loop(0, NEAR, round_rows, 0)
    receive(ma_copy, NEAR)

    m_turned = mall[...].reshape(NEAR * ROWS, LANES).T
    m_high, m_low = split(m_turned[0:W])
    both = mm(jnp.concatenate([m_high, m_low], axis=0), bs[...])
    yb[...] = both[0:W] + both[W:]
    middle = slice(LANES, 2 * LANES)
    nothing = jnp.zeros((RANK, LANES), F32)
    first_core = jnp.logical_and(jnp.logical_not(on_diagonal), core == 0)
    second_core = jnp.logical_and(jnp.logical_not(on_diagonal), core == 1)

    @pl.when(first_core)
    def _():
        s2[0:64, :] = yb[0:64, 0:LANES]
        s2[64:128, :] = yb[0:64, middle]

    @pl.when(second_core)
    def _():
        s2[0:64, :] = yb[0:64, 0:LANES]
        s2[64:96, :] = yb[64:96, middle]
        s2[96:128, :] = nothing

    @pl.when(on_diagonal)
    def _():
        s2[0:32, :] = yb[64:96, 0:LANES]
        s2[32:64, :] = yb[64:96, middle]
        s2[64:96, :] = yb[64:96, 2 * LANES :]
        s2[96:128, :] = nothing

    def r3_copy(d):
        to = lax.rem(z + d, DEPTH)
        return remote(
            s2.at[pl.ds(pl.multiple_of(to * 8, 8), 8)],
            r3.at[d - 1],
            r3s.at[d - 1],
            r3r.at[d - 1],
            z_peer(to),
        )

    send(r3_copy, DEPTH)
    receive(r3_copy, DEPTH)
    z_own = pl.ds(pl.multiple_of(z * 8, 8), 8)
    s3[z_own, :] = s2[z_own, :] + jnp.sum(r3[...], axis=0)

    def g3_copy(d):
        return remote(
            s3.at[z_own],
            s3.at[z_own],
            g3s.at[d - 1],
            g3r.at[d - 1],
            z_peer(lax.rem(z + d, DEPTH)),
        )

    send(g3_copy, DEPTH)
    receive(g3_copy, DEPTH)


    zb[...] = jnp.zeros_like(zb)

    @pl.when(first_core)
    def _():
        zb[0:64, 0:LANES] = s3[0:64, :]
        zb[0:64, middle] = s3[64:128, :]

    @pl.when(second_core)
    def _():
        zb[0:64, 0:LANES] = s3[0:64, :]
        zb[64:96, middle] = s3[64:96, :]

    @pl.when(on_diagonal)
    def _():
        zb[64:96, 0:LANES] = s3[0:32, :]
        zb[64:96, middle] = s3[32:64, :]
        zb[64:96, 2 * LANES :] = s3[64:96, :]

    z_high, z_low = split(zb[...])
    zs[0:LANES, :] = z_high
    zs[LANES:, :] = z_low
    onto = mm_t(bs[...], zs[...])
    ub[...] = (onto[:, 0:LANES] + onto[:, LANES:]).reshape(NEAR, ROWS, LANES)

    def u_copy(e):
        return remote(
            ub.at[e], urecv.at[e - 1], us.at[e - 1], ur.at[e - 1], near_peer(before(e))
        )

    send(u_copy, NEAR)

    quads = mm_t(zs[...], zs[...])
    gram = quads[0:LANES, 0:LANES] + quads[LANES:, 0:LANES]
    gram = gram + (quads[0:LANES, LANES:] + quads[LANES:, LANES:])
    row_at = lax.broadcasted_iota(jnp.int32, (RANK, LANES), 0)
    lane_at = lax.broadcasted_iota(jnp.int32, (RANK, LANES), 1)
    beside = jnp.zeros((RANK, LANES), F32)
    for k in range(3):
        here = jnp.logical_and(lane_at >= k * RANK, lane_at < (k + 1) * RANK)
        beside = jnp.where(here, gram[k * RANK : (k + 1) * RANK], beside)
    gmine[...] = beside
    gs_copy = remote(gmine, gsib, gss.at[0], gsr.at[0], sibling)
    send_one(gs_copy)
    gs_copy.wait_recv()
    g_half = pl.ds(pl.multiple_of(core * 16, 16), 16)
    gall[plane] = gmine[g_half, :] + gsib[g_half, :]

    def gp_copy(d, source):
        return remote(
            gall.at[source],
            gall.at[source],
            gps.at[d - 1],
            gpr.at[source],
            plane_peer(lax.rem(plane + d, PLANE)),
        )

    around(PLANE, lambda d: gp_copy(d, plane).start())
    pending.append(lambda: around(PLANE, lambda d: gp_copy(d, plane).wait_send()))

    receive(u_copy, NEAR)
    img_own = pl.ds(pl.multiple_of(plane * 32 + zh * 16, 16), 16)
    img[img_own, :] = ub[0] + jnp.sum(urecv[...], axis=0)
    iz_copy = remote(img.at[img_own], img.at[img_own], izs.at[0], izr.at[0], opposite)
    send_one(iz_copy)

    around(
        PLANE, lambda d: gp_copy(d, lax.rem(plane + PLANE - d, PLANE)).wait_recv()
    )
    ghalf[g_half, :] = jnp.sum(gall[...], axis=0)
    gh_copy = remote(
        ghalf.at[g_half], ghalf.at[g_half], ghs.at[0], ghr.at[0], sibling
    )
    send_one(gh_copy)
    gh_copy.wait_recv()

    left = [ghalf[...] for _ in range(3)]
    right = [(lane_at == row_at + k * RANK).astype(F32) for k in range(3)]
    for j in range(RANK - 1):
        for k in range(3):
            at = k * RANK + j
            pivot = left[k][j : j + 1, at : at + 1]
            column = left[k][:, at : at + 1] / pivot
            factor = jnp.where(row_at > j, column, 0.0)
            left[k] = left[k] - factor * left[k][j : j + 1, :]
            right[k] = right[k] - factor * right[k][j : j + 1, :]
    inverse = []
    for k in range(3):
        diagonal = jnp.sum(
            jnp.where(lane_at == row_at + k * RANK, left[k], 0.0), axis=1, keepdims=True
        )
        inverse.append(right[k] / jnp.sqrt(diagonal))
    inverse.append(jnp.zeros((RANK, LANES), F32))
    inverse = jnp.concatenate(inverse, axis=0)

    iz_copy.wait_recv()
    img_pair = pl.ds(pl.multiple_of(plane * 32, 32), 32)

    def ix_copy(d):
        return remote(
            img.at[img_pair],
            img.at[img_pair],
            ixs.at[d - 1],
            ixr.at[d - 1],
            plane_peer(lax.rem(plane + d, PLANE)),
        )

    send(ix_copy, PLANE)
    receive(ix_copy, PLANE)
    images = mm_t(img[...], inverse, HIGH) * (1.0 / GROUPS)

    img_high, img_low = split(images.T)
    for half in range(2):
        qb[half, QB_USED:QB, :] = jnp.zeros((QB - QB_USED, LANES), F32)
    for k in range(3):
        rows = slice(k * RANK, (k + 1) * RANK)
        both = jnp.concatenate([img_high[rows], img_low[rows]], axis=0)
        first = mm(both, acts[k, 0:TOK, :])
        second = mm(img_high[rows], acts[k, TOK : 2 * TOK, :])
        share = first[0:RANK] + first[RANK:] + second
        for tile in range(FFL // LANES):
            part = share[:, tile * LANES : (tile + 1) * LANES]
            for half, row, start, count in pieces(
                tile * W + k * RANK, RANK, QB_USED
            ):
                qb[half, row : row + count, :] = part[start : start + count]

    qc_copy = remote(qb.at[1 - core], qcrecv, qcs.at[0], qcr.at[0], sibling)
    send_one(qc_copy)

    pf[core, xx, yy] = s3[...]

    def g2_copy(portion, d):
        axis = 1 - portion
        at = portion * 3 + d - 1
        block = pf.at[core, xx, yy, pl.ds(portion * 64, 64)]
        to = lax.rem(side(axis) + d, SIDE)
        return remote(block, block, g2s.at[at], g2r.at[at], side_peer(axis, to))

    def line(portion, index):
        rows = pl.ds(portion * 64, 64)
        if portion == 0:
            return pf.at[core, index, pl.ds(0, SIDE), rows]
        return pf.at[core, pl.ds(0, SIDE), index, rows]

    def g1_copy(portion, d):
        at = portion * 3 + d - 1
        block = line(portion, side(portion))
        to = lax.rem(side(portion) + d, SIDE)
        return remote(block, block, g1s.at[at], g1r.at[at], side_peer(portion, to))

    def gc_copy(portion, d):
        block = line(portion, lax.rem(side(portion) + SIDE - d, SIDE))
        at = portion * SIDE + d
        return remote(block, block, gcs.at[at], gcr.at[at], sibling)

    for portion in range(2):
        for d in (2, 1, 3):
            send_one(g2_copy(portion, d))

    qc_copy.wait_recv()
    qh[...] = qb[core] + qcrecv[...]

    def zl_peer(index):
        return (index * 2 + core, mp)

    def qr_copy(d):
        to = lax.rem(zl + d, ZLO)
        return remote(
            qh.at[pl.ds(pl.multiple_of(to * QS, 8), QS)],
            qr.at[d - 1],
            qrs.at[d - 1],
            qrr.at[d - 1],
            zl_peer(to),
        )

    send(qr_copy, ZLO)

    for portion in range(2):
        for d in (1, 3, 2):
            g2_copy(portion, d).wait_recv()
        for d in (2, 1, 3):
            send_one(g1_copy(portion, d))
        send_one(gc_copy(portion, 0))

    receive(qr_copy, ZLO)
    q_own = pl.ds(pl.multiple_of(zl * QS, 8), QS)
    qf[core, q_own, :] = qh[q_own, :] + jnp.sum(qr[...], axis=0)

    def qg_copy(d):
        return remote(
            qf.at[core, q_own],
            qf.at[core, q_own],
            qgs.at[d - 1],
            qgr.at[d - 1],
            zl_peer(lax.rem(zl + d, ZLO)),
        )

    def qd_copy(d):
        rows = pl.ds(pl.multiple_of(lax.rem(zl + ZLO - d, ZLO) * QS, 8), QS)
        return remote(
            qf.at[core, rows], qf.at[core, rows], qds.at[d], qdr.at[d], sibling
        )

    send(qg_copy, ZLO)
    send_one(qd_copy(0))

    for d in (1, 3, 2):
        for portion in range(2):
            g1_copy(portion, d).wait_recv()
            send_one(gc_copy(portion, d))
    for d in range(SIDE):
        for portion in range(2):
            gc_copy(portion, d).wait_recv()

    for of_core in range(2):
        for chip in range(PLANE):
            for row, k, tile in tiles_of(of_core, chip)[1]:
                ptf[k * RANK : (k + 1) * RANK, tile * LANES : (tile + 1) * LANES] = pf[
                    of_core, chip // SIDE, chip % SIDE, row : row + RANK, :
                ]
    scaled = inverse[0:W, 0:W] * math.sqrt(D)

    def left_factor(tile, carry):
        at = pl.ds(pl.multiple_of(tile * 4 * LANES, LANES), 4 * LANES)
        pfin[:, at] = mm(scaled, ptf[:, at], HIGH)
        return carry

    lax.fori_loop(0, D // (4 * LANES), left_factor, 0)
    out_copy = pltpu.make_async_copy(pfin, p_out, outs.at[0])
    out_copy.start()
    pending.append(out_copy.wait)

    def hand_on(d):
        qg_copy(d).wait_recv()
        qd_copy(d).start()

    around(ZLO, hand_on)
    pending.append(lambda: around(ZLO, lambda d: qd_copy(d).wait_send()))
    qd_copy(0).wait_recv()
    receive(qd_copy, ZLO)

    for tile in range(FFL // LANES):
        parts = [
            qf[half, row : row + count, :]
            for half, row, _, count in pieces(tile * W, W, QB_USED)
        ]
        whole = parts[0] if len(parts) == 1 else jnp.concatenate(parts, axis=0)
        q_out[:, tile * LANES : (tile + 1) * LANES] = whole

    finish()


def on_device(inputs, out_grad, gate_pre, up_pre, hidden_grad, q_start):
    vmem = pl.BlockSpec(memory_space=pltpu.VMEM)
    far = pl.BlockSpec(memory_space=pl.ANY)
    buffers = [
        pltpu.VMEM((TOK, FFL), BF16),
        pltpu.VMEM((TOK, FFL), BF16),
        pltpu.VMEM((TOK, FFL), BF16),
        pltpu.VMEM((3, 2 * TOK, FFL), BF16),
        pltpu.VMEM((2 * LANES, FFL), BF16),
        pltpu.VMEM((TOK, LANES), F32),
        pltpu.VMEM((PLANE - 1, 32, LANES), F32),
        pltpu.VMEM((32, LANES), F32),
        pltpu.VMEM((16, LANES), F32),
        pltpu.VMEM((2 * TILES, ROWS, LANES), F32),
        pltpu.VMEM((NEAR, 3, ROWS, LANES), F32),
        pltpu.VMEM((NEAR * ROWS, 3 * LANES), BF16),
        pltpu.VMEM((NEAR, ROWS, LANES), F32),
        pltpu.VMEM((W, 3 * LANES), F32),
        pltpu.VMEM((SHARE, LANES), F32),
        pltpu.VMEM((DEPTH - 1, 8, LANES), F32),
        pltpu.VMEM((SHARE, LANES), F32),
        pltpu.VMEM((LANES, 3 * LANES), F32),
        pltpu.VMEM((2 * LANES, 3 * LANES), BF16),
        pltpu.VMEM((NEAR, ROWS, LANES), F32),
        pltpu.VMEM((NEAR - 1, ROWS, LANES), F32),
        pltpu.VMEM((RANK, LANES), F32),
        pltpu.VMEM((RANK, LANES), F32),
        pltpu.VMEM((PLANE, 16, LANES), F32),
        pltpu.VMEM((RANK, LANES), F32),
        pltpu.VMEM((2, SIDE, SIDE, SHARE, LANES), F32),
        pltpu.VMEM((W, D), F32),
        pltpu.VMEM((W, D), F32),
        pltpu.VMEM((TOK, LANES), F32),
        pltpu.VMEM((2, QB, LANES), F32),
        pltpu.VMEM((QB, LANES), F32),
        pltpu.VMEM((QB, LANES), F32),
        pltpu.VMEM((ZLO - 1, QS, LANES), F32),
        pltpu.VMEM((2, QB, LANES), F32),
    ]
    counts = [12]
    counts += [15, 15, 1, 1]
    counts += [31, 31, 31, 31]
    counts += [15, 15, 15, 15]
    counts += [31, 31]
    counts += [1, 1, 15, 16, 1, 1]
    counts += [6, 6, 6, 6, 8, 8]
    counts += [1, 1, 15, 15]
    counts += [1, 1, 7, 7, 7, 7, 8, 8]
    counts += [1]
    flags = [pltpu.SemaphoreType.DMA((count,)) for count in counts]
    p_turned, q_turned = pl.pallas_call(
        kernel,
        out_shape=(
            jax.ShapeDtypeStruct((W, D), F32),
            jax.ShapeDtypeStruct((W, FFL), F32),
        ),
        in_specs=[vmem, vmem, far, far, far, vmem],
        out_specs=(far, vmem),
        scratch_shapes=buffers + flags,
        compiler_params=pltpu.CompilerParams(
            collective_id=0, has_side_effects=True, vmem_limit_bytes=56 * 2**20
        ),
        name="power_step",
    )(inputs, out_grad, gate_pre, up_pre, hidden_grad, q_start.T)
    return p_turned.T, q_turned.T


def solution(mesh):
    in_specs = (
        P(("dp", "mp"), None),
        P(("dp", "mp"), None),
        P("dp", "mp"),
        P("dp", "mp"),
        P("dp", "mp"),
        P("mp", None),
    )
    out_specs = (P(), P("mp", None))
    return jax.shard_map(
        on_device, mesh=mesh, in_specs=in_specs, out_specs=out_specs, check_vma=False
    )
```

```python
import functools
import math

import jax
import jax.numpy as jnp
from jax import lax
from jax.experimental import pallas as pl
from jax.experimental.pallas import tpu as pltpu
from jax.sharding import PartitionSpec as P

MESH = pl.DeviceIdType.MESH
F32 = jnp.float32
BF16 = jnp.bfloat16
HIGH = lax.Precision.HIGHEST

D = 4608
TOK = 512
FFL = 1152
ROWS = 16
RANK = 32
W = 3 * RANK
LANES = 128
SIDE = 4
PLANE = SIDE * SIDE
ZLO = 8
DEPTH = 16
GROUPS = 16

TILES = D // LANES
NEAR = 2 * PLANE
SHARE = 128
QB = 448
QB_USED = 432
QS = QB // ZLO
HALF = TOK // 2


def split(value):
    high = value.astype(BF16)
    low = (value - high.astype(F32)).astype(BF16)
    return high, low


def mm(left, right, precision=None):
    return lax.dot_general(
        left,
        right,
        (((1,), (0,)), ((), ())),
        preferred_element_type=F32,
        precision=precision,
    )


def mm_t(left, right, precision=None):
    return lax.dot_general(
        left,
        right,
        (((1,), (1,)), ((), ())),
        preferred_element_type=F32,
        precision=precision,
    )


def tiles_of(core, plane):
    x, y = divmod(plane, SIDE)
    if x == y:
        first = 12 + 6 * x + 3 * core
        return (
            [(1, first + i) for i in range(3)],
            [(32 * i, 2, first + i) for i in range(3)],
        )
    at = plane - plane // (SIDE + 1) - 1
    if core == 0:
        return (
            [(0, 3 * at), (0, 3 * at + 1)],
            [
                (0, 0, 3 * at),
                (32, 1, 3 * at),
                (64, 0, 3 * at + 1),
                (96, 1, 3 * at + 1),
            ],
        )
    return (
        [(0, 3 * at + 2), (1, at)],
        [(0, 0, 3 * at + 2), (32, 1, 3 * at + 2), (64, 2, at)],
    )


def staged(core, plane):
    x, y = lax.div(plane, SIDE), lax.rem(plane, SIDE)
    at = plane - lax.div(plane, SIDE + 1) - 1
    return jnp.where(x == y, 48 + 6 * x + 3 * core, 4 * at + 2 * core)


def pieces(start, count, used):
    out = []
    at = start
    while at < start + count:
        block, row = divmod(at, used)
        here = min(used - row, start + count - at)
        out.append((block, row, at - start, here))
        at += here
    return out


def kernel(
    in_ref,
    og_ref,
    gate_ref,
    up_ref,
    cot_ref,
    q_ref,
    p_out,
    q_out,
    gate_in,
    up_in,
    cot_in,
    acts,
    qs,
    mpart,
    mrecv,
    maway,
    mzrecv,
    bst,
    bt,
    bs,
    mall,
    yb,
    s2,
    r3,
    s3,
    zb,
    zs,
    ub,
    urecv,
    gmine,
    gsib,
    gall,
    ghalf,
    pf,
    ptf,
    pfin,
    img,
    qb,
    qcrecv,
    qh,
    qr,
    qf,
    loads,
    ms,
    mr,
    mzs,
    mzr,
    bsend,
    brecv,
    mas,
    mar,
    r3s,
    r3r,
    g3s,
    g3r,
    us,
    ur,
    gss,
    gsr,
    gps,
    gpr,
    ghs,
    ghr,
    g2s,
    g2r,
    g1s,
    g1r,
    gcs,
    gcr,
    izs,
    izr,
    ixs,
    ixr,
    qcs,
    qcr,
    qrs,
    qrr,
    qgs,
    qgr,
    qds,
    qdr,
    outs,
):
    dp, mp = lax.axis_index("dp"), lax.axis_index("mp")
    core, zl = lax.rem(dp, 2), lax.div(dp, 2)
    zh, plane = lax.rem(mp, 2), lax.div(mp, 2)
    xx, yy = lax.div(plane, SIDE), lax.rem(plane, SIDE)
    z = zh * ZLO + zl
    on_diagonal = xx == yy
    sibling = (zl * 2 + 1 - core, mp)
    opposite = (dp, plane * 2 + 1 - zh)

    def plane_peer(index):
        return (dp, index * 2 + zh)

    def z_peer(index):
        return (lax.rem(index, ZLO) * 2 + core, plane * 2 + lax.div(index, ZLO))

    def side_peer(axis, index):
        along_x = (dp, (index * SIDE + yy) * 2 + zh)
        along_y = (dp, (xx * SIDE + index) * 2 + zh)
        return along_x if axis == 0 else along_y

    def side(axis):
        return xx if axis == 0 else yy

    def after(e):
        x = lax.rem(xx + lax.div(lax.rem(e, PLANE), SIDE), SIDE)
        y = lax.rem(yy + lax.rem(e, SIDE), SIDE)
        return lax.rem(core + lax.div(e, PLANE), 2), x * SIDE + y

    def before(e):
        x = lax.rem(xx + SIDE - lax.div(lax.rem(e, PLANE), SIDE), SIDE)
        y = lax.rem(yy + SIDE - lax.rem(e, SIDE), SIDE)
        return lax.rem(core + lax.div(e, PLANE), 2), x * SIDE + y

    def near_peer(place):
        return (zl * 2 + place[0], place[1] * 2 + zh)

    def remote(src, dst, send, recv, to):
        return pltpu.make_async_remote_copy(
            src_ref=src,
            dst_ref=dst,
            send_sem=send,
            recv_sem=recv,
            device_id=to,
            device_id_type=MESH,
        )

    def around(count, body, first=1):
        def step(index, carry):
            body(index)
            return carry

        lax.fori_loop(first, count, step, 0)

    pending = []

    def far_first(count, body):
        if count == NEAR:

            def step(i):
                d = 1 + lax.rem(25 - i, 15)
                body(d)
                body(PLANE + d)

            around(15, step, first=0)
            body(jnp.int32(PLANE))
        elif count == PLANE:
            around(15, lambda i: body(1 + lax.rem(25 - i, 15)), first=0)
        else:
            half = count // 2
            around(
                count - 1,
                lambda i: body(
                    half + (1 - 2 * lax.rem(i, 2)) * lax.div(i + 1, 2)
                ),
                first=0,
            )

    def drain(bytes_of, semaphore):
        pltpu.make_async_copy(bytes_of, bytes_of, semaphore).wait()

    def send(make, count, bytes_of, semaphore):
        far_first(count, lambda d: make(d).start())
        pending.append(lambda: drain(bytes_of, semaphore))

    def send_one(copy):
        copy.start()
        pending.append(copy.wait_send)

    def finish():
        while pending:
            pending.pop(0)()

    barrier = pltpu.get_barrier_semaphore()

    def greet(to):
        pl.semaphore_signal(barrier, inc=1, device_id=to, device_id_type=MESH)

    around(DEPTH, lambda d: greet(z_peer(lax.rem(z + d, DEPTH))))
    around(NEAR, lambda e: greet(near_peer(after(e))))

    quarter = PLANE // 2

    def load(half, part, which):
        chips = pl.ds(part * quarter, quarter)
        src, dst = (
            (gate_ref, gate_in),
            (up_ref, up_in),
            (cot_ref, cot_in),
        )[which]
        return pltpu.make_async_copy(
            src.at[chips, zh if half else 1 - zh],
            dst.at[half, chips],
            loads.at[half * 6 + part * 3 + which],
        )

    for half in range(2):
        for part in range(2):
            for which in range(3):
                load(half, part, which).start()

    place = 0
    for chip_type in (False, True):
        for chip in range(PLANE):
            if (chip // SIDE == chip % SIDE) != chip_type:
                continue
            for of_core in range(2):
                for array, tile in tiles_of(of_core, chip)[0]:
                    source = (in_ref, og_ref)[array]
                    bst[place] = source[:, tile * LANES : (tile + 1) * LANES].astype(F32)
                    place += 1

    def activate(half, i):
        rows = pl.ds(pl.multiple_of(i * ROWS, ROWS), ROWS)
        g = gate_in[half, i].astype(F32)
        u = up_in[half, i].astype(F32)
        e = cot_in[half, i].astype(F32)
        s = 1.0 / (1.0 + jnp.exp(-g))
        silu = g * s
        values = (e * u * s * (1.0 + g * (1.0 - s)), e * silu, silu * u)
        for k, value in enumerate(values):
            high, low = split(value)
            acts[k, half, 0, rows, :] = high
            acts[k, half, 1, rows, :] = low

    def b_copy(e, count):
        to = after(e)
        return remote(
            bst.at[pl.ds(staged(*to), count)],
            bt.at[e, pl.ds(0, count)],
            bsend.at[0],
            brecv.at[lax.div(e, PLANE)],
            near_peer(to),
        )

    def b_each(e, act, diagonal):
        @pl.when(diagonal)
        def _():
            act(b_copy(e, 3))

        @pl.when(jnp.logical_not(diagonal))
        def _():
            act(b_copy(e, 2))

    def to_diagonal(e):
        chip = after(e)[1]
        return lax.div(chip, SIDE) == lax.rem(chip, SIDE)

    q_high, q_low = split(q_ref[...])
    qs[...] = jnp.zeros_like(qs)
    qs[0:W, :] = q_high
    qs[LANES : LANES + W, :] = q_low

    lane = lax.broadcasted_iota(jnp.int32, (HALF, LANES), 1)

    def mix(half):
        for k in range(3):
            first = mm_t(acts[k, half, 0], qs[...])
            second = mm_t(acts[k, half, 1], qs[0:LANES, :])
            both = first[:, 0:LANES] + first[:, LANES:] + second
            if k == 0:
                mpart[half] = both
            else:
                mpart[half] = jnp.where(lane >= k * RANK, both, mpart[half])

    plane_rows = pl.ds(pl.multiple_of(plane * ROWS, ROWS), ROWS)

    def m_copy(half, d):
        to = after(d)[1]
        return remote(
            mpart.at[half, pl.ds(pl.multiple_of(to * ROWS, ROWS), ROWS)],
            mrecv.at[half, d - 1],
            ms.at[half],
            mr.at[half],
            plane_peer(to),
        )

    def m_send(half):
        send(lambda d: m_copy(half, d), PLANE, mrecv.at[half], ms.at[half])

    def m_sum(half):
        drain(mrecv.at[half], mr.at[half])
        return mpart[half, plane_rows, :] + jnp.sum(mrecv[half], axis=0)

    for half in range(2):
        for part in range(2):
            for which in range(3):
                load(half, part, which).wait()
            around(
                (part + 1) * quarter,
                lambda i: activate(half, i),
                first=part * quarter,
            )
        mix(half)
        if half == 0:
            pl.semaphore_wait(barrier, DEPTH - 1 + NEAR - 1)
        m_send(half)
        if half == 0:
            around(PLANE, lambda e: b_each(e, lambda c: c.start(), to_diagonal(e)))
    maway[...] = m_sum(0)
    mz_copy = remote(maway, mzrecv, mzs.at[0], mzr.at[0], opposite)
    send_one(mz_copy)
    around(
        NEAR, lambda e: b_each(e, lambda c: c.start(), to_diagonal(e)), first=PLANE
    )

    def b_sent():
        for count, here in ((3, on_diagonal), (2, jnp.logical_not(on_diagonal))):

            @pl.when(here)
            def _():
                drain(bst.at[pl.ds(0, 2 * TILES - count)], bsend.at[0])

    pending.append(b_sent)

    def b_receive(group):
        slots = pl.ds(1, PLANE - 1) if group == 0 else pl.ds(PLANE, PLANE)
        for count, here in ((3, on_diagonal), (2, jnp.logical_not(on_diagonal))):

            @pl.when(here)
            def _():
                drain(bt.at[slots, pl.ds(0, count)], brecv.at[group])

    mhome = m_sum(1)

    own_tiles = staged(core, plane)
    for tile in range(2):
        bt[0, tile] = bst[own_tiles + tile]

    @pl.when(on_diagonal)
    def _():
        bt[0, 2] = bst[own_tiles + 2]

    def round_rows(e):
        rows = pl.ds(pl.multiple_of(e * ROWS, ROWS), ROWS)
        for tile in range(2):
            bs[rows, tile * LANES : (tile + 1) * LANES] = bt[e, tile].astype(BF16)

        @pl.when(on_diagonal)
        def _():
            bs[rows, 2 * LANES :] = bt[e, 2].astype(BF16)

        @pl.when(jnp.logical_not(on_diagonal))
        def _():
            bs[rows, 2 * LANES :] = jnp.zeros((ROWS, LANES), BF16)

    b_receive(0)
    around(PLANE, round_rows, first=0)

    mz_copy.wait_recv()
    mall[0] = (mhome + mzrecv[...]) * (1.0 / GROUPS)

    def ma_copy(e):
        return remote(
            mall.at[0], mall.at[e], mas.at[0], mar.at[0], near_peer(after(e))
        )

    ma_bytes = mall.at[pl.ds(1, NEAR - 1)]
    send(ma_copy, NEAR, ma_bytes, mas.at[0])

    b_receive(1)
    around(NEAR, round_rows, first=PLANE)
    drain(ma_bytes, mar.at[0])

    m_turned = mall[...].reshape(NEAR * ROWS, LANES).T
    m_high, m_low = split(m_turned[0:W])
    both = mm(jnp.concatenate([m_high, m_low], axis=0), bs[...])
    yb[...] = both[0:W] + both[W:]
    middle = slice(LANES, 2 * LANES)
    nothing = jnp.zeros((RANK, LANES), F32)
    first_core = jnp.logical_and(jnp.logical_not(on_diagonal), core == 0)
    second_core = jnp.logical_and(jnp.logical_not(on_diagonal), core == 1)

    @pl.when(first_core)
    def _():
        s2[0:64, :] = yb[0:64, 0:LANES]
        s2[64:128, :] = yb[0:64, middle]

    @pl.when(second_core)
    def _():
        s2[0:64, :] = yb[0:64, 0:LANES]
        s2[64:96, :] = yb[64:96, middle]
        s2[96:128, :] = nothing

    @pl.when(on_diagonal)
    def _():
        s2[0:32, :] = yb[64:96, 0:LANES]
        s2[32:64, :] = yb[64:96, middle]
        s2[64:96, :] = yb[64:96, 2 * LANES :]
        s2[96:128, :] = nothing

    def r3_copy(d):
        to = lax.rem(z + d, DEPTH)
        return remote(
            s2.at[pl.ds(pl.multiple_of(to * 8, 8), 8)],
            r3.at[d - 1],
            r3s.at[0],
            r3r.at[0],
            z_peer(to),
        )

    send(r3_copy, DEPTH, r3, r3s.at[0])
    drain(r3, r3r.at[0])
    z_own = pl.ds(pl.multiple_of(z * 8, 8), 8)
    s3[z_own, :] = s2[z_own, :] + jnp.sum(r3[...], axis=0)

    def g3_copy(d):
        return remote(
            s3.at[z_own],
            s3.at[z_own],
            g3s.at[0],
            g3r.at[0],
            z_peer(lax.rem(z + d, DEPTH)),
        )

    g3_bytes = s3.at[pl.ds(0, SHARE - 8)]
    send(g3_copy, DEPTH, g3_bytes, g3s.at[0])
    drain(g3_bytes, g3r.at[0])


    zb[...] = jnp.zeros_like(zb)

    @pl.when(first_core)
    def _():
        zb[0:64, 0:LANES] = s3[0:64, :]
        zb[0:64, middle] = s3[64:128, :]

    @pl.when(second_core)
    def _():
        zb[0:64, 0:LANES] = s3[0:64, :]
        zb[64:96, middle] = s3[64:96, :]

    @pl.when(on_diagonal)
    def _():
        zb[64:96, 0:LANES] = s3[0:32, :]
        zb[64:96, middle] = s3[32:64, :]
        zb[64:96, 2 * LANES :] = s3[64:96, :]

    z_high, z_low = split(zb[...])
    zs[0:LANES, :] = z_high
    zs[LANES:, :] = z_low
    onto = mm_t(bs[...], zs[...])
    ub[...] = (onto[:, 0:LANES] + onto[:, LANES:]).reshape(NEAR, ROWS, LANES)

    def u_copy(e):
        return remote(
            ub.at[e], urecv.at[e - 1], us.at[0], ur.at[0], near_peer(before(e))
        )

    send(u_copy, NEAR, urecv, us.at[0])

    pf[core, xx, yy] = s3[...]

    def g2_copy(portion, d):
        axis = 1 - portion
        at = portion * 3 + d - 1
        block = pf.at[core, xx, yy, pl.ds(portion * 64, 64)]
        to = lax.rem(side(axis) + d, SIDE)
        return remote(block, block, g2s.at[at], g2r.at[at], side_peer(axis, to))

    def line(portion, index):
        rows = pl.ds(portion * 64, 64)
        if portion == 0:
            return pf.at[core, index, pl.ds(0, SIDE), rows]
        return pf.at[core, pl.ds(0, SIDE), index, rows]

    def g1_copy(portion, d):
        at = portion * 3 + d - 1
        block = line(portion, side(portion))
        to = lax.rem(side(portion) + d, SIDE)
        return remote(block, block, g1s.at[at], g1r.at[at], side_peer(portion, to))

    for portion in range(2):
        for d in (2, 1, 3):
            send_one(g2_copy(portion, d))


    quads = mm_t(zs[...], zs[...])
    gram = quads[0:LANES, 0:LANES] + quads[LANES:, 0:LANES]
    gram = gram + (quads[0:LANES, LANES:] + quads[LANES:, LANES:])
    row_at = lax.broadcasted_iota(jnp.int32, (RANK, LANES), 0)
    lane_at = lax.broadcasted_iota(jnp.int32, (RANK, LANES), 1)
    beside = jnp.zeros((RANK, LANES), F32)
    for k in range(3):
        here = jnp.logical_and(lane_at >= k * RANK, lane_at < (k + 1) * RANK)
        beside = jnp.where(here, gram[k * RANK : (k + 1) * RANK], beside)
    gmine[...] = beside
    gs_copy = remote(gmine, gsib, gss.at[0], gsr.at[0], sibling)
    send_one(gs_copy)
    gs_copy.wait_recv()
    g_half = pl.ds(pl.multiple_of(core * 16, 16), 16)
    gall[plane] = gmine[g_half, :] + gsib[g_half, :]

    def gp_copy(d):
        return remote(
            gall.at[plane],
            gall.at[plane],
            gps.at[0],
            gpr.at[0],
            plane_peer(after(d)[1]),
        )

    far_first(PLANE, lambda d: gp_copy(d).start())
    gp_bytes = gall.at[pl.ds(0, PLANE - 1)]
    pending.append(lambda: drain(gp_bytes, gps.at[0]))

    drain(urecv, ur.at[0])
    img[1, plane_rows, :] = ub[0] + jnp.sum(urecv[...], axis=0)
    iz_copy = remote(
        img.at[1, plane_rows], img.at[0, plane_rows], izs.at[0], izr.at[0], opposite
    )
    send_one(iz_copy)

    def ix_copy(half, d):
        return remote(
            img.at[half, plane_rows],
            img.at[half, plane_rows],
            ixs.at[half],
            ixr.at[half],
            plane_peer(after(d)[1]),
        )

    def ix_bytes(half):
        return img.at[half, pl.ds(0, HALF - ROWS)]

    def ix_send(half):
        send(lambda d: ix_copy(half, d), PLANE, ix_bytes(half), ixs.at[half])

    def ix_receive(half):
        drain(ix_bytes(half), ixr.at[half])

    ix_send(1)

    for portion in range(2):
        for d in (1, 3, 2):
            g2_copy(portion, d).wait_recv()
        for d in (2, 1, 3):
            send_one(g1_copy(portion, d))

    drain(gp_bytes, gpr.at[0])
    ghalf[g_half, :] = jnp.sum(gall[...], axis=0)
    gh_copy = remote(
        ghalf.at[g_half], ghalf.at[g_half], ghs.at[0], ghr.at[0], sibling
    )
    send_one(gh_copy)
    gh_copy.wait_recv()

    left = [ghalf[...] for _ in range(3)]
    right = [(lane_at == row_at + k * RANK).astype(F32) for k in range(3)]
    def eliminate(j):
        for k in range(3):
            at = k * RANK + j
            pivot = left[k][j : j + 1, at : at + 1]
            column = left[k][:, at : at + 1] / pivot
            factor = jnp.where(row_at > j, column, 0.0)
            left[k] = left[k] - factor * left[k][j : j + 1, :]
            right[k] = right[k] - factor * right[k][j : j + 1, :]

    middle_step = RANK // 2
    for j in range(middle_step):
        eliminate(j)
    iz_copy.wait_recv()
    ix_send(0)
    for j in range(middle_step, RANK - 1):
        eliminate(j)
    inverse = []
    for k in range(3):
        diagonal = jnp.sum(
            jnp.where(lane_at == row_at + k * RANK, left[k], 0.0), axis=1, keepdims=True
        )
        inverse.append(right[k] / jnp.sqrt(diagonal))
    inverse.append(jnp.zeros((RANK, LANES), F32))
    inverse = jnp.concatenate(inverse, axis=0)

    for side_half in range(2):
        qb[side_half, QB_USED:QB, :] = jnp.zeros((QB - QB_USED, LANES), F32)
    for half in (1, 0):
        ix_receive(half)
        if half == 0:
            for portion in range(2):
                for d in (1, 3, 2):
                    g1_copy(portion, d).wait_recv()
            gc_copy = remote(
                pf.at[core], pf.at[core], gcs.at[0], gcr.at[0], sibling
            )
            send_one(gc_copy)
        images = mm_t(img[half], inverse, HIGH) * (1.0 / GROUPS)
        img_high, img_low = split(images.T)
        for k in range(3):
            rows = slice(k * RANK, (k + 1) * RANK)
            both = jnp.concatenate([img_high[rows], img_low[rows]], axis=0)
            first = mm(both, acts[k, half, 0])
            second = mm(img_high[rows], acts[k, half, 1])
            share = first[0:RANK] + first[RANK:] + second
            for tile in range(FFL // LANES):
                part = share[:, tile * LANES : (tile + 1) * LANES]
                for block, row, start, count in pieces(
                    tile * W + k * RANK, RANK, QB_USED
                ):
                    piece = part[start : start + count]
                    if half == 0:
                        piece = piece + qb[block, row : row + count, :]
                    qb[block, row : row + count, :] = piece

    qc_copy = remote(qb.at[1 - core], qcrecv, qcs.at[0], qcr.at[0], sibling)
    send_one(qc_copy)

    qc_copy.wait_recv()
    qh[...] = qb[core] + qcrecv[...]

    def zl_peer(index):
        return (index * 2 + core, mp)

    def q_rows(index):
        return pl.ds(pl.multiple_of(index * QS, 8), QS)

    def qr_copy(d):
        to = lax.rem(zl + d, ZLO)
        return remote(
            qh.at[q_rows(to)], qr.at[d - 1], qrs.at[0], qrr.at[0], zl_peer(to)
        )

    send(qr_copy, ZLO, qr, qrs.at[0])

    gc_copy.wait_recv()

    for of_core in range(2):
        for chip in range(PLANE):
            for row, k, tile in tiles_of(of_core, chip)[1]:
                ptf[k * RANK : (k + 1) * RANK, tile * LANES : (tile + 1) * LANES] = pf[
                    of_core, chip // SIDE, chip % SIDE, row : row + RANK, :
                ]
    scaled = inverse[0:W, 0:W] * math.sqrt(D)

    def left_factor(tile, carry):
        at = pl.ds(pl.multiple_of(tile * 4 * LANES, LANES), 4 * LANES)
        pfin[:, at] = mm(scaled, ptf[:, at], HIGH)
        return carry

    lax.fori_loop(0, D // (4 * LANES), left_factor, 0)
    out_copy = pltpu.make_async_copy(pfin, p_out, outs.at[0])
    out_copy.start()
    pending.append(out_copy.wait)

    finish()

    drain(qr, qrr.at[0])
    q_own = q_rows(zl)
    qf[core, q_own, :] = qh[q_own, :] + jnp.sum(qr[...], axis=0)

    def qg_copy(d):
        own = qf.at[core, q_own]
        to = zl_peer(lax.rem(zl + d, ZLO))
        return remote(own, own, qgs.at[0], qgr.at[0], to)

    qg_bytes = qf.at[core, pl.ds(0, QB - QS)]
    send(qg_copy, ZLO, qg_bytes, qgs.at[0])
    drain(qg_bytes, qgr.at[0])
    qd_copy = remote(qf.at[core], qf.at[core], qds.at[0], qdr.at[0], sibling)
    send_one(qd_copy)
    qd_copy.wait_recv()

    for tile in range(FFL // LANES):
        parts = [
            qf[half, row : row + count, :]
            for half, row, _, count in pieces(tile * W, W, QB_USED)
        ]
        whole = parts[0] if len(parts) == 1 else jnp.concatenate(parts, axis=0)
        q_out[:, tile * LANES : (tile + 1) * LANES] = whole

    finish()


def deliver(p_ref, q_ref, p_out, q_out, p_held, q_held, come, go):
    count = 6
    rows = [pl.ds(i * (W // count), W // count) for i in range(count)]
    arrays = [(p_ref, p_held, p_out, part) for part in rows]
    arrays.append((q_ref, q_held, q_out, pl.ds(0, W)))
    into = [
        pltpu.make_async_copy(src.at[part], held.at[part], come.at[i])
        for i, (src, held, _, part) in enumerate(arrays)
    ]
    out = [
        pltpu.make_async_copy(held.at[part], dst.at[part], go.at[i])
        for i, (_, held, dst, part) in enumerate(arrays)
    ]
    for copy in into:
        copy.start()
    for first, second in zip(into, out):
        first.wait()
        second.start()
    for copy in out:
        copy.wait()


def on_device(inputs, out_grad, gate_pre, up_pre, hidden_grad, q_start):
    vmem = pl.BlockSpec(memory_space=pltpu.VMEM)
    far = pl.BlockSpec(memory_space=pl.ANY)
    buffers = [
        pltpu.VMEM((2, PLANE, ROWS, FFL), BF16),
        pltpu.VMEM((2, PLANE, ROWS, FFL), BF16),
        pltpu.VMEM((2, PLANE, ROWS, FFL), BF16),
        pltpu.VMEM((3, 2, 2, HALF, FFL), BF16),
        pltpu.VMEM((2 * LANES, FFL), BF16),
        pltpu.VMEM((2, HALF, LANES), F32),
        pltpu.VMEM((2, PLANE - 1, ROWS, LANES), F32),
        pltpu.VMEM((ROWS, LANES), F32),
        pltpu.VMEM((16, LANES), F32),
        pltpu.VMEM((2 * TILES, ROWS, LANES), F32),
        pltpu.VMEM((NEAR, 3, ROWS, LANES), F32),
        pltpu.VMEM((NEAR * ROWS, 3 * LANES), BF16),
        pltpu.VMEM((NEAR, ROWS, LANES), F32),
        pltpu.VMEM((W, 3 * LANES), F32),
        pltpu.VMEM((SHARE, LANES), F32),
        pltpu.VMEM((DEPTH - 1, 8, LANES), F32),
        pltpu.VMEM((SHARE, LANES), F32),
        pltpu.VMEM((LANES, 3 * LANES), F32),
        pltpu.VMEM((2 * LANES, 3 * LANES), BF16),
        pltpu.VMEM((NEAR, ROWS, LANES), F32),
        pltpu.VMEM((NEAR - 1, ROWS, LANES), F32),
        pltpu.VMEM((RANK, LANES), F32),
        pltpu.VMEM((RANK, LANES), F32),
        pltpu.VMEM((PLANE, 16, LANES), F32),
        pltpu.VMEM((RANK, LANES), F32),
        pltpu.VMEM((2, SIDE, SIDE, SHARE, LANES), F32),
        pltpu.VMEM((W, D), F32),
        pltpu.VMEM((W, D), F32),
        pltpu.VMEM((2, HALF, LANES), F32),
        pltpu.VMEM((2, QB, LANES), F32),
        pltpu.VMEM((QB, LANES), F32),
        pltpu.VMEM((QB, LANES), F32),
        pltpu.VMEM((ZLO - 1, QS, LANES), F32),
        pltpu.VMEM((2, QB, LANES), F32),
    ]
    counts = [12]
    counts += [2, 2, 1, 1]
    counts += [1, 2, 1, 1]
    counts += [1, 1, 1, 1]
    counts += [1, 1]
    counts += [1, 1, 1, 1, 1, 1]
    counts += [6, 6, 6, 6, 1, 1]
    counts += [1, 1, 2, 2]
    counts += [1, 1, 1, 1, 1, 1, 1, 1]
    counts += [1]
    flags = [pltpu.SemaphoreType.DMA((count,)) for count in counts]
    by_half = [
        array.reshape(PLANE, 2, ROWS, FFL) for array in (gate_pre, up_pre, hidden_grad)
    ]
    p_turned, q_turned = pl.pallas_call(
        kernel,
        out_shape=(
            jax.ShapeDtypeStruct((W, D), F32),
            jax.ShapeDtypeStruct((W, FFL), F32),
        ),
        in_specs=[vmem, vmem, far, far, far, vmem],
        out_specs=(far, vmem),
        scratch_shapes=buffers + flags,
        compiler_params=pltpu.CompilerParams(
            collective_id=0, has_side_effects=True, vmem_limit_bytes=56 * 2**20
        ),
        name="power_step",
    )(inputs, out_grad, *by_half, q_start.T)
    shapes = (
        jax.ShapeDtypeStruct((W, D), F32),
        jax.ShapeDtypeStruct((W, FFL), F32),
    )
    p_turned, q_turned = pl.pallas_call(
        deliver,
        out_shape=shapes,
        in_specs=[far, far],
        out_specs=(far, far),
        scratch_shapes=[
            pltpu.VMEM((W, D), F32),
            pltpu.VMEM((W, FFL), F32),
            pltpu.SemaphoreType.DMA((7,)),
            pltpu.SemaphoreType.DMA((7,)),
        ],
        compiler_params=pltpu.CompilerParams(vmem_limit_bytes=56 * 2**20),
        name="deliver",
    )(p_turned, q_turned)
    return p_turned.T, q_turned.T


def solution(mesh):
    in_specs = (
        P(("dp", "mp"), None),
        P(("dp", "mp"), None),
        P("dp", "mp"),
        P("dp", "mp"),
        P("dp", "mp"),
        P("mp", None),
    )
    out_specs = (P(), P("mp", None))
    return jax.shard_map(
        on_device, mesh=mesh, in_specs=in_specs, out_specs=out_specs, check_vma=False
    )
```

```python
import functools
import math

import jax
import jax.numpy as jnp
from jax import lax
from jax.experimental import pallas as pl
from jax.experimental.pallas import tpu as pltpu
from jax.sharding import PartitionSpec as P

MESH = pl.DeviceIdType.MESH
F32 = jnp.float32
BF16 = jnp.bfloat16
HIGH = lax.Precision.HIGHEST

D = 4608
TOK = 512
FFL = 1152
ROWS = 16
RANK = 32
W = 3 * RANK
LANES = 128
SIDE = 4
PLANE = SIDE * SIDE
ZLO = 8
DEPTH = 16
GROUPS = 16

TILES = D // LANES
NEAR = 2 * PLANE
SHARE = 128
QB = 448
QB_USED = 432
QS = QB // ZLO
HALF = TOK // 2


def split(value):
    high = value.astype(BF16)
    low = (value - high.astype(F32)).astype(BF16)
    return high, low


def mm(left, right, precision=None):
    return lax.dot_general(
        left,
        right,
        (((1,), (0,)), ((), ())),
        preferred_element_type=F32,
        precision=precision,
    )


def mm_t(left, right, precision=None):
    return lax.dot_general(
        left,
        right,
        (((1,), (1,)), ((), ())),
        preferred_element_type=F32,
        precision=precision,
    )


def tiles_of(core, plane):
    x, y = divmod(plane, SIDE)
    if x == y:
        first = 12 + 6 * x + 3 * core
        return (
            [(1, first + i) for i in range(3)],
            [(32 * i, 2, first + i) for i in range(3)],
        )
    at = plane - plane // (SIDE + 1) - 1
    if core == 0:
        return (
            [(0, 3 * at), (0, 3 * at + 1)],
            [
                (0, 0, 3 * at),
                (32, 1, 3 * at),
                (64, 0, 3 * at + 1),
                (96, 1, 3 * at + 1),
            ],
        )
    return (
        [(0, 3 * at + 2), (1, at)],
        [(0, 0, 3 * at + 2), (32, 1, 3 * at + 2), (64, 2, at)],
    )


def staged(core, plane):
    x, y = lax.div(plane, SIDE), lax.rem(plane, SIDE)
    at = plane - lax.div(plane, SIDE + 1) - 1
    return jnp.where(x == y, 48 + 6 * x + 3 * core, 4 * at + 2 * core)


def pieces(start, count, used):
    out = []
    at = start
    while at < start + count:
        block, row = divmod(at, used)
        here = min(used - row, start + count - at)
        out.append((block, row, at - start, here))
        at += here
    return out


def kernel(
    in_ref,
    og_ref,
    gate_ref,
    up_ref,
    cot_ref,
    q_ref,
    p_out,
    q_out,
    gate_in,
    up_in,
    cot_in,
    acts,
    qs,
    mpart,
    mrecv,
    maway,
    mzrecv,
    bst,
    bt,
    bs,
    mall,
    yb,
    s2,
    r3,
    s3,
    zb,
    zs,
    ub,
    urecv,
    gmine,
    gsib,
    gall,
    ghalf,
    pf,
    ptf,
    img,
    qb,
    qcrecv,
    qh,
    qr,
    qx,
    qy,
    qf,
    loads,
    ms,
    mr,
    mzs,
    mzr,
    bsend,
    brecv,
    mas,
    mar,
    r3s,
    r3r,
    g3s,
    g3r,
    us,
    ur,
    gss,
    gsr,
    gps,
    gpr,
    ghs,
    ghr,
    g2s,
    g2r,
    g1s,
    g1r,
    gcs,
    gcr,
    izs,
    izr,
    ixs,
    ixr,
    qcs,
    qcr,
    qrs,
    qrr,
    qgs,
    qgr,
    qds,
    qdr,
):
    dp, mp = lax.axis_index("dp"), lax.axis_index("mp")
    core, zl = lax.rem(dp, 2), lax.div(dp, 2)
    zh, plane = lax.rem(mp, 2), lax.div(mp, 2)
    xx, yy = lax.div(plane, SIDE), lax.rem(plane, SIDE)
    z = zh * ZLO + zl
    on_diagonal = xx == yy
    sibling = (zl * 2 + 1 - core, mp)
    opposite = (dp, plane * 2 + 1 - zh)

    def plane_peer(index):
        return (dp, index * 2 + zh)

    def z_peer(index):
        return (lax.rem(index, ZLO) * 2 + core, plane * 2 + lax.div(index, ZLO))

    def side_peer(axis, index):
        along_x = (dp, (index * SIDE + yy) * 2 + zh)
        along_y = (dp, (xx * SIDE + index) * 2 + zh)
        return along_x if axis == 0 else along_y

    def side(axis):
        return xx if axis == 0 else yy

    def after(e):
        x = lax.rem(xx + lax.div(lax.rem(e, PLANE), SIDE), SIDE)
        y = lax.rem(yy + lax.rem(e, SIDE), SIDE)
        return lax.rem(core + lax.div(e, PLANE), 2), x * SIDE + y

    def before(e):
        x = lax.rem(xx + SIDE - lax.div(lax.rem(e, PLANE), SIDE), SIDE)
        y = lax.rem(yy + SIDE - lax.rem(e, SIDE), SIDE)
        return lax.rem(core + lax.div(e, PLANE), 2), x * SIDE + y

    def near_peer(place):
        return (zl * 2 + place[0], place[1] * 2 + zh)

    def remote(src, dst, send, recv, to):
        return pltpu.make_async_remote_copy(
            src_ref=src,
            dst_ref=dst,
            send_sem=send,
            recv_sem=recv,
            device_id=to,
            device_id_type=MESH,
        )

    def around(count, body, first=1):
        def step(index, carry):
            body(index)
            return carry

        lax.fori_loop(first, count, step, 0)

    pending = []

    def far_first(count, body):
        if count == NEAR:

            def step(i):
                d = 1 + lax.rem(25 - i, 15)
                body(d)
                body(PLANE + d)

            body(jnp.int32(PLANE))
            around(15, lambda i: body(PLANE + 1 + lax.rem(25 - i, 15)), first=0)
            around(15, lambda i: body(1 + lax.rem(25 - i, 15)), first=0)
        elif count == PLANE:
            around(15, lambda i: body(1 + lax.rem(25 - i, 15)), first=0)
        else:
            half = count // 2
            around(
                count - 1,
                lambda i: body(
                    half + (1 - 2 * lax.rem(i, 2)) * lax.div(i + 1, 2)
                ),
                first=0,
            )

    def drain(bytes_of, semaphore):
        pltpu.make_async_copy(bytes_of, bytes_of, semaphore).wait()

    def send(make, count, bytes_of, semaphore):
        far_first(count, lambda d: make(d).start())
        pending.append(lambda: drain(bytes_of, semaphore))

    def send_one(copy):
        copy.start()
        pending.append(copy.wait_send)

    def finish():
        while pending:
            pending.pop(0)()

    barrier = pltpu.get_barrier_semaphore()

    def greet(to):
        pl.semaphore_signal(barrier, inc=1, device_id=to, device_id_type=MESH)

    around(DEPTH, lambda d: greet(z_peer(lax.rem(z + d, DEPTH))))
    around(NEAR, lambda e: greet(near_peer(after(e))))

    quarter = PLANE // 2

    def load(half, part, which):
        chips = pl.ds(part * quarter, quarter)
        src, dst = (
            (gate_ref, gate_in),
            (up_ref, up_in),
            (cot_ref, cot_in),
        )[which]
        return pltpu.make_async_copy(
            src.at[chips, zh if half else 1 - zh],
            dst.at[half, chips],
            loads.at[half * 6 + part * 3 + which],
        )

    for half in range(2):
        for part in range(2):
            for which in range(3):
                load(half, part, which).start()

    place = 0
    for chip_type in (False, True):
        for chip in range(PLANE):
            if (chip // SIDE == chip % SIDE) != chip_type:
                continue
            for of_core in range(2):
                for array, tile in tiles_of(of_core, chip)[0]:
                    source = (in_ref, og_ref)[array]
                    bst[place] = source[:, tile * LANES : (tile + 1) * LANES].astype(F32)
                    place += 1

    def activate(half, i):
        rows = pl.ds(pl.multiple_of(i * ROWS, ROWS), ROWS)
        g = gate_in[half, i].astype(F32)
        u = up_in[half, i].astype(F32)
        e = cot_in[half, i].astype(F32)
        s = 1.0 / (1.0 + jnp.exp(-g))
        silu = g * s
        values = (e * u * s * (1.0 + g * (1.0 - s)), e * silu, silu * u)
        for k, value in enumerate(values):
            high, low = split(value)
            acts[k, half, 0, rows, :] = high
            acts[k, half, 1, rows, :] = low

    def b_copy(e, count):
        to = after(e)
        return remote(
            bst.at[pl.ds(staged(*to), count)],
            bt.at[e, pl.ds(0, count)],
            bsend.at[0],
            brecv.at[lax.div(e, PLANE)],
            near_peer(to),
        )

    def b_each(e, act, diagonal):
        @pl.when(diagonal)
        def _():
            act(b_copy(e, 3))

        @pl.when(jnp.logical_not(diagonal))
        def _():
            act(b_copy(e, 2))

    def to_diagonal(e):
        chip = after(e)[1]
        return lax.div(chip, SIDE) == lax.rem(chip, SIDE)

    q_high, q_low = split(q_ref[...])
    qs[...] = jnp.zeros_like(qs)
    qs[0:W, :] = q_high
    qs[LANES : LANES + W, :] = q_low

    lane = lax.broadcasted_iota(jnp.int32, (HALF, LANES), 1)

    def mix(half):
        for k in range(3):
            first = mm_t(acts[k, half, 0], qs[...])
            second = mm_t(acts[k, half, 1], qs[0:LANES, :])
            both = first[:, 0:LANES] + first[:, LANES:] + second
            if k == 0:
                mpart[half] = both
            else:
                mpart[half] = jnp.where(lane >= k * RANK, both, mpart[half])

    plane_rows = pl.ds(pl.multiple_of(plane * ROWS, ROWS), ROWS)

    def m_copy(half, d):
        to = after(d)[1]
        return remote(
            mpart.at[half, pl.ds(pl.multiple_of(to * ROWS, ROWS), ROWS)],
            mrecv.at[half, d - 1],
            ms.at[half],
            mr.at[half],
            plane_peer(to),
        )

    def m_send(half):
        send(lambda d: m_copy(half, d), PLANE, mrecv.at[half], ms.at[half])

    def m_sum(half):
        drain(mrecv.at[half], mr.at[half])
        return mpart[half, plane_rows, :] + jnp.sum(mrecv[half], axis=0)

    for half in range(2):
        for part in range(2):
            for which in range(3):
                load(half, part, which).wait()
            around(
                (part + 1) * quarter,
                lambda i: activate(half, i),
                first=part * quarter,
            )
        mix(half)
        if half == 0:
            pl.semaphore_wait(barrier, DEPTH - 1 + NEAR - 1)
        m_send(half)
        if half == 0:
            around(PLANE, lambda e: b_each(e, lambda c: c.start(), to_diagonal(e)))
    maway[...] = m_sum(0)
    mz_copy = remote(maway, mzrecv, mzs.at[0], mzr.at[0], opposite)
    send_one(mz_copy)
    around(
        NEAR, lambda e: b_each(e, lambda c: c.start(), to_diagonal(e)), first=PLANE
    )

    def b_sent():
        for count, here in ((3, on_diagonal), (2, jnp.logical_not(on_diagonal))):

            @pl.when(here)
            def _():
                drain(bst.at[pl.ds(0, 2 * TILES - count)], bsend.at[0])

    pending.append(b_sent)

    def b_receive(group):
        slots = pl.ds(1, PLANE - 1) if group == 0 else pl.ds(PLANE, PLANE)
        for count, here in ((3, on_diagonal), (2, jnp.logical_not(on_diagonal))):

            @pl.when(here)
            def _():
                drain(bt.at[slots, pl.ds(0, count)], brecv.at[group])

    mhome = m_sum(1)

    own_tiles = staged(core, plane)
    for tile in range(2):
        bt[0, tile] = bst[own_tiles + tile]

    @pl.when(on_diagonal)
    def _():
        bt[0, 2] = bst[own_tiles + 2]

    def round_rows(e):
        rows = pl.ds(pl.multiple_of(e * ROWS, ROWS), ROWS)
        for tile in range(2):
            bs[rows, tile * LANES : (tile + 1) * LANES] = bt[e, tile].astype(BF16)

        @pl.when(on_diagonal)
        def _():
            bs[rows, 2 * LANES :] = bt[e, 2].astype(BF16)

        @pl.when(jnp.logical_not(on_diagonal))
        def _():
            bs[rows, 2 * LANES :] = jnp.zeros((ROWS, LANES), BF16)

    b_receive(0)
    around(PLANE, round_rows, first=0)

    mz_copy.wait_recv()
    mall[0] = (mhome + mzrecv[...]) * (1.0 / GROUPS)

    def ma_copy(e):
        return remote(
            mall.at[0], mall.at[e], mas.at[0], mar.at[0], near_peer(after(e))
        )

    ma_bytes = mall.at[pl.ds(1, NEAR - 1)]
    send(ma_copy, NEAR, ma_bytes, mas.at[0])

    b_receive(1)
    around(NEAR, round_rows, first=PLANE)
    drain(ma_bytes, mar.at[0])

    m_turned = mall[...].reshape(NEAR * ROWS, LANES).T
    m_high, m_low = split(m_turned[0:W])
    both = mm(jnp.concatenate([m_high, m_low], axis=0), bs[...])
    yb[...] = both[0:W] + both[W:]
    middle = slice(LANES, 2 * LANES)
    nothing = jnp.zeros((RANK, LANES), F32)
    first_core = jnp.logical_and(jnp.logical_not(on_diagonal), core == 0)
    second_core = jnp.logical_and(jnp.logical_not(on_diagonal), core == 1)

    @pl.when(first_core)
    def _():
        s2[0:64, :] = yb[0:64, 0:LANES]
        s2[64:128, :] = yb[0:64, middle]

    @pl.when(second_core)
    def _():
        s2[0:64, :] = yb[0:64, 0:LANES]
        s2[64:96, :] = yb[64:96, middle]
        s2[96:128, :] = nothing

    @pl.when(on_diagonal)
    def _():
        s2[0:32, :] = yb[64:96, 0:LANES]
        s2[32:64, :] = yb[64:96, middle]
        s2[64:96, :] = yb[64:96, 2 * LANES :]
        s2[96:128, :] = nothing

    def r3_copy(d):
        to = lax.rem(z + d, DEPTH)
        return remote(
            s2.at[pl.ds(pl.multiple_of(to * 8, 8), 8)],
            r3.at[d - 1],
            r3s.at[0],
            r3r.at[0],
            z_peer(to),
        )

    send(r3_copy, DEPTH, r3, r3s.at[0])
    drain(r3, r3r.at[0])
    z_own = pl.ds(pl.multiple_of(z * 8, 8), 8)
    s3[z_own, :] = s2[z_own, :] + jnp.sum(r3[...], axis=0)

    def g3_copy(d):
        return remote(
            s3.at[z_own],
            s3.at[z_own],
            g3s.at[0],
            g3r.at[0],
            z_peer(lax.rem(z + d, DEPTH)),
        )

    g3_bytes = s3.at[pl.ds(0, SHARE - 8)]
    send(g3_copy, DEPTH, g3_bytes, g3s.at[0])
    drain(g3_bytes, g3r.at[0])


    zb[...] = jnp.zeros_like(zb)

    @pl.when(first_core)
    def _():
        zb[0:64, 0:LANES] = s3[0:64, :]
        zb[0:64, middle] = s3[64:128, :]

    @pl.when(second_core)
    def _():
        zb[0:64, 0:LANES] = s3[0:64, :]
        zb[64:96, middle] = s3[64:96, :]

    @pl.when(on_diagonal)
    def _():
        zb[64:96, 0:LANES] = s3[0:32, :]
        zb[64:96, middle] = s3[32:64, :]
        zb[64:96, 2 * LANES :] = s3[64:96, :]

    z_high, z_low = split(zb[...])
    zs[0:LANES, :] = z_high
    zs[LANES:, :] = z_low
    onto = mm_t(bs[...], zs[...])
    ub[...] = (onto[:, 0:LANES] + onto[:, LANES:]).reshape(NEAR, ROWS, LANES)

    def u_copy(e):
        return remote(
            ub.at[e], urecv.at[e - 1], us.at[0], ur.at[0], near_peer(before(e))
        )

    send(u_copy, NEAR, urecv, us.at[0])

    pf[core, xx, yy] = s3[...]

    def g2_copy(portion, d):
        axis = 1 - portion
        at = portion * 3 + d - 1
        block = pf.at[core, xx, yy, pl.ds(portion * 64, 64)]
        to = lax.rem(side(axis) + d, SIDE)
        return remote(block, block, g2s.at[at], g2r.at[at], side_peer(axis, to))

    def line(portion, index):
        rows = pl.ds(portion * 64, 64)
        if portion == 0:
            return pf.at[core, index, pl.ds(0, SIDE), rows]
        return pf.at[core, pl.ds(0, SIDE), index, rows]

    def g1_copy(portion, d):
        at = portion * 3 + d - 1
        block = line(portion, side(portion))
        to = lax.rem(side(portion) + d, SIDE)
        return remote(block, block, g1s.at[at], g1r.at[at], side_peer(portion, to))

    for portion in range(2):
        for d in (2, 1, 3):
            send_one(g2_copy(portion, d))


    quads = mm_t(zs[...], zs[...])
    gram = quads[0:LANES, 0:LANES] + quads[LANES:, 0:LANES]
    gram = gram + (quads[0:LANES, LANES:] + quads[LANES:, LANES:])
    row_at = lax.broadcasted_iota(jnp.int32, (RANK, LANES), 0)
    lane_at = lax.broadcasted_iota(jnp.int32, (RANK, LANES), 1)
    beside = jnp.zeros((RANK, LANES), F32)
    for k in range(3):
        here = jnp.logical_and(lane_at >= k * RANK, lane_at < (k + 1) * RANK)
        beside = jnp.where(here, gram[k * RANK : (k + 1) * RANK], beside)
    gmine[...] = beside
    gs_copy = remote(gmine, gsib, gss.at[0], gsr.at[0], sibling)
    send_one(gs_copy)
    gs_copy.wait_recv()
    g_half = pl.ds(pl.multiple_of(core * 16, 16), 16)
    gall[plane] = gmine[g_half, :] + gsib[g_half, :]

    def gp_copy(d):
        return remote(
            gall.at[plane],
            gall.at[plane],
            gps.at[0],
            gpr.at[0],
            plane_peer(after(d)[1]),
        )

    far_first(PLANE, lambda d: gp_copy(d).start())
    gp_bytes = gall.at[pl.ds(0, PLANE - 1)]
    pending.append(lambda: drain(gp_bytes, gps.at[0]))

    drain(urecv, ur.at[0])
    img[1, plane_rows, :] = ub[0] + jnp.sum(urecv[...], axis=0)
    iz_copy = remote(
        img.at[1, plane_rows], img.at[0, plane_rows], izs.at[0], izr.at[0], opposite
    )
    send_one(iz_copy)

    def ix_copy(half, d):
        return remote(
            img.at[half, plane_rows],
            img.at[half, plane_rows],
            ixs.at[half],
            ixr.at[half],
            plane_peer(after(d)[1]),
        )

    def ix_bytes(half):
        return img.at[half, pl.ds(0, HALF - ROWS)]

    def ix_send(half):
        send(lambda d: ix_copy(half, d), PLANE, ix_bytes(half), ixs.at[half])

    def ix_receive(half):
        drain(ix_bytes(half), ixr.at[half])

    ix_send(1)

    for portion in range(2):
        for d in (1, 3, 2):
            g2_copy(portion, d).wait_recv()
        for d in (2, 1, 3):
            send_one(g1_copy(portion, d))

    drain(gp_bytes, gpr.at[0])
    ghalf[g_half, :] = jnp.sum(gall[...], axis=0)
    gh_copy = remote(
        ghalf.at[g_half], ghalf.at[g_half], ghs.at[0], ghr.at[0], sibling
    )
    send_one(gh_copy)
    gh_copy.wait_recv()

    left = [ghalf[...] for _ in range(3)]
    right = [(lane_at == row_at + k * RANK).astype(F32) for k in range(3)]
    def eliminate(j):
        for k in range(3):
            at = k * RANK + j
            pivot = left[k][j : j + 1, at : at + 1]
            column = left[k][:, at : at + 1] / pivot
            factor = jnp.where(row_at > j, column, 0.0)
            left[k] = left[k] - factor * left[k][j : j + 1, :]
            right[k] = right[k] - factor * right[k][j : j + 1, :]

    middle_step = RANK // 2
    for j in range(middle_step):
        eliminate(j)
    iz_copy.wait_recv()
    ix_send(0)
    for j in range(middle_step, RANK - 1):
        eliminate(j)
    inverse = []
    for k in range(3):
        diagonal = jnp.sum(
            jnp.where(lane_at == row_at + k * RANK, left[k], 0.0), axis=1, keepdims=True
        )
        inverse.append(right[k] / jnp.sqrt(diagonal))
    inverse.append(jnp.zeros((RANK, LANES), F32))
    inverse = jnp.concatenate(inverse, axis=0)

    for side_half in range(2):
        qb[side_half, QB_USED:QB, :] = jnp.zeros((QB - QB_USED, LANES), F32)
    for half in (1, 0):
        ix_receive(half)
        if half == 0:
            for portion in range(2):
                for d in (1, 3, 2):
                    g1_copy(portion, d).wait_recv()
            gc_copy = remote(
                pf.at[core], pf.at[core], gcs.at[0], gcr.at[0], sibling
            )
            send_one(gc_copy)
        images = mm_t(img[half], inverse, HIGH) * (1.0 / GROUPS)
        img_high, img_low = split(images.T)
        for k in range(3):
            rows = slice(k * RANK, (k + 1) * RANK)
            both = jnp.concatenate([img_high[rows], img_low[rows]], axis=0)
            first = mm(both, acts[k, half, 0])
            second = mm(img_high[rows], acts[k, half, 1])
            share = first[0:RANK] + first[RANK:] + second
            for tile in range(FFL // LANES):
                part = share[:, tile * LANES : (tile + 1) * LANES]
                for block, row, start, count in pieces(
                    tile * W + k * RANK, RANK, QB_USED
                ):
                    piece = part[start : start + count]
                    if half == 0:
                        piece = piece + qb[block, row : row + count, :]
                    qb[block, row : row + count, :] = piece

    qc_copy = remote(qb.at[1 - core], qcrecv, qcs.at[0], qcr.at[0], sibling)
    send_one(qc_copy)

    qc_copy.wait_recv()
    qh[...] = qb[core] + qcrecv[...]

    def zl_peer(index):
        return (index * 2 + core, mp)

    def q_rows(index):
        return pl.ds(pl.multiple_of(index * QS, 8), QS)

    across = lax.rem(zl + 4, ZLO)
    run_start = zl - lax.rem(zl, 4)

    def in_run(d):
        return run_start + lax.rem(zl + d, 4)

    def qr_copy(d, far):
        to = in_run(d)
        owner = lax.rem(to + 4, ZLO) if far else to
        return remote(
            qh.at[q_rows(owner)],
            qr.at[far, d - 1],
            qrs.at[far],
            qrr.at[far],
            zl_peer(to),
        )

    for far_chunk in (1, 0):
        for d in (2, 3, 1):
            qr_copy(d, far_chunk).start()

    q_own, q_across = q_rows(zl), q_rows(across)
    drain(qr.at[1], qrr.at[1])
    qx[...] = qh[q_across, :] + jnp.sum(qr[1], axis=0)
    qx_copy = remote(qx, qy, qrs.at[2], qrr.at[2], zl_peer(across))
    send_one(qx_copy)

    gc_copy.wait_recv()

    for of_core in range(2):
        for chip in range(PLANE):
            for row, k, tile in tiles_of(of_core, chip)[1]:
                ptf[k * RANK : (k + 1) * RANK, tile * LANES : (tile + 1) * LANES] = pf[
                    of_core, chip // SIDE, chip % SIDE, row : row + RANK, :
                ]
    scaled = inverse[0:W, 0:W] * math.sqrt(D)

    def left_factor(tile, carry):
        at = pl.ds(pl.multiple_of(tile * 4 * LANES, LANES), 4 * LANES)
        p_out[:, at] = mm(scaled, ptf[:, at], HIGH)
        return carry

    lax.fori_loop(0, D // (4 * LANES), left_factor, 0)

    finish()

    drain(qr.at[0], qrr.at[0])
    for far_chunk in range(2):
        drain(qr.at[far_chunk], qrs.at[far_chunk])
    qx_copy.wait_recv()
    qf[core, q_own, :] = qh[q_own, :] + jnp.sum(qr[0], axis=0) + qy[...]

    def qg_copy(rows, kind, to):
        block = qf.at[core, rows]
        return remote(block, block, qgs.at[kind], qgr.at[kind], zl_peer(to))

    def run_rows(start):
        return qf.at[core, pl.ds(pl.multiple_of(start * QS, 8), 4 * QS)]

    def qd_copy(start, kind):
        block = run_rows(start)
        return remote(block, block, qds.at[kind], qdr.at[kind], sibling)

    qa_copy = qg_copy(q_own, 2, across)
    send_one(qa_copy)
    for d in (2, 3, 1):
        qg_copy(q_own, 0, in_run(d)).start()
    qa_copy.wait_recv()
    for d in (2, 3, 1):
        qg_copy(q_across, 1, in_run(d)).start()
    run_bytes = qr.at[0]
    drain(run_bytes, qgr.at[0])
    send_one(qd_copy(run_start, 0))
    drain(run_bytes, qgr.at[1])
    send_one(qd_copy(4 - run_start, 1))
    for kind in range(2):
        drain(run_bytes, qgs.at[kind])
    for kind in range(2):
        qd_copy(run_start, kind).wait_recv()

    for tile in range(FFL // LANES):
        parts = [
            qf[half, row : row + count, :]
            for half, row, _, count in pieces(tile * W, W, QB_USED)
        ]
        whole = parts[0] if len(parts) == 1 else jnp.concatenate(parts, axis=0)
        q_out[:, tile * LANES : (tile + 1) * LANES] = whole

    finish()


def deliver(p_ref, q_ref, p_out, q_out, go):
    count = 6
    parts = [pl.ds(i * (W // count), W // count) for i in range(count)]
    copies = [
        pltpu.make_async_copy(p_ref.at[part], p_out.at[part], go.at[i])
        for i, part in enumerate(parts)
    ]
    copies.append(pltpu.make_async_copy(q_ref, q_out, go.at[count]))
    for copy in copies:
        copy.start()
    for copy in copies:
        copy.wait()


def on_device(inputs, out_grad, gate_pre, up_pre, hidden_grad, q_start):
    vmem = pl.BlockSpec(memory_space=pltpu.VMEM)
    far = pl.BlockSpec(memory_space=pl.ANY)
    buffers = [
        pltpu.VMEM((2, PLANE, ROWS, FFL), BF16),
        pltpu.VMEM((2, PLANE, ROWS, FFL), BF16),
        pltpu.VMEM((2, PLANE, ROWS, FFL), BF16),
        pltpu.VMEM((3, 2, 2, HALF, FFL), BF16),
        pltpu.VMEM((2 * LANES, FFL), BF16),
        pltpu.VMEM((2, HALF, LANES), F32),
        pltpu.VMEM((2, PLANE - 1, ROWS, LANES), F32),
        pltpu.VMEM((ROWS, LANES), F32),
        pltpu.VMEM((16, LANES), F32),
        pltpu.VMEM((2 * TILES, ROWS, LANES), F32),
        pltpu.VMEM((NEAR, 3, ROWS, LANES), F32),
        pltpu.VMEM((NEAR * ROWS, 3 * LANES), BF16),
        pltpu.VMEM((NEAR, ROWS, LANES), F32),
        pltpu.VMEM((W, 3 * LANES), F32),
        pltpu.VMEM((SHARE, LANES), F32),
        pltpu.VMEM((DEPTH - 1, 8, LANES), F32),
        pltpu.VMEM((SHARE, LANES), F32),
        pltpu.VMEM((LANES, 3 * LANES), F32),
        pltpu.VMEM((2 * LANES, 3 * LANES), BF16),
        pltpu.VMEM((NEAR, ROWS, LANES), F32),
        pltpu.VMEM((NEAR - 1, ROWS, LANES), F32),
        pltpu.VMEM((RANK, LANES), F32),
        pltpu.VMEM((RANK, LANES), F32),
        pltpu.VMEM((PLANE, 16, LANES), F32),
        pltpu.VMEM((RANK, LANES), F32),
        pltpu.VMEM((2, SIDE, SIDE, SHARE, LANES), F32),
        pltpu.VMEM((W, D), F32),
        pltpu.VMEM((2, HALF, LANES), F32),
        pltpu.VMEM((2, QB, LANES), F32),
        pltpu.VMEM((QB, LANES), F32),
        pltpu.VMEM((QB, LANES), F32),
        pltpu.VMEM((2, 3, QS, LANES), F32),
        pltpu.VMEM((QS, LANES), F32),
        pltpu.VMEM((QS, LANES), F32),
        pltpu.VMEM((2, QB, LANES), F32),
    ]
    counts = [12]
    counts += [2, 2, 1, 1]
    counts += [1, 2, 1, 1]
    counts += [1, 1, 1, 1]
    counts += [1, 1]
    counts += [1, 1, 1, 1, 1, 1]
    counts += [6, 6, 6, 6, 1, 1]
    counts += [1, 1, 2, 2]
    counts += [1, 1, 3, 3, 3, 3, 2, 2]
    flags = [pltpu.SemaphoreType.DMA((count,)) for count in counts]
    by_half = [
        array.reshape(PLANE, 2, ROWS, FFL) for array in (gate_pre, up_pre, hidden_grad)
    ]
    p_turned, q_turned = pl.pallas_call(
        kernel,
        out_shape=(pltpu.VMEM((W, D), F32), pltpu.VMEM((W, FFL), F32)),
        in_specs=[vmem, vmem, far, far, far, vmem],
        out_specs=(vmem, vmem),
        scratch_shapes=buffers + flags,
        compiler_params=pltpu.CompilerParams(
            collective_id=0, has_side_effects=True, vmem_limit_bytes=56 * 2**20
        ),
        name="power_step",
    )(inputs, out_grad, *by_half, q_start.T)
    shapes = (
        jax.ShapeDtypeStruct((W, D), F32),
        jax.ShapeDtypeStruct((W, FFL), F32),
    )
    p_turned, q_turned = pl.pallas_call(
        deliver,
        out_shape=shapes,
        in_specs=[vmem, vmem],
        out_specs=(far, far),
        scratch_shapes=[
            pltpu.SemaphoreType.DMA((7,)),
        ],
        name="deliver",
    )(
        pltpu.with_memory_space_constraint(p_turned, pltpu.VMEM),
        pltpu.with_memory_space_constraint(q_turned, pltpu.VMEM),
    )
    return p_turned.T, q_turned.T


def solution(mesh):
    in_specs = (
        P(("dp", "mp"), None),
        P(("dp", "mp"), None),
        P("dp", "mp"),
        P("dp", "mp"),
        P("dp", "mp"),
        P("mp", None),
    )
    out_specs = (P(), P("mp", None))
    return jax.shard_map(
        on_device, mesh=mesh, in_specs=in_specs, out_specs=out_specs, check_vma=False
    )
```

```python
import functools
import math

import jax
import jax.numpy as jnp
from jax import lax
from jax.experimental import pallas as pl
from jax.experimental.pallas import tpu as pltpu
from jax.sharding import PartitionSpec as P

MESH = pl.DeviceIdType.MESH
F32 = jnp.float32
BF16 = jnp.bfloat16
HIGH = lax.Precision.HIGHEST

D = 4608
TOK = 512
FFL = 1152
ROWS = 16
RANK = 32
W = 3 * RANK
LANES = 128
SIDE = 4
PLANE = SIDE * SIDE
ZLO = 8
DEPTH = 16
GROUPS = 16

TILES = D // LANES
NEAR = 2 * PLANE
SHARE = 128
QB = 448
QB_USED = 432
QS = QB // ZLO
HALF = TOK // 2


def split(value):
    high = value.astype(BF16)
    low = (value - high.astype(F32)).astype(BF16)
    return high, low


def mm(left, right, precision=None):
    return lax.dot_general(
        left,
        right,
        (((1,), (0,)), ((), ())),
        preferred_element_type=F32,
        precision=precision,
    )


def mm_t(left, right, precision=None):
    return lax.dot_general(
        left,
        right,
        (((1,), (1,)), ((), ())),
        preferred_element_type=F32,
        precision=precision,
    )


def tiles_of(core, plane):
    x, y = divmod(plane, SIDE)
    if x == y:
        first = 12 + 6 * x + 3 * core
        return (
            [(1, first + i) for i in range(3)],
            [(32 * i, 2, first + i) for i in range(3)],
        )
    at = plane - plane // (SIDE + 1) - 1
    if core == 0:
        return (
            [(0, 3 * at), (0, 3 * at + 1)],
            [
                (0, 0, 3 * at),
                (32, 1, 3 * at),
                (64, 0, 3 * at + 1),
                (96, 1, 3 * at + 1),
            ],
        )
    return (
        [(0, 3 * at + 2), (1, at)],
        [(0, 0, 3 * at + 2), (32, 1, 3 * at + 2), (64, 2, at)],
    )


def staged(core, plane):
    x, y = lax.div(plane, SIDE), lax.rem(plane, SIDE)
    at = plane - lax.div(plane, SIDE + 1) - 1
    return jnp.where(x == y, 48 + 6 * x + 3 * core, 4 * at + 2 * core)


def pieces(start, count, used):
    out = []
    at = start
    while at < start + count:
        block, row = divmod(at, used)
        here = min(used - row, start + count - at)
        out.append((block, row, at - start, here))
        at += here
    return out


def kernel(
    in_ref,
    og_ref,
    gate_ref,
    up_ref,
    cot_ref,
    q_ref,
    p_out,
    q_out,
    gate_in,
    up_in,
    cot_in,
    acts,
    qs,
    mpart,
    mrecv,
    maway,
    mzrecv,
    bst,
    bt,
    bs,
    mall,
    yb,
    s2,
    r3,
    s3,
    zb,
    zs,
    ub,
    urecv,
    gmine,
    gsib,
    gall,
    ghalf,
    pf,
    ptf,
    img,
    qb,
    qcrecv,
    qh,
    qr,
    qx,
    qy,
    qf,
    loads,
    ms,
    mr,
    mzs,
    mzr,
    bsend,
    brecv,
    mas,
    mar,
    r3s,
    r3r,
    g3s,
    g3r,
    us,
    ur,
    gss,
    gsr,
    gps,
    gpr,
    ghs,
    ghr,
    g2s,
    g2r,
    g1s,
    g1r,
    gcs,
    gcr,
    izs,
    izr,
    ixs,
    ixr,
    qcs,
    qcr,
    qrs,
    qrr,
    qgs,
    qgr,
    qds,
    qdr,
):
    dp, mp = lax.axis_index("dp"), lax.axis_index("mp")
    core, zl = lax.rem(dp, 2), lax.div(dp, 2)
    zh, plane = lax.rem(mp, 2), lax.div(mp, 2)
    xx, yy = lax.div(plane, SIDE), lax.rem(plane, SIDE)
    z = zh * ZLO + zl
    on_diagonal = xx == yy
    sibling = (zl * 2 + 1 - core, mp)
    opposite = (dp, plane * 2 + 1 - zh)

    def plane_peer(index):
        return (dp, index * 2 + zh)

    def z_peer(index):
        return (lax.rem(index, ZLO) * 2 + core, plane * 2 + lax.div(index, ZLO))

    def side_peer(axis, index):
        along_x = (dp, (index * SIDE + yy) * 2 + zh)
        along_y = (dp, (xx * SIDE + index) * 2 + zh)
        return along_x if axis == 0 else along_y

    def side(axis):
        return xx if axis == 0 else yy

    def after(e):
        x = lax.rem(xx + lax.div(lax.rem(e, PLANE), SIDE), SIDE)
        y = lax.rem(yy + lax.rem(e, SIDE), SIDE)
        return lax.rem(core + lax.div(e, PLANE), 2), x * SIDE + y

    def before(e):
        x = lax.rem(xx + SIDE - lax.div(lax.rem(e, PLANE), SIDE), SIDE)
        y = lax.rem(yy + SIDE - lax.rem(e, SIDE), SIDE)
        return lax.rem(core + lax.div(e, PLANE), 2), x * SIDE + y

    def near_peer(place):
        return (zl * 2 + place[0], place[1] * 2 + zh)

    def remote(src, dst, send, recv, to):
        return pltpu.make_async_remote_copy(
            src_ref=src,
            dst_ref=dst,
            send_sem=send,
            recv_sem=recv,
            device_id=to,
            device_id_type=MESH,
        )

    def around(count, body, first=1):
        def step(index, carry):
            body(index)
            return carry

        lax.fori_loop(first, count, step, 0)

    pending = []

    def far_first(count, body):
        if count == NEAR:
            body(jnp.int32(PLANE))
            around(15, lambda i: body(PLANE + 1 + lax.rem(25 - i, 15)), first=0)
            around(15, lambda i: body(1 + lax.rem(25 - i, 15)), first=0)
        elif count == PLANE:
            around(15, lambda i: body(1 + lax.rem(25 - i, 15)), first=0)
        else:
            half = count // 2
            around(
                count - 1,
                lambda i: body(
                    half + (1 - 2 * lax.rem(i, 2)) * lax.div(i + 1, 2)
                ),
                first=0,
            )

    def drain(bytes_of, semaphore):
        pltpu.make_async_copy(bytes_of, bytes_of, semaphore).wait()

    def send(make, count, bytes_of, semaphore):
        far_first(count, lambda d: make(d).start())
        pending.append(lambda: drain(bytes_of, semaphore))

    def send_one(copy):
        copy.start()
        pending.append(copy.wait_send)

    def finish():
        while pending:
            pending.pop(0)()

    barrier = pltpu.get_barrier_semaphore()

    def greet(to):
        pl.semaphore_signal(barrier, inc=1, device_id=to, device_id_type=MESH)

    around(DEPTH, lambda d: greet(z_peer(lax.rem(z + d, DEPTH))))
    around(NEAR, lambda e: greet(near_peer(after(e))))

    quarter = PLANE // 2

    def load(half, part, which):
        chips = pl.ds(part * quarter, quarter)
        src, dst = (
            (gate_ref, gate_in),
            (up_ref, up_in),
            (cot_ref, cot_in),
        )[which]
        return pltpu.make_async_copy(
            src.at[chips, zh if half else 1 - zh],
            dst.at[half, chips],
            loads.at[half * 6 + part * 3 + which],
        )

    for half in range(2):
        for part in range(2):
            for which in range(3):
                load(half, part, which).start()

    place = 0
    for chip_type in (False, True):
        for chip in range(PLANE):
            if (chip // SIDE == chip % SIDE) != chip_type:
                continue
            for of_core in range(2):
                for array, tile in tiles_of(of_core, chip)[0]:
                    source = (in_ref, og_ref)[array]
                    bst[place] = source[:, tile * LANES : (tile + 1) * LANES].astype(F32)
                    place += 1

    def activate(half, i):
        rows = pl.ds(pl.multiple_of(i * ROWS, ROWS), ROWS)
        g = gate_in[half, i].astype(F32)
        u = up_in[half, i].astype(F32)
        e = cot_in[half, i].astype(F32)
        s = 1.0 / (1.0 + jnp.exp(-g))
        silu = g * s
        values = (e * u * s * (1.0 + g * (1.0 - s)), e * silu, silu * u)
        for k, value in enumerate(values):
            high, low = split(value)
            acts[k, half, 0, rows, :] = high
            acts[k, half, 1, rows, :] = low

    def b_copy(e, count):
        to = after(e)
        return remote(
            bst.at[pl.ds(staged(*to), count)],
            bt.at[e, pl.ds(0, count)],
            bsend.at[0],
            brecv.at[lax.div(e, PLANE)],
            near_peer(to),
        )

    def b_each(e, act, diagonal):
        @pl.when(diagonal)
        def _():
            act(b_copy(e, 3))

        @pl.when(jnp.logical_not(diagonal))
        def _():
            act(b_copy(e, 2))

    def to_diagonal(e):
        chip = after(e)[1]
        return lax.div(chip, SIDE) == lax.rem(chip, SIDE)

    q_high, q_low = split(q_ref[...])
    qs[...] = jnp.zeros_like(qs)
    qs[0:W, :] = q_high
    qs[LANES : LANES + W, :] = q_low

    lane = lax.broadcasted_iota(jnp.int32, (HALF, LANES), 1)

    def mix(half):
        for k in range(3):
            first = mm_t(acts[k, half, 0], qs[...])
            second = mm_t(acts[k, half, 1], qs[0:LANES, :])
            both = first[:, 0:LANES] + first[:, LANES:] + second
            if k == 0:
                mpart[half] = both
            else:
                mpart[half] = jnp.where(lane >= k * RANK, both, mpart[half])

    plane_rows = pl.ds(pl.multiple_of(plane * ROWS, ROWS), ROWS)

    def m_copy(half, d):
        to = after(d)[1]
        return remote(
            mpart.at[half, pl.ds(pl.multiple_of(to * ROWS, ROWS), ROWS)],
            mrecv.at[half, d - 1],
            ms.at[half],
            mr.at[half],
            plane_peer(to),
        )

    def m_send(half):
        send(lambda d: m_copy(half, d), PLANE, mrecv.at[half], ms.at[half])

    def m_sum(half):
        drain(mrecv.at[half], mr.at[half])
        return mpart[half, plane_rows, :] + jnp.sum(mrecv[half], axis=0)

    for half in range(2):
        for part in range(2):
            for which in range(3):
                load(half, part, which).wait()
            around(
                (part + 1) * quarter,
                lambda i: activate(half, i),
                first=part * quarter,
            )
        mix(half)
        if half == 0:
            pl.semaphore_wait(barrier, DEPTH - 1 + NEAR - 1)
        m_send(half)
        if half == 0:
            around(PLANE, lambda e: b_each(e, lambda c: c.start(), to_diagonal(e)))
    maway[...] = m_sum(0)
    mz_copy = remote(maway, mzrecv, mzs.at[0], mzr.at[0], opposite)
    send_one(mz_copy)
    around(
        NEAR, lambda e: b_each(e, lambda c: c.start(), to_diagonal(e)), first=PLANE
    )

    def b_sent():
        for count, here in ((3, on_diagonal), (2, jnp.logical_not(on_diagonal))):

            @pl.when(here)
            def _():
                drain(bst.at[pl.ds(0, 2 * TILES - count)], bsend.at[0])

    pending.append(b_sent)

    def b_receive(group):
        slots = pl.ds(1, PLANE - 1) if group == 0 else pl.ds(PLANE, PLANE)
        for count, here in ((3, on_diagonal), (2, jnp.logical_not(on_diagonal))):

            @pl.when(here)
            def _():
                drain(bt.at[slots, pl.ds(0, count)], brecv.at[group])

    mhome = m_sum(1)

    own_tiles = staged(core, plane)
    for tile in range(2):
        bt[0, tile] = bst[own_tiles + tile]

    @pl.when(on_diagonal)
    def _():
        bt[0, 2] = bst[own_tiles + 2]

    def round_rows(e):
        rows = pl.ds(pl.multiple_of(e * ROWS, ROWS), ROWS)
        for tile in range(2):
            bs[rows, tile * LANES : (tile + 1) * LANES] = bt[e, tile].astype(BF16)

        @pl.when(on_diagonal)
        def _():
            bs[rows, 2 * LANES :] = bt[e, 2].astype(BF16)

        @pl.when(jnp.logical_not(on_diagonal))
        def _():
            bs[rows, 2 * LANES :] = jnp.zeros((ROWS, LANES), BF16)

    b_receive(0)
    around(PLANE, round_rows, first=0)

    mz_copy.wait_recv()
    mall[0] = (mhome + mzrecv[...]) * (1.0 / GROUPS)

    def ma_copy(e):
        return remote(
            mall.at[0], mall.at[e], mas.at[0], mar.at[0], near_peer(after(e))
        )

    ma_bytes = mall.at[pl.ds(1, NEAR - 1)]
    send(ma_copy, NEAR, ma_bytes, mas.at[0])

    b_receive(1)
    around(NEAR, round_rows, first=PLANE)
    drain(ma_bytes, mar.at[0])

    m_turned = mall[...].reshape(NEAR * ROWS, LANES).T
    m_high, m_low = split(m_turned[0:W])
    both = mm(jnp.concatenate([m_high, m_low], axis=0), bs[...])
    yb[...] = both[0:W] + both[W:]
    middle = slice(LANES, 2 * LANES)
    nothing = jnp.zeros((RANK, LANES), F32)
    first_core = jnp.logical_and(jnp.logical_not(on_diagonal), core == 0)
    second_core = jnp.logical_and(jnp.logical_not(on_diagonal), core == 1)

    @pl.when(first_core)
    def _():
        s2[0:64, :] = yb[0:64, 0:LANES]
        s2[64:128, :] = yb[0:64, middle]

    @pl.when(second_core)
    def _():
        s2[0:64, :] = yb[0:64, 0:LANES]
        s2[64:96, :] = yb[64:96, middle]
        s2[96:128, :] = nothing

    @pl.when(on_diagonal)
    def _():
        s2[0:32, :] = yb[64:96, 0:LANES]
        s2[32:64, :] = yb[64:96, middle]
        s2[64:96, :] = yb[64:96, 2 * LANES :]
        s2[96:128, :] = nothing

    def r3_copy(d):
        to = lax.rem(z + d, DEPTH)
        return remote(
            s2.at[pl.ds(pl.multiple_of(to * 8, 8), 8)],
            r3.at[d - 1],
            r3s.at[0],
            r3r.at[0],
            z_peer(to),
        )

    send(r3_copy, DEPTH, r3, r3s.at[0])
    drain(r3, r3r.at[0])
    z_own = pl.ds(pl.multiple_of(z * 8, 8), 8)
    s3[z_own, :] = s2[z_own, :] + jnp.sum(r3[...], axis=0)

    def g3_copy(d):
        return remote(
            s3.at[z_own],
            s3.at[z_own],
            g3s.at[0],
            g3r.at[0],
            z_peer(lax.rem(z + d, DEPTH)),
        )

    g3_bytes = s3.at[pl.ds(0, SHARE - 8)]
    send(g3_copy, DEPTH, g3_bytes, g3s.at[0])
    drain(g3_bytes, g3r.at[0])


    zb[...] = jnp.zeros_like(zb)

    @pl.when(first_core)
    def _():
        zb[0:64, 0:LANES] = s3[0:64, :]
        zb[0:64, middle] = s3[64:128, :]

    @pl.when(second_core)
    def _():
        zb[0:64, 0:LANES] = s3[0:64, :]
        zb[64:96, middle] = s3[64:96, :]

    @pl.when(on_diagonal)
    def _():
        zb[64:96, 0:LANES] = s3[0:32, :]
        zb[64:96, middle] = s3[32:64, :]
        zb[64:96, 2 * LANES :] = s3[64:96, :]

    z_high, z_low = split(zb[...])
    zs[0:LANES, :] = z_high
    zs[LANES:, :] = z_low
    onto = mm_t(bs[...], zs[...])
    ub[...] = (onto[:, 0:LANES] + onto[:, LANES:]).reshape(NEAR, ROWS, LANES)

    def u_copy(e):
        return remote(
            ub.at[e], urecv.at[e - 1], us.at[0], ur.at[0], near_peer(before(e))
        )

    send(u_copy, NEAR, urecv, us.at[0])

    pf[core, xx, yy] = s3[...]

    def g2_copy(portion, d):
        axis = 1 - portion
        at = portion * 3 + d - 1
        block = pf.at[core, xx, yy, pl.ds(portion * 64, 64)]
        to = lax.rem(side(axis) + d, SIDE)
        return remote(block, block, g2s.at[at], g2r.at[at], side_peer(axis, to))

    def line(portion, index):
        rows = pl.ds(portion * 64, 64)
        if portion == 0:
            return pf.at[core, index, pl.ds(0, SIDE), rows]
        return pf.at[core, pl.ds(0, SIDE), index, rows]

    def g1_copy(portion, d):
        at = portion * 3 + d - 1
        block = line(portion, side(portion))
        to = lax.rem(side(portion) + d, SIDE)
        return remote(block, block, g1s.at[at], g1r.at[at], side_peer(portion, to))

    for portion in range(2):
        for d in (2, 1, 3):
            send_one(g2_copy(portion, d))


    quads = mm_t(zs[...], zs[...])
    gram = quads[0:LANES, 0:LANES] + quads[LANES:, 0:LANES]
    gram = gram + (quads[0:LANES, LANES:] + quads[LANES:, LANES:])
    row_at = lax.broadcasted_iota(jnp.int32, (RANK, LANES), 0)
    lane_at = lax.broadcasted_iota(jnp.int32, (RANK, LANES), 1)
    beside = jnp.zeros((RANK, LANES), F32)
    for k in range(3):
        here = jnp.logical_and(lane_at >= k * RANK, lane_at < (k + 1) * RANK)
        beside = jnp.where(here, gram[k * RANK : (k + 1) * RANK], beside)
    gmine[...] = beside
    gs_copy = remote(gmine, gsib, gss.at[0], gsr.at[0], sibling)
    send_one(gs_copy)
    gs_copy.wait_recv()
    g_half = pl.ds(pl.multiple_of(core * 16, 16), 16)
    gall[plane] = gmine[g_half, :] + gsib[g_half, :]

    def gp_copy(d):
        return remote(
            gall.at[plane],
            gall.at[plane],
            gps.at[0],
            gpr.at[0],
            plane_peer(after(d)[1]),
        )

    far_first(PLANE, lambda d: gp_copy(d).start())
    gp_bytes = gall.at[pl.ds(0, PLANE - 1)]
    pending.append(lambda: drain(gp_bytes, gps.at[0]))

    drain(urecv, ur.at[0])
    img[1, plane_rows, :] = ub[0] + jnp.sum(urecv[...], axis=0)
    iz_copy = remote(
        img.at[1, plane_rows], img.at[0, plane_rows], izs.at[0], izr.at[0], opposite
    )
    send_one(iz_copy)

    def ix_copy(half, d):
        return remote(
            img.at[half, plane_rows],
            img.at[half, plane_rows],
            ixs.at[half],
            ixr.at[half],
            plane_peer(after(d)[1]),
        )

    def ix_bytes(half):
        return img.at[half, pl.ds(0, HALF - ROWS)]

    def ix_send(half):
        send(lambda d: ix_copy(half, d), PLANE, ix_bytes(half), ixs.at[half])

    def ix_receive(half):
        drain(ix_bytes(half), ixr.at[half])

    ix_send(1)

    for portion in range(2):
        for d in (1, 3, 2):
            g2_copy(portion, d).wait_recv()
        for d in (2, 1, 3):
            send_one(g1_copy(portion, d))

    drain(gp_bytes, gpr.at[0])
    ghalf[g_half, :] = jnp.sum(gall[...], axis=0)
    gh_copy = remote(
        ghalf.at[g_half], ghalf.at[g_half], ghs.at[0], ghr.at[0], sibling
    )
    send_one(gh_copy)
    gh_copy.wait_recv()

    left = [ghalf[...] for _ in range(3)]
    right = [(lane_at == row_at + k * RANK).astype(F32) for k in range(3)]
    def eliminate(j):
        for k in range(3):
            at = k * RANK + j
            pivot = left[k][j : j + 1, at : at + 1]
            column = left[k][:, at : at + 1] / pivot
            factor = jnp.where(row_at > j, column, 0.0)
            left[k] = left[k] - factor * left[k][j : j + 1, :]
            right[k] = right[k] - factor * right[k][j : j + 1, :]

    middle_step = RANK // 2
    for j in range(middle_step):
        eliminate(j)
    iz_copy.wait_recv()
    ix_send(0)
    for j in range(middle_step, RANK - 1):
        eliminate(j)
    inverse = []
    for k in range(3):
        diagonal = jnp.sum(
            jnp.where(lane_at == row_at + k * RANK, left[k], 0.0), axis=1, keepdims=True
        )
        inverse.append(right[k] / jnp.sqrt(diagonal))
    inverse.append(jnp.zeros((RANK, LANES), F32))
    inverse = jnp.concatenate(inverse, axis=0)

    for side_half in range(2):
        qb[side_half, QB_USED:QB, :] = jnp.zeros((QB - QB_USED, LANES), F32)
    for half in (1, 0):
        ix_receive(half)
        if half == 0:
            for portion in range(2):
                for d in (1, 3, 2):
                    g1_copy(portion, d).wait_recv()
            gc_copy = remote(
                pf.at[core], pf.at[core], gcs.at[0], gcr.at[0], sibling
            )
            send_one(gc_copy)
        images = mm_t(img[half], inverse, HIGH) * (1.0 / GROUPS)
        img_high, img_low = split(images.T)
        for k in range(3):
            rows = slice(k * RANK, (k + 1) * RANK)
            both = jnp.concatenate([img_high[rows], img_low[rows]], axis=0)
            first = mm(both, acts[k, half, 0])
            second = mm(img_high[rows], acts[k, half, 1])
            share = first[0:RANK] + first[RANK:] + second
            for tile in range(FFL // LANES):
                part = share[:, tile * LANES : (tile + 1) * LANES]
                for block, row, start, count in pieces(
                    tile * W + k * RANK, RANK, QB_USED
                ):
                    piece = part[start : start + count]
                    if half == 0:
                        piece = piece + qb[block, row : row + count, :]
                    qb[block, row : row + count, :] = piece

    qc_copy = remote(qb.at[1 - core], qcrecv, qcs.at[0], qcr.at[0], sibling)
    send_one(qc_copy)

    qc_copy.wait_recv()
    qh[...] = qb[core] + qcrecv[...]

    def zl_peer(index):
        return (index * 2 + core, mp)

    def q_rows(index):
        return pl.ds(pl.multiple_of(index * QS, 8), QS)

    across = lax.rem(zl + 4, ZLO)
    run_start = zl - lax.rem(zl, 4)

    def in_run(d):
        return run_start + lax.rem(zl + d, 4)

    def qr_copy(d, far):
        to = in_run(d)
        owner = lax.rem(to + 4, ZLO) if far else to
        return remote(
            qh.at[q_rows(owner)],
            qr.at[far, d - 1],
            qrs.at[far],
            qrr.at[far],
            zl_peer(to),
        )

    for far_chunk in (1, 0):
        for d in (2, 3, 1):
            qr_copy(d, far_chunk).start()

    q_own, q_across = q_rows(zl), q_rows(across)

    def qx_copy(far):
        return remote(
            qx.at[far],
            qy.at[1 - far],
            qrs.at[2 + far],
            qrr.at[3 - far],
            zl_peer(across),
        )

    for far_chunk, rows in ((1, q_across), (0, q_own)):
        drain(qr.at[far_chunk], qrr.at[far_chunk])
        qx[far_chunk] = qh[rows, :] + jnp.sum(qr[far_chunk], axis=0)
        qx_copy(far_chunk).start()

    gc_copy.wait_recv()

    for of_core in range(2):
        for chip in range(PLANE):
            for row, k, tile in tiles_of(of_core, chip)[1]:
                ptf[k * RANK : (k + 1) * RANK, tile * LANES : (tile + 1) * LANES] = pf[
                    of_core, chip // SIDE, chip % SIDE, row : row + RANK, :
                ]
    scaled = inverse[0:W, 0:W] * math.sqrt(D)

    def left_factor(tile, carry):
        at = pl.ds(pl.multiple_of(tile * 4 * LANES, LANES), 4 * LANES)
        p_out[:, at] = mm(scaled, ptf[:, at], HIGH)
        return carry

    lax.fori_loop(0, D // (4 * LANES), left_factor, 0)

    finish()

    def qg_copy(rows, kind, to):
        block = qf.at[core, rows]
        return remote(block, block, qgs.at[kind], qgr.at[kind], zl_peer(to))

    def run_rows(start):
        return qf.at[core, pl.ds(pl.multiple_of(start * QS, 8), 4 * QS)]

    def qd_copy(start, kind):
        block = run_rows(start)
        return remote(block, block, qds.at[kind], qdr.at[kind], sibling)

    for kind, rows in ((0, q_own), (1, q_across)):
        qx_copy(1 - kind).wait_recv()
        qf[core, rows, :] = qx[kind] + qy[kind]
        for d in (2, 3, 1):
            qg_copy(rows, kind, in_run(d)).start()
    run_bytes = qr.at[0]
    drain(run_bytes, qgr.at[0])
    send_one(qd_copy(run_start, 0))
    drain(run_bytes, qgr.at[1])
    send_one(qd_copy(4 - run_start, 1))
    for kind in range(2):
        drain(run_bytes, qrs.at[kind])
        qx_copy(kind).wait_send()
        drain(run_bytes, qgs.at[kind])
    for kind in range(2):
        qd_copy(run_start, kind).wait_recv()

    for tile in range(FFL // LANES):
        parts = [
            qf[half, row : row + count, :]
            for half, row, _, count in pieces(tile * W, W, QB_USED)
        ]
        whole = parts[0] if len(parts) == 1 else jnp.concatenate(parts, axis=0)
        q_out[:, tile * LANES : (tile + 1) * LANES] = whole

    finish()


def deliver(p_ref, q_ref, p_out, q_out, go):
    count = 6
    parts = [pl.ds(i * (W // count), W // count) for i in range(count)]
    copies = [
        pltpu.make_async_copy(p_ref.at[part], p_out.at[part], go.at[i])
        for i, part in enumerate(parts)
    ]
    copies.append(pltpu.make_async_copy(q_ref, q_out, go.at[count]))
    for copy in copies:
        copy.start()
    for copy in copies:
        copy.wait()


def on_device(inputs, out_grad, gate_pre, up_pre, hidden_grad, q_start):
    vmem = pl.BlockSpec(memory_space=pltpu.VMEM)
    far = pl.BlockSpec(memory_space=pl.ANY)
    buffers = [
        pltpu.VMEM((2, PLANE, ROWS, FFL), BF16),
        pltpu.VMEM((2, PLANE, ROWS, FFL), BF16),
        pltpu.VMEM((2, PLANE, ROWS, FFL), BF16),
        pltpu.VMEM((3, 2, 2, HALF, FFL), BF16),
        pltpu.VMEM((2 * LANES, FFL), BF16),
        pltpu.VMEM((2, HALF, LANES), F32),
        pltpu.VMEM((2, PLANE - 1, ROWS, LANES), F32),
        pltpu.VMEM((ROWS, LANES), F32),
        pltpu.VMEM((16, LANES), F32),
        pltpu.VMEM((2 * TILES, ROWS, LANES), F32),
        pltpu.VMEM((NEAR, 3, ROWS, LANES), F32),
        pltpu.VMEM((NEAR * ROWS, 3 * LANES), BF16),
        pltpu.VMEM((NEAR, ROWS, LANES), F32),
        pltpu.VMEM((W, 3 * LANES), F32),
        pltpu.VMEM((SHARE, LANES), F32),
        pltpu.VMEM((DEPTH - 1, 8, LANES), F32),
        pltpu.VMEM((SHARE, LANES), F32),
        pltpu.VMEM((LANES, 3 * LANES), F32),
        pltpu.VMEM((2 * LANES, 3 * LANES), BF16),
        pltpu.VMEM((NEAR, ROWS, LANES), F32),
        pltpu.VMEM((NEAR - 1, ROWS, LANES), F32),
        pltpu.VMEM((RANK, LANES), F32),
        pltpu.VMEM((RANK, LANES), F32),
        pltpu.VMEM((PLANE, 16, LANES), F32),
        pltpu.VMEM((RANK, LANES), F32),
        pltpu.VMEM((2, SIDE, SIDE, SHARE, LANES), F32),
        pltpu.VMEM((W, D), F32),
        pltpu.VMEM((2, HALF, LANES), F32),
        pltpu.VMEM((2, QB, LANES), F32),
        pltpu.VMEM((QB, LANES), F32),
        pltpu.VMEM((QB, LANES), F32),
        pltpu.VMEM((2, 3, QS, LANES), F32),
        pltpu.VMEM((2, QS, LANES), F32),
        pltpu.VMEM((2, QS, LANES), F32),
        pltpu.VMEM((2, QB, LANES), F32),
    ]
    counts = [12]
    counts += [2, 2, 1, 1]
    counts += [1, 2, 1, 1]
    counts += [1, 1, 1, 1]
    counts += [1, 1]
    counts += [1, 1, 1, 1, 1, 1]
    counts += [6, 6, 6, 6, 1, 1]
    counts += [1, 1, 2, 2]
    counts += [1, 1, 4, 4, 2, 2, 2, 2]
    flags = [pltpu.SemaphoreType.DMA((count,)) for count in counts]
    by_half = [
        array.reshape(PLANE, 2, ROWS, FFL) for array in (gate_pre, up_pre, hidden_grad)
    ]
    p_turned, q_turned = pl.pallas_call(
        kernel,
        out_shape=(pltpu.VMEM((W, D), F32), pltpu.VMEM((W, FFL), F32)),
        in_specs=[vmem, vmem, far, far, far, vmem],
        out_specs=(vmem, vmem),
        scratch_shapes=buffers + flags,
        compiler_params=pltpu.CompilerParams(
            collective_id=0, has_side_effects=True, vmem_limit_bytes=56 * 2**20
        ),
        name="power_step",
    )(inputs, out_grad, *by_half, q_start.T)
    shapes = (
        jax.ShapeDtypeStruct((W, D), F32),
        jax.ShapeDtypeStruct((W, FFL), F32),
    )
    p_turned, q_turned = pl.pallas_call(
        deliver,
        out_shape=shapes,
        in_specs=[vmem, vmem],
        out_specs=(far, far),
        scratch_shapes=[
            pltpu.SemaphoreType.DMA((7,)),
        ],
        name="deliver",
    )(
        pltpu.with_memory_space_constraint(p_turned, pltpu.VMEM),
        pltpu.with_memory_space_constraint(q_turned, pltpu.VMEM),
    )
    return p_turned.T, q_turned.T


def solution(mesh):
    in_specs = (
        P(("dp", "mp"), None),
        P(("dp", "mp"), None),
        P("dp", "mp"),
        P("dp", "mp"),
        P("dp", "mp"),
        P("mp", None),
    )
    out_specs = (P(), P("mp", None))
    return jax.shard_map(
        on_device, mesh=mesh, in_specs=in_specs, out_specs=out_specs, check_vma=False
    )
```

```python
import functools
import math

import jax
import jax.numpy as jnp
from jax import lax
from jax.experimental import pallas as pl
from jax.experimental.pallas import tpu as pltpu
from jax.sharding import PartitionSpec as P

MESH = pl.DeviceIdType.MESH
F32 = jnp.float32
BF16 = jnp.bfloat16
HIGH = lax.Precision.HIGHEST

D = 4608
TOK = 512
FFL = 1152
ROWS = 16
RANK = 32
W = 3 * RANK
LANES = 128
SIDE = 4
PLANE = SIDE * SIDE
ZLO = 8
DEPTH = 16
GROUPS = 16

TILES = D // LANES
NEAR = 2 * PLANE
SHARE = 128
QB = 448
QB_USED = 432
QS = QB // ZLO
HALF = TOK // 2


def split(value):
    high = value.astype(BF16)
    low = (value - high.astype(F32)).astype(BF16)
    return high, low


def mm(left, right, precision=None):
    return lax.dot_general(
        left,
        right,
        (((1,), (0,)), ((), ())),
        preferred_element_type=F32,
        precision=precision,
    )


def mm_t(left, right, precision=None):
    return lax.dot_general(
        left,
        right,
        (((1,), (1,)), ((), ())),
        preferred_element_type=F32,
        precision=precision,
    )


def tiles_of(core, plane):
    x, y = divmod(plane, SIDE)
    if x == y:
        first = 12 + 6 * x + 3 * core
        return (
            [(1, first + i) for i in range(3)],
            [(32 * i, 2, first + i) for i in range(3)],
        )
    at = plane - plane // (SIDE + 1) - 1
    if core == 0:
        return (
            [(0, 3 * at), (0, 3 * at + 1)],
            [
                (0, 0, 3 * at),
                (32, 1, 3 * at),
                (64, 0, 3 * at + 1),
                (96, 1, 3 * at + 1),
            ],
        )
    return (
        [(0, 3 * at + 2), (1, at)],
        [(0, 0, 3 * at + 2), (32, 1, 3 * at + 2), (64, 2, at)],
    )


def staged(core, plane):
    x, y = lax.div(plane, SIDE), lax.rem(plane, SIDE)
    at = plane - lax.div(plane, SIDE + 1) - 1
    return jnp.where(x == y, 48 + 6 * x + 3 * core, 4 * at + 2 * core)


def pieces(start, count, used):
    out = []
    at = start
    while at < start + count:
        block, row = divmod(at, used)
        here = min(used - row, start + count - at)
        out.append((block, row, at - start, here))
        at += here
    return out


def kernel(
    in_ref,
    og_ref,
    gate_ref,
    up_ref,
    cot_ref,
    q_ref,
    p_out,
    q_out,
    gate_in,
    up_in,
    cot_in,
    acts,
    qs,
    mpart,
    mrecv,
    maway,
    mzrecv,
    bst,
    bt,
    bs,
    mall,
    yb,
    s2,
    r3,
    s3,
    zb,
    zs,
    ub,
    urecv,
    gmine,
    gsib,
    gall,
    ghalf,
    pf,
    ptf,
    img,
    qb,
    qcrecv,
    qh,
    qr,
    qx,
    qy,
    qf,
    loads,
    ms,
    mr,
    mzs,
    mzr,
    bsend,
    brecv,
    mas,
    mar,
    r3s,
    r3r,
    g3s,
    g3r,
    us,
    ur,
    gss,
    gsr,
    gps,
    gpr,
    ghs,
    ghr,
    g2s,
    g2r,
    g1s,
    g1r,
    gcs,
    gcr,
    izs,
    izr,
    ixs,
    ixr,
    qcs,
    qcr,
    qrs,
    qrr,
    qgs,
    qgr,
    qds,
    qdr,
):
    dp, mp = lax.axis_index("dp"), lax.axis_index("mp")
    core, zl = lax.rem(dp, 2), lax.div(dp, 2)
    zh, plane = lax.rem(mp, 2), lax.div(mp, 2)
    xx, yy = lax.div(plane, SIDE), lax.rem(plane, SIDE)
    z = zh * ZLO + zl
    on_diagonal = xx == yy
    sibling = (zl * 2 + 1 - core, mp)
    opposite = (dp, plane * 2 + 1 - zh)

    def plane_peer(index):
        return (dp, index * 2 + zh)

    def z_peer(index):
        return (lax.rem(index, ZLO) * 2 + core, plane * 2 + lax.div(index, ZLO))

    def side_peer(axis, index):
        along_x = (dp, (index * SIDE + yy) * 2 + zh)
        along_y = (dp, (xx * SIDE + index) * 2 + zh)
        return along_x if axis == 0 else along_y

    def side(axis):
        return xx if axis == 0 else yy

    def after(e):
        x = lax.rem(xx + lax.div(lax.rem(e, PLANE), SIDE), SIDE)
        y = lax.rem(yy + lax.rem(e, SIDE), SIDE)
        return lax.rem(core + lax.div(e, PLANE), 2), x * SIDE + y

    def before(e):
        x = lax.rem(xx + SIDE - lax.div(lax.rem(e, PLANE), SIDE), SIDE)
        y = lax.rem(yy + SIDE - lax.rem(e, SIDE), SIDE)
        return lax.rem(core + lax.div(e, PLANE), 2), x * SIDE + y

    def near_peer(place):
        return (zl * 2 + place[0], place[1] * 2 + zh)

    def remote(src, dst, send, recv, to):
        return pltpu.make_async_remote_copy(
            src_ref=src,
            dst_ref=dst,
            send_sem=send,
            recv_sem=recv,
            device_id=to,
            device_id_type=MESH,
        )

    def around(count, body, first=1):
        def step(index, carry):
            body(index)
            return carry

        lax.fori_loop(first, count, step, 0)

    pending = []

    def far_first(count, body):
        if count == NEAR:
            body(jnp.int32(PLANE))
            around(15, lambda i: body(PLANE + 1 + lax.rem(25 - i, 15)), first=0)
            around(15, lambda i: body(1 + lax.rem(25 - i, 15)), first=0)
        elif count == PLANE:
            around(15, lambda i: body(1 + lax.rem(25 - i, 15)), first=0)
        else:
            half = count // 2
            around(
                count - 1,
                lambda i: body(
                    half + (1 - 2 * lax.rem(i, 2)) * lax.div(i + 1, 2)
                ),
                first=0,
            )

    def drain(bytes_of, semaphore):
        pltpu.make_async_copy(bytes_of, bytes_of, semaphore).wait()

    def send(make, count, bytes_of, semaphore):
        far_first(count, lambda d: make(d).start())
        pending.append(lambda: drain(bytes_of, semaphore))

    def send_one(copy):
        copy.start()
        pending.append(copy.wait_send)

    def finish():
        while pending:
            pending.pop(0)()

    barrier = pltpu.get_barrier_semaphore()

    def greet(to):
        pl.semaphore_signal(barrier, inc=1, device_id=to, device_id_type=MESH)

    around(DEPTH, lambda d: greet(z_peer(lax.rem(z + d, DEPTH))))
    around(NEAR, lambda e: greet(near_peer(after(e))))

    quarter = PLANE // 2

    def load(half, part, which):
        chips = pl.ds(part * quarter, quarter)
        src, dst = (
            (gate_ref, gate_in),
            (up_ref, up_in),
            (cot_ref, cot_in),
        )[which]
        return pltpu.make_async_copy(
            src.at[chips, zh if half else 1 - zh],
            dst.at[half, chips],
            loads.at[half * 6 + part * 3 + which],
        )

    for half in range(2):
        for part in range(2):
            for which in range(3):
                load(half, part, which).start()

    place = 0
    for chip_type in (False, True):
        for chip in range(PLANE):
            if (chip // SIDE == chip % SIDE) != chip_type:
                continue
            for of_core in range(2):
                for array, tile in tiles_of(of_core, chip)[0]:
                    source = (in_ref, og_ref)[array]
                    bst[place] = source[:, tile * LANES : (tile + 1) * LANES].astype(F32)
                    place += 1

    def activate(half, i):
        rows = pl.ds(pl.multiple_of(i * ROWS, ROWS), ROWS)
        g = gate_in[half, i].astype(F32)
        u = up_in[half, i].astype(F32)
        e = cot_in[half, i].astype(F32)
        s = 1.0 / (1.0 + jnp.exp(-g))
        silu = g * s
        values = (e * u * s * (1.0 + g * (1.0 - s)), e * silu, silu * u)
        for k, value in enumerate(values):
            high, low = split(value)
            acts[k, half, 0, rows, :] = high
            acts[k, half, 1, rows, :] = low

    def b_copy(e, count):
        to = after(e)
        return remote(
            bst.at[pl.ds(staged(*to), count)],
            bt.at[e, pl.ds(0, count)],
            bsend.at[0],
            brecv.at[lax.div(e, PLANE)],
            near_peer(to),
        )

    def b_each(e, act, diagonal):
        @pl.when(diagonal)
        def _():
            act(b_copy(e, 3))

        @pl.when(jnp.logical_not(diagonal))
        def _():
            act(b_copy(e, 2))

    def to_diagonal(e):
        chip = after(e)[1]
        return lax.div(chip, SIDE) == lax.rem(chip, SIDE)

    q_high, q_low = split(q_ref[...])
    qs[...] = jnp.zeros_like(qs)
    qs[0:W, :] = q_high
    qs[LANES : LANES + W, :] = q_low

    lane = lax.broadcasted_iota(jnp.int32, (HALF, LANES), 1)

    def mix(half):
        for k in range(3):
            first = mm_t(acts[k, half, 0], qs[...])
            second = mm_t(acts[k, half, 1], qs[0:LANES, :])
            both = first[:, 0:LANES] + first[:, LANES:] + second
            if k == 0:
                mpart[half] = both
            else:
                mpart[half] = jnp.where(lane >= k * RANK, both, mpart[half])

    plane_rows = pl.ds(pl.multiple_of(plane * ROWS, ROWS), ROWS)

    def m_copy(half, d):
        to = after(d)[1]
        return remote(
            mpart.at[half, pl.ds(pl.multiple_of(to * ROWS, ROWS), ROWS)],
            mrecv.at[half, d - 1],
            ms.at[half],
            mr.at[half],
            plane_peer(to),
        )

    def m_send(half):
        send(lambda d: m_copy(half, d), PLANE, mrecv.at[half], ms.at[half])

    def m_sum(half):
        drain(mrecv.at[half], mr.at[half])
        return mpart[half, plane_rows, :] + jnp.sum(mrecv[half], axis=0)

    for half in range(2):
        for part in range(2):
            for which in range(3):
                load(half, part, which).wait()
            around(
                (part + 1) * quarter,
                lambda i: activate(half, i),
                first=part * quarter,
            )
        mix(half)
        if half == 0:
            pl.semaphore_wait(barrier, DEPTH - 1 + NEAR - 1)
        m_send(half)
        if half == 0:
            around(PLANE, lambda e: b_each(e, lambda c: c.start(), to_diagonal(e)))
    maway[...] = m_sum(0)
    mz_copy = remote(maway, mzrecv, mzs.at[0], mzr.at[0], opposite)
    send_one(mz_copy)
    around(
        NEAR, lambda e: b_each(e, lambda c: c.start(), to_diagonal(e)), first=PLANE
    )

    def b_sent():
        for count, here in ((3, on_diagonal), (2, jnp.logical_not(on_diagonal))):

            @pl.when(here)
            def _():
                drain(bst.at[pl.ds(0, 2 * TILES - count)], bsend.at[0])

    pending.append(b_sent)

    def b_receive(group):
        slots = pl.ds(1, PLANE - 1) if group == 0 else pl.ds(PLANE, PLANE)
        for count, here in ((3, on_diagonal), (2, jnp.logical_not(on_diagonal))):

            @pl.when(here)
            def _():
                drain(bt.at[slots, pl.ds(0, count)], brecv.at[group])

    mhome = m_sum(1)

    own_tiles = staged(core, plane)
    for tile in range(2):
        bt[0, tile] = bst[own_tiles + tile]

    @pl.when(on_diagonal)
    def _():
        bt[0, 2] = bst[own_tiles + 2]

    def round_rows(e):
        rows = pl.ds(pl.multiple_of(e * ROWS, ROWS), ROWS)
        for tile in range(2):
            bs[rows, tile * LANES : (tile + 1) * LANES] = bt[e, tile].astype(BF16)

        @pl.when(on_diagonal)
        def _():
            bs[rows, 2 * LANES :] = bt[e, 2].astype(BF16)

        @pl.when(jnp.logical_not(on_diagonal))
        def _():
            bs[rows, 2 * LANES :] = jnp.zeros((ROWS, LANES), BF16)

    b_receive(0)
    around(PLANE, round_rows, first=0)

    mz_copy.wait_recv()
    mall[0] = (mhome + mzrecv[...]) * (1.0 / GROUPS)

    def ma_copy(e):
        return remote(
            mall.at[0], mall.at[e], mas.at[0], mar.at[0], near_peer(after(e))
        )

    ma_bytes = mall.at[pl.ds(1, NEAR - 1)]
    send(ma_copy, NEAR, ma_bytes, mas.at[0])

    b_receive(1)
    around(NEAR, round_rows, first=PLANE)
    drain(ma_bytes, mar.at[0])

    m_turned = mall[...].reshape(NEAR * ROWS, LANES).T
    m_high, m_low = split(m_turned[0:W])
    both = mm(jnp.concatenate([m_high, m_low], axis=0), bs[...])
    yb[...] = both[0:W] + both[W:]
    middle = slice(LANES, 2 * LANES)
    nothing = jnp.zeros((RANK, LANES), F32)
    first_core = jnp.logical_and(jnp.logical_not(on_diagonal), core == 0)
    second_core = jnp.logical_and(jnp.logical_not(on_diagonal), core == 1)

    @pl.when(first_core)
    def _():
        s2[0:64, :] = yb[0:64, 0:LANES]
        s2[64:128, :] = yb[0:64, middle]

    @pl.when(second_core)
    def _():
        s2[0:64, :] = yb[0:64, 0:LANES]
        s2[64:96, :] = yb[64:96, middle]
        s2[96:128, :] = nothing

    @pl.when(on_diagonal)
    def _():
        s2[0:32, :] = yb[64:96, 0:LANES]
        s2[32:64, :] = yb[64:96, middle]
        s2[64:96, :] = yb[64:96, 2 * LANES :]
        s2[96:128, :] = nothing

    def r3_copy(d):
        to = lax.rem(z + d, DEPTH)
        return remote(
            s2.at[pl.ds(pl.multiple_of(to * 8, 8), 8)],
            r3.at[d - 1],
            r3s.at[0],
            r3r.at[0],
            z_peer(to),
        )

    send(r3_copy, DEPTH, r3, r3s.at[0])
    drain(r3, r3r.at[0])
    z_own = pl.ds(pl.multiple_of(z * 8, 8), 8)
    s3[z_own, :] = s2[z_own, :] + jnp.sum(r3[...], axis=0)

    def g3_copy(d):
        return remote(
            s3.at[z_own],
            s3.at[z_own],
            g3s.at[0],
            g3r.at[0],
            z_peer(lax.rem(z + d, DEPTH)),
        )

    g3_bytes = s3.at[pl.ds(0, SHARE - 8)]
    send(g3_copy, DEPTH, g3_bytes, g3s.at[0])
    drain(g3_bytes, g3r.at[0])


    zb[...] = jnp.zeros_like(zb)

    @pl.when(first_core)
    def _():
        zb[0:64, 0:LANES] = s3[0:64, :]
        zb[0:64, middle] = s3[64:128, :]

    @pl.when(second_core)
    def _():
        zb[0:64, 0:LANES] = s3[0:64, :]
        zb[64:96, middle] = s3[64:96, :]

    @pl.when(on_diagonal)
    def _():
        zb[64:96, 0:LANES] = s3[0:32, :]
        zb[64:96, middle] = s3[32:64, :]
        zb[64:96, 2 * LANES :] = s3[64:96, :]

    z_high, z_low = split(zb[...])
    zs[0:LANES, :] = z_high
    zs[LANES:, :] = z_low
    onto = mm_t(bs[...], zs[...])
    ub[...] = (onto[:, 0:LANES] + onto[:, LANES:]).reshape(NEAR, ROWS, LANES)

    def u_copy(e):
        return remote(
            ub.at[e], urecv.at[e - 1], us.at[0], ur.at[0], near_peer(before(e))
        )

    send(u_copy, NEAR, urecv, us.at[0])

    pf[core, xx, yy] = s3[...]

    def g2_copy(portion, d):
        axis = 1 - portion
        at = portion * 3 + d - 1
        block = pf.at[core, xx, yy, pl.ds(portion * 64, 64)]
        to = lax.rem(side(axis) + d, SIDE)
        return remote(block, block, g2s.at[at], g2r.at[at], side_peer(axis, to))

    def line(portion, index):
        rows = pl.ds(portion * 64, 64)
        if portion == 0:
            return pf.at[core, index, pl.ds(0, SIDE), rows]
        return pf.at[core, pl.ds(0, SIDE), index, rows]

    def g1_copy(portion, d):
        at = portion * 3 + d - 1
        block = line(portion, side(portion))
        to = lax.rem(side(portion) + d, SIDE)
        return remote(block, block, g1s.at[at], g1r.at[at], side_peer(portion, to))

    for portion in range(2):
        for d in (2, 1, 3):
            send_one(g2_copy(portion, d))


    gram = mm_t(zb[...], zb[...], HIGH)
    row_at = lax.broadcasted_iota(jnp.int32, (RANK, LANES), 0)
    lane_at = lax.broadcasted_iota(jnp.int32, (RANK, LANES), 1)
    beside = jnp.zeros((RANK, LANES), F32)
    for k in range(3):
        here = jnp.logical_and(lane_at >= k * RANK, lane_at < (k + 1) * RANK)
        beside = jnp.where(here, gram[k * RANK : (k + 1) * RANK], beside)
    gmine[...] = beside
    gs_copy = remote(gmine, gsib, gss.at[0], gsr.at[0], sibling)
    send_one(gs_copy)
    gs_copy.wait_recv()
    g_half = pl.ds(pl.multiple_of(core * 16, 16), 16)
    gall[plane] = gmine[g_half, :] + gsib[g_half, :]

    def gp_copy(d):
        return remote(
            gall.at[plane],
            gall.at[plane],
            gps.at[0],
            gpr.at[0],
            plane_peer(after(d)[1]),
        )

    far_first(PLANE, lambda d: gp_copy(d).start())
    gp_bytes = gall.at[pl.ds(0, PLANE - 1)]
    pending.append(lambda: drain(gp_bytes, gps.at[0]))

    drain(urecv, ur.at[0])
    img[1, plane_rows, :] = ub[0] + jnp.sum(urecv[...], axis=0)
    iz_copy = remote(
        img.at[1, plane_rows], img.at[0, plane_rows], izs.at[0], izr.at[0], opposite
    )
    send_one(iz_copy)

    def ix_copy(half, d):
        return remote(
            img.at[half, plane_rows],
            img.at[half, plane_rows],
            ixs.at[half],
            ixr.at[half],
            plane_peer(after(d)[1]),
        )

    def ix_bytes(half):
        return img.at[half, pl.ds(0, HALF - ROWS)]

    def ix_send(half):
        send(lambda d: ix_copy(half, d), PLANE, ix_bytes(half), ixs.at[half])

    def ix_receive(half):
        drain(ix_bytes(half), ixr.at[half])

    ix_send(1)

    for portion in range(2):
        for d in (1, 3, 2):
            g2_copy(portion, d).wait_recv()
        for d in (2, 1, 3):
            send_one(g1_copy(portion, d))

    drain(gp_bytes, gpr.at[0])
    ghalf[g_half, :] = jnp.sum(gall[...], axis=0)
    gh_copy = remote(
        ghalf.at[g_half], ghalf.at[g_half], ghs.at[0], ghr.at[0], sibling
    )
    send_one(gh_copy)
    gh_copy.wait_recv()

    left = [ghalf[...] for _ in range(3)]
    right = [(lane_at == row_at + k * RANK).astype(F32) for k in range(3)]
    def eliminate(j):
        for k in range(3):
            at = k * RANK + j
            pivot = left[k][j : j + 1, at : at + 1]
            column = left[k][:, at : at + 1] / pivot
            factor = jnp.where(row_at > j, column, 0.0)
            left[k] = left[k] - factor * left[k][j : j + 1, :]
            right[k] = right[k] - factor * right[k][j : j + 1, :]

    middle_step = RANK // 2
    for j in range(middle_step):
        eliminate(j)
    iz_copy.wait_recv()
    ix_send(0)
    for j in range(middle_step, RANK - 1):
        eliminate(j)
    inverse = []
    for k in range(3):
        diagonal = jnp.sum(
            jnp.where(lane_at == row_at + k * RANK, left[k], 0.0), axis=1, keepdims=True
        )
        inverse.append(right[k] / jnp.sqrt(diagonal))
    inverse.append(jnp.zeros((RANK, LANES), F32))
    inverse = jnp.concatenate(inverse, axis=0)

    for side_half in range(2):
        qb[side_half, QB_USED:QB, :] = jnp.zeros((QB - QB_USED, LANES), F32)
    for half in (1, 0):
        ix_receive(half)
        if half == 0:
            for portion in range(2):
                for d in (1, 3, 2):
                    g1_copy(portion, d).wait_recv()
            gc_copy = remote(
                pf.at[core], pf.at[core], gcs.at[0], gcr.at[0], sibling
            )
            send_one(gc_copy)
        images = mm_t(img[half], inverse, HIGH) * (1.0 / GROUPS)
        img_high, img_low = split(images.T)
        for k in range(3):
            rows = slice(k * RANK, (k + 1) * RANK)
            both = jnp.concatenate([img_high[rows], img_low[rows]], axis=0)
            first = mm(both, acts[k, half, 0])
            second = mm(img_high[rows], acts[k, half, 1])
            share = first[0:RANK] + first[RANK:] + second
            for tile in range(FFL // LANES):
                part = share[:, tile * LANES : (tile + 1) * LANES]
                for block, row, start, count in pieces(
                    tile * W + k * RANK, RANK, QB_USED
                ):
                    piece = part[start : start + count]
                    if half == 0:
                        piece = piece + qb[block, row : row + count, :]
                    qb[block, row : row + count, :] = piece

    qc_copy = remote(qb.at[1 - core], qcrecv, qcs.at[0], qcr.at[0], sibling)
    send_one(qc_copy)

    qc_copy.wait_recv()
    qh[...] = qb[core] + qcrecv[...]

    def zl_peer(index):
        return (index * 2 + core, mp)

    def q_rows(index):
        return pl.ds(pl.multiple_of(index * QS, 8), QS)

    across = lax.rem(zl + 4, ZLO)
    run_start = zl - lax.rem(zl, 4)

    def in_run(d):
        return run_start + lax.rem(zl + d, 4)

    def qr_copy(d, far):
        to = in_run(d)
        owner = lax.rem(to + 4, ZLO) if far else to
        return remote(
            qh.at[q_rows(owner)],
            qr.at[far, d - 1],
            qrs.at[far],
            qrr.at[far],
            zl_peer(to),
        )

    for far_chunk in (1, 0):
        for d in (2, 3, 1):
            qr_copy(d, far_chunk).start()

    q_own, q_across = q_rows(zl), q_rows(across)

    def qx_copy(far):
        return remote(
            qx.at[far],
            qy.at[1 - far],
            qrs.at[2 + far],
            qrr.at[3 - far],
            zl_peer(across),
        )

    for far_chunk, rows in ((1, q_across), (0, q_own)):
        drain(qr.at[far_chunk], qrr.at[far_chunk])
        qx[far_chunk] = qh[rows, :] + jnp.sum(qr[far_chunk], axis=0)
        qx_copy(far_chunk).start()

    gc_copy.wait_recv()

    for of_core in range(2):
        for chip in range(PLANE):
            for row, k, tile in tiles_of(of_core, chip)[1]:
                ptf[k * RANK : (k + 1) * RANK, tile * LANES : (tile + 1) * LANES] = pf[
                    of_core, chip // SIDE, chip % SIDE, row : row + RANK, :
                ]
    scaled = inverse[0:W, 0:W] * math.sqrt(D)

    def left_factor(tile, carry):
        at = pl.ds(pl.multiple_of(tile * 4 * LANES, LANES), 4 * LANES)
        p_out[:, at] = mm(scaled, ptf[:, at], HIGH)
        return carry

    lax.fori_loop(0, D // (4 * LANES), left_factor, 0)

    finish()

    def qg_copy(rows, kind, to):
        block = qf.at[core, rows]
        return remote(block, block, qgs.at[kind], qgr.at[kind], zl_peer(to))

    def run_rows(start):
        return qf.at[core, pl.ds(pl.multiple_of(start * QS, 8), 4 * QS)]

    def qd_copy(start, kind):
        block = run_rows(start)
        return remote(block, block, qds.at[kind], qdr.at[kind], sibling)

    for kind, rows in ((0, q_own), (1, q_across)):
        qx_copy(1 - kind).wait_recv()
        qf[core, rows, :] = qx[kind] + qy[kind]
        for d in (2, 3, 1):
            qg_copy(rows, kind, in_run(d)).start()
    run_bytes = qr.at[0]
    drain(run_bytes, qgr.at[0])
    send_one(qd_copy(run_start, 0))
    drain(run_bytes, qgr.at[1])
    send_one(qd_copy(4 - run_start, 1))
    for kind in range(2):
        drain(run_bytes, qrs.at[kind])
        qx_copy(kind).wait_send()
        drain(run_bytes, qgs.at[kind])
    for kind in range(2):
        qd_copy(run_start, kind).wait_recv()

    for tile in range(FFL // LANES):
        parts = [
            qf[half, row : row + count, :]
            for half, row, _, count in pieces(tile * W, W, QB_USED)
        ]
        whole = parts[0] if len(parts) == 1 else jnp.concatenate(parts, axis=0)
        q_out[:, tile * LANES : (tile + 1) * LANES] = whole

    finish()


def deliver(p_ref, q_ref, p_out, q_out, go):
    count = 6
    parts = [pl.ds(i * (W // count), W // count) for i in range(count)]
    copies = [
        pltpu.make_async_copy(p_ref.at[part], p_out.at[part], go.at[i])
        for i, part in enumerate(parts)
    ]
    copies.append(pltpu.make_async_copy(q_ref, q_out, go.at[count]))
    for copy in copies:
        copy.start()
    for copy in copies:
        copy.wait()


def on_device(inputs, out_grad, gate_pre, up_pre, hidden_grad, q_start):
    vmem = pl.BlockSpec(memory_space=pltpu.VMEM)
    far = pl.BlockSpec(memory_space=pl.ANY)
    buffers = [
        pltpu.VMEM((2, PLANE, ROWS, FFL), BF16),
        pltpu.VMEM((2, PLANE, ROWS, FFL), BF16),
        pltpu.VMEM((2, PLANE, ROWS, FFL), BF16),
        pltpu.VMEM((3, 2, 2, HALF, FFL), BF16),
        pltpu.VMEM((2 * LANES, FFL), BF16),
        pltpu.VMEM((2, HALF, LANES), F32),
        pltpu.VMEM((2, PLANE - 1, ROWS, LANES), F32),
        pltpu.VMEM((ROWS, LANES), F32),
        pltpu.VMEM((16, LANES), F32),
        pltpu.VMEM((2 * TILES, ROWS, LANES), F32),
        pltpu.VMEM((NEAR, 3, ROWS, LANES), F32),
        pltpu.VMEM((NEAR * ROWS, 3 * LANES), BF16),
        pltpu.VMEM((NEAR, ROWS, LANES), F32),
        pltpu.VMEM((W, 3 * LANES), F32),
        pltpu.VMEM((SHARE, LANES), F32),
        pltpu.VMEM((DEPTH - 1, 8, LANES), F32),
        pltpu.VMEM((SHARE, LANES), F32),
        pltpu.VMEM((LANES, 3 * LANES), F32),
        pltpu.VMEM((2 * LANES, 3 * LANES), BF16),
        pltpu.VMEM((NEAR, ROWS, LANES), F32),
        pltpu.VMEM((NEAR - 1, ROWS, LANES), F32),
        pltpu.VMEM((RANK, LANES), F32),
        pltpu.VMEM((RANK, LANES), F32),
        pltpu.VMEM((PLANE, 16, LANES), F32),
        pltpu.VMEM((RANK, LANES), F32),
        pltpu.VMEM((2, SIDE, SIDE, SHARE, LANES), F32),
        pltpu.VMEM((W, D), F32),
        pltpu.VMEM((2, HALF, LANES), F32),
        pltpu.VMEM((2, QB, LANES), F32),
        pltpu.VMEM((QB, LANES), F32),
        pltpu.VMEM((QB, LANES), F32),
        pltpu.VMEM((2, 3, QS, LANES), F32),
        pltpu.VMEM((2, QS, LANES), F32),
        pltpu.VMEM((2, QS, LANES), F32),
        pltpu.VMEM((2, QB, LANES), F32),
    ]
    counts = [12]
    counts += [2, 2, 1, 1]
    counts += [1, 2, 1, 1]
    counts += [1, 1, 1, 1]
    counts += [1, 1]
    counts += [1, 1, 1, 1, 1, 1]
    counts += [6, 6, 6, 6, 1, 1]
    counts += [1, 1, 2, 2]
    counts += [1, 1, 4, 4, 2, 2, 2, 2]
    flags = [pltpu.SemaphoreType.DMA((count,)) for count in counts]
    by_half = [
        array.reshape(PLANE, 2, ROWS, FFL) for array in (gate_pre, up_pre, hidden_grad)
    ]
    p_turned, q_turned = pl.pallas_call(
        kernel,
        out_shape=(pltpu.VMEM((W, D), F32), pltpu.VMEM((W, FFL), F32)),
        in_specs=[vmem, vmem, far, far, far, vmem],
        out_specs=(vmem, vmem),
        scratch_shapes=buffers + flags,
        compiler_params=pltpu.CompilerParams(
            collective_id=0, has_side_effects=True, vmem_limit_bytes=56 * 2**20
        ),
        name="power_step",
    )(inputs, out_grad, *by_half, q_start.T)
    shapes = (
        jax.ShapeDtypeStruct((W, D), F32),
        jax.ShapeDtypeStruct((W, FFL), F32),
    )
    p_turned, q_turned = pl.pallas_call(
        deliver,
        out_shape=shapes,
        in_specs=[vmem, vmem],
        out_specs=(far, far),
        scratch_shapes=[
            pltpu.SemaphoreType.DMA((7,)),
        ],
        name="deliver",
    )(
        pltpu.with_memory_space_constraint(p_turned, pltpu.VMEM),
        pltpu.with_memory_space_constraint(q_turned, pltpu.VMEM),
    )
    return p_turned.T, q_turned.T


def solution(mesh):
    in_specs = (
        P(("dp", "mp"), None),
        P(("dp", "mp"), None),
        P("dp", "mp"),
        P("dp", "mp"),
        P("dp", "mp"),
        P("mp", None),
    )
    out_specs = (P(), P("mp", None))
    return jax.shard_map(
        on_device, mesh=mesh, in_specs=in_specs, out_specs=out_specs, check_vma=False
    )
```

```python
import functools
import math

import jax
import jax.numpy as jnp
from jax import lax
from jax.experimental import pallas as pl
from jax.experimental.pallas import tpu as pltpu
from jax.sharding import PartitionSpec as P

MESH = pl.DeviceIdType.MESH
F32 = jnp.float32
BF16 = jnp.bfloat16
HIGH = lax.Precision.HIGHEST

D = 4608
TOK = 512
FFL = 1152
ROWS = 16
RANK = 32
W = 3 * RANK
LANES = 128
SIDE = 4
PLANE = SIDE * SIDE
ZLO = 8
DEPTH = 16
GROUPS = 16

TILES = D // LANES
NEAR = 2 * PLANE
SHARE = 128
QB = 448
QB_USED = 432
QS = QB // ZLO
HALF = TOK // 2


def split(value):
    high = value.astype(BF16)
    low = (value - high.astype(F32)).astype(BF16)
    return high, low


def mm(left, right, precision=None):
    return lax.dot_general(
        left,
        right,
        (((1,), (0,)), ((), ())),
        preferred_element_type=F32,
        precision=precision,
    )


def mm_t(left, right, precision=None):
    return lax.dot_general(
        left,
        right,
        (((1,), (1,)), ((), ())),
        preferred_element_type=F32,
        precision=precision,
    )


def tiles_of(core, plane):
    x, y = divmod(plane, SIDE)
    if x == y:
        first = 12 + 6 * x + 3 * core
        return (
            [(1, first + i) for i in range(3)],
            [(32 * i, 2, first + i) for i in range(3)],
        )
    at = plane - plane // (SIDE + 1) - 1
    if core == 0:
        return (
            [(0, 3 * at), (0, 3 * at + 1)],
            [
                (0, 0, 3 * at),
                (32, 1, 3 * at),
                (64, 0, 3 * at + 1),
                (96, 1, 3 * at + 1),
            ],
        )
    return (
        [(0, 3 * at + 2), (1, at)],
        [(0, 0, 3 * at + 2), (32, 1, 3 * at + 2), (64, 2, at)],
    )


def staged(core, plane):
    x, y = lax.div(plane, SIDE), lax.rem(plane, SIDE)
    at = plane - lax.div(plane, SIDE + 1) - 1
    return jnp.where(x == y, 48 + 6 * x + 3 * core, 4 * at + 2 * core)


def pieces(start, count, used):
    out = []
    at = start
    while at < start + count:
        block, row = divmod(at, used)
        here = min(used - row, start + count - at)
        out.append((block, row, at - start, here))
        at += here
    return out


def kernel(
    in_ref,
    og_ref,
    gate_ref,
    up_ref,
    cot_ref,
    q_ref,
    p_out,
    q_out,
    gate_in,
    up_in,
    cot_in,
    acts,
    qs,
    mpart,
    mrecv,
    maway,
    mzrecv,
    bst,
    bt,
    bs,
    mall,
    yb,
    s2,
    r3,
    s3,
    zb,
    zs,
    ub,
    urecv,
    gmine,
    gsib,
    gall,
    ghalf,
    pf,
    ptf,
    img,
    qb,
    qcrecv,
    qh,
    qr,
    qx,
    qy,
    qf,
    loads,
    ms,
    mr,
    mzs,
    mzr,
    bsend,
    brecv,
    mas,
    mar,
    r3s,
    r3r,
    g3s,
    g3r,
    us,
    ur,
    gss,
    gsr,
    gps,
    gpr,
    ghs,
    ghr,
    g2s,
    g2r,
    g1s,
    g1r,
    gcs,
    gcr,
    izs,
    izr,
    ixs,
    ixr,
    qcs,
    qcr,
    qrs,
    qrr,
    qgs,
    qgr,
    qds,
    qdr,
):
    dp, mp = lax.axis_index("dp"), lax.axis_index("mp")
    core, zl = lax.rem(dp, 2), lax.div(dp, 2)
    zh, plane = lax.rem(mp, 2), lax.div(mp, 2)
    xx, yy = lax.div(plane, SIDE), lax.rem(plane, SIDE)
    z = zh * ZLO + zl
    on_diagonal = xx == yy
    sibling = (zl * 2 + 1 - core, mp)
    opposite = (dp, plane * 2 + 1 - zh)

    def plane_peer(index):
        return (dp, index * 2 + zh)

    def z_peer(index):
        return (lax.rem(index, ZLO) * 2 + core, plane * 2 + lax.div(index, ZLO))

    def side_peer(axis, index):
        along_x = (dp, (index * SIDE + yy) * 2 + zh)
        along_y = (dp, (xx * SIDE + index) * 2 + zh)
        return along_x if axis == 0 else along_y

    def side(axis):
        return xx if axis == 0 else yy

    def after(e):
        x = lax.rem(xx + lax.div(lax.rem(e, PLANE), SIDE), SIDE)
        y = lax.rem(yy + lax.rem(e, SIDE), SIDE)
        return lax.rem(core + lax.div(e, PLANE), 2), x * SIDE + y

    def before(e):
        x = lax.rem(xx + SIDE - lax.div(lax.rem(e, PLANE), SIDE), SIDE)
        y = lax.rem(yy + SIDE - lax.rem(e, SIDE), SIDE)
        return lax.rem(core + lax.div(e, PLANE), 2), x * SIDE + y

    def near_peer(place):
        return (zl * 2 + place[0], place[1] * 2 + zh)

    def remote(src, dst, send, recv, to):
        return pltpu.make_async_remote_copy(
            src_ref=src,
            dst_ref=dst,
            send_sem=send,
            recv_sem=recv,
            device_id=to,
            device_id_type=MESH,
        )

    def around(count, body, first=1):
        def step(index, carry):
            body(index)
            return carry

        lax.fori_loop(first, count, step, 0)

    pending = []

    def far_first(count, body):
        if count == NEAR:
            body(jnp.int32(PLANE))
            around(15, lambda i: body(PLANE + 1 + lax.rem(25 - i, 15)), first=0)
            around(15, lambda i: body(1 + lax.rem(25 - i, 15)), first=0)
        elif count == PLANE:
            around(15, lambda i: body(1 + lax.rem(25 - i, 15)), first=0)
        else:
            half = count // 2
            around(
                count - 1,
                lambda i: body(
                    half + (1 - 2 * lax.rem(i, 2)) * lax.div(i + 1, 2)
                ),
                first=0,
            )

    def drain(bytes_of, semaphore):
        pltpu.make_async_copy(bytes_of, bytes_of, semaphore).wait()

    def send(make, count, bytes_of, semaphore):
        far_first(count, lambda d: make(d).start())
        pending.append(lambda: drain(bytes_of, semaphore))

    def send_one(copy):
        copy.start()
        pending.append(copy.wait_send)

    def finish():
        while pending:
            pending.pop(0)()

    barrier = pltpu.get_barrier_semaphore()

    def greet(to):
        pl.semaphore_signal(barrier, inc=1, device_id=to, device_id_type=MESH)

    around(DEPTH, lambda d: greet(z_peer(lax.rem(z + d, DEPTH))))
    around(NEAR, lambda e: greet(near_peer(after(e))))

    quarter = PLANE // 2

    def load(half, part, which):
        chips = pl.ds(part * quarter, quarter)
        src, dst = (
            (gate_ref, gate_in),
            (up_ref, up_in),
            (cot_ref, cot_in),
        )[which]
        return pltpu.make_async_copy(
            src.at[chips, zh if half else 1 - zh],
            dst.at[half, chips],
            loads.at[half * 6 + part * 3 + which],
        )

    for half in range(2):
        for part in range(2):
            for which in range(3):
                load(half, part, which).start()

    place = 0
    for chip_type in (False, True):
        for chip in range(PLANE):
            if (chip // SIDE == chip % SIDE) != chip_type:
                continue
            for of_core in range(2):
                for array, tile in tiles_of(of_core, chip)[0]:
                    source = (in_ref, og_ref)[array]
                    bst[place] = source[:, tile * LANES : (tile + 1) * LANES].astype(F32)
                    place += 1

    def activate(half, i):
        rows = pl.ds(pl.multiple_of(i * ROWS, ROWS), ROWS)
        g = gate_in[half, i].astype(F32)
        u = up_in[half, i].astype(F32)
        e = cot_in[half, i].astype(F32)
        s = 1.0 / (1.0 + jnp.exp(-g))
        silu = g * s
        values = (e * u * s * (1.0 + g * (1.0 - s)), e * silu, silu * u)
        for k, value in enumerate(values):
            high, low = split(value)
            acts[k, half, 0, rows, :] = high
            acts[k, half, 1, rows, :] = low

    def b_copy(e, count):
        to = after(e)
        return remote(
            bst.at[pl.ds(staged(*to), count)],
            bt.at[e, pl.ds(0, count)],
            bsend.at[0],
            brecv.at[lax.div(e, PLANE)],
            near_peer(to),
        )

    def b_each(e, act, diagonal):
        @pl.when(diagonal)
        def _():
            act(b_copy(e, 3))

        @pl.when(jnp.logical_not(diagonal))
        def _():
            act(b_copy(e, 2))

    def to_diagonal(e):
        chip = after(e)[1]
        return lax.div(chip, SIDE) == lax.rem(chip, SIDE)

    q_high, q_low = split(q_ref[...])
    qs[...] = jnp.zeros_like(qs)
    qs[0:W, :] = q_high
    qs[LANES : LANES + W, :] = q_low

    lane = lax.broadcasted_iota(jnp.int32, (HALF, LANES), 1)

    def mix(half):
        for k in range(3):
            first = mm_t(acts[k, half, 0], qs[...])
            second = mm_t(acts[k, half, 1], qs[0:LANES, :])
            both = first[:, 0:LANES] + first[:, LANES:] + second
            if k == 0:
                mpart[half] = both
            else:
                mpart[half] = jnp.where(lane >= k * RANK, both, mpart[half])

    plane_rows = pl.ds(pl.multiple_of(plane * ROWS, ROWS), ROWS)

    def m_copy(half, d):
        to = after(d)[1]
        return remote(
            mpart.at[half, pl.ds(pl.multiple_of(to * ROWS, ROWS), ROWS)],
            mrecv.at[half, d - 1],
            ms.at[half],
            mr.at[half],
            plane_peer(to),
        )

    def m_send(half):
        send(lambda d: m_copy(half, d), PLANE, mrecv.at[half], ms.at[half])

    def m_sum(half):
        drain(mrecv.at[half], mr.at[half])
        return mpart[half, plane_rows, :] + jnp.sum(mrecv[half], axis=0)

    for half in range(2):
        for part in range(2):
            for which in range(3):
                load(half, part, which).wait()
            around(
                (part + 1) * quarter,
                lambda i: activate(half, i),
                first=part * quarter,
            )
        mix(half)
        if half == 0:
            pl.semaphore_wait(barrier, DEPTH - 1 + NEAR - 1)
        m_send(half)
        if half == 0:
            around(PLANE, lambda e: b_each(e, lambda c: c.start(), to_diagonal(e)))
    maway[...] = m_sum(0)
    mz_copy = remote(maway, mzrecv, mzs.at[0], mzr.at[0], opposite)
    send_one(mz_copy)
    around(
        NEAR, lambda e: b_each(e, lambda c: c.start(), to_diagonal(e)), first=PLANE
    )

    def b_sent():
        for count, here in ((3, on_diagonal), (2, jnp.logical_not(on_diagonal))):

            @pl.when(here)
            def _():
                drain(bst.at[pl.ds(0, 2 * TILES - count)], bsend.at[0])

    pending.append(b_sent)

    def b_receive(group):
        slots = pl.ds(1, PLANE - 1) if group == 0 else pl.ds(PLANE, PLANE)
        for count, here in ((3, on_diagonal), (2, jnp.logical_not(on_diagonal))):

            @pl.when(here)
            def _():
                drain(bt.at[slots, pl.ds(0, count)], brecv.at[group])

    mhome = m_sum(1)

    own_tiles = staged(core, plane)
    for tile in range(2):
        bt[0, tile] = bst[own_tiles + tile]

    @pl.when(on_diagonal)
    def _():
        bt[0, 2] = bst[own_tiles + 2]

    def round_rows(e):
        rows = pl.ds(pl.multiple_of(e * ROWS, ROWS), ROWS)
        for tile in range(2):
            bs[rows, tile * LANES : (tile + 1) * LANES] = bt[e, tile].astype(BF16)

        @pl.when(on_diagonal)
        def _():
            bs[rows, 2 * LANES :] = bt[e, 2].astype(BF16)

        @pl.when(jnp.logical_not(on_diagonal))
        def _():
            bs[rows, 2 * LANES :] = jnp.zeros((ROWS, LANES), BF16)

    b_receive(0)
    around(PLANE, round_rows, first=0)

    mz_copy.wait_recv()
    mall[0] = (mhome + mzrecv[...]) * (1.0 / GROUPS)

    def ma_copy(e):
        return remote(
            mall.at[0], mall.at[e], mas.at[0], mar.at[0], near_peer(after(e))
        )

    ma_bytes = mall.at[pl.ds(1, NEAR - 1)]
    send(ma_copy, NEAR, ma_bytes, mas.at[0])

    b_receive(1)
    around(NEAR, round_rows, first=PLANE)
    drain(ma_bytes, mar.at[0])

    m_turned = mall[...].reshape(NEAR * ROWS, LANES).T
    m_high, m_low = split(m_turned[0:W])
    both = mm(jnp.concatenate([m_high, m_low], axis=0), bs[...])
    yb[...] = both[0:W] + both[W:]
    middle = slice(LANES, 2 * LANES)
    nothing = jnp.zeros((RANK, LANES), F32)
    first_core = jnp.logical_and(jnp.logical_not(on_diagonal), core == 0)
    second_core = jnp.logical_and(jnp.logical_not(on_diagonal), core == 1)

    @pl.when(first_core)
    def _():
        s2[0:64, :] = yb[0:64, 0:LANES]
        s2[64:128, :] = yb[0:64, middle]

    @pl.when(second_core)
    def _():
        s2[0:64, :] = yb[0:64, 0:LANES]
        s2[64:96, :] = yb[64:96, middle]
        s2[96:128, :] = nothing

    @pl.when(on_diagonal)
    def _():
        s2[0:32, :] = yb[64:96, 0:LANES]
        s2[32:64, :] = yb[64:96, middle]
        s2[64:96, :] = yb[64:96, 2 * LANES :]
        s2[96:128, :] = nothing

    def r3_copy(d):
        to = lax.rem(z + d, DEPTH)
        return remote(
            s2.at[pl.ds(pl.multiple_of(to * 8, 8), 8)],
            r3.at[d - 1],
            r3s.at[0],
            r3r.at[0],
            z_peer(to),
        )

    send(r3_copy, DEPTH, r3, r3s.at[0])
    drain(r3, r3r.at[0])
    z_own = pl.ds(pl.multiple_of(z * 8, 8), 8)
    s3[z_own, :] = s2[z_own, :] + jnp.sum(r3[...], axis=0)

    def g3_copy(d):
        return remote(
            s3.at[z_own],
            s3.at[z_own],
            g3s.at[0],
            g3r.at[0],
            z_peer(lax.rem(z + d, DEPTH)),
        )

    g3_bytes = s3.at[pl.ds(0, SHARE - 8)]
    send(g3_copy, DEPTH, g3_bytes, g3s.at[0])
    drain(g3_bytes, g3r.at[0])


    zb[...] = jnp.zeros_like(zb)

    @pl.when(first_core)
    def _():
        zb[0:64, 0:LANES] = s3[0:64, :]
        zb[0:64, middle] = s3[64:128, :]

    @pl.when(second_core)
    def _():
        zb[0:64, 0:LANES] = s3[0:64, :]
        zb[64:96, middle] = s3[64:96, :]

    @pl.when(on_diagonal)
    def _():
        zb[64:96, 0:LANES] = s3[0:32, :]
        zb[64:96, middle] = s3[32:64, :]
        zb[64:96, 2 * LANES :] = s3[64:96, :]

    z_high, z_low = split(zb[...])
    zs[0:LANES, :] = z_high
    zs[LANES:, :] = z_low
    onto = mm_t(bs[...], zs[...])
    ub[...] = (onto[:, 0:LANES] + onto[:, LANES:]).reshape(NEAR, ROWS, LANES)

    def u_copy(e):
        return remote(
            ub.at[e], urecv.at[e - 1], us.at[0], ur.at[0], near_peer(before(e))
        )

    send(u_copy, NEAR, urecv, us.at[0])

    pf[core, xx, yy] = s3[...]

    def g2_copy(portion, d):
        axis = 1 - portion
        at = portion * 3 + d - 1
        block = pf.at[core, xx, yy, pl.ds(portion * 64, 64)]
        to = lax.rem(side(axis) + d, SIDE)
        return remote(block, block, g2s.at[at], g2r.at[at], side_peer(axis, to))

    def line(portion, index):
        rows = pl.ds(portion * 64, 64)
        if portion == 0:
            return pf.at[core, index, pl.ds(0, SIDE), rows]
        return pf.at[core, pl.ds(0, SIDE), index, rows]

    def g1_copy(portion, d):
        at = portion * 3 + d - 1
        block = line(portion, side(portion))
        to = lax.rem(side(portion) + d, SIDE)
        return remote(block, block, g1s.at[at], g1r.at[at], side_peer(portion, to))


    gram = mm_t(zb[...], zb[...], HIGH)
    row_at = lax.broadcasted_iota(jnp.int32, (RANK, LANES), 0)
    lane_at = lax.broadcasted_iota(jnp.int32, (RANK, LANES), 1)
    beside = jnp.zeros((RANK, LANES), F32)
    for k in range(3):
        here = jnp.logical_and(lane_at >= k * RANK, lane_at < (k + 1) * RANK)
        beside = jnp.where(here, gram[k * RANK : (k + 1) * RANK], beside)
    gmine[...] = beside
    gs_copy = remote(gmine, gsib, gss.at[0], gsr.at[0], sibling)
    send_one(gs_copy)
    gs_copy.wait_recv()
    g_half = pl.ds(pl.multiple_of(core * 16, 16), 16)
    gall[plane] = gmine[g_half, :] + gsib[g_half, :]

    def gp_copy(d):
        return remote(
            gall.at[plane],
            gall.at[plane],
            gps.at[0],
            gpr.at[0],
            plane_peer(after(d)[1]),
        )

    far_first(PLANE, lambda d: gp_copy(d).start())
    gp_bytes = gall.at[pl.ds(0, PLANE - 1)]
    pending.append(lambda: drain(gp_bytes, gps.at[0]))

    for portion in range(2):
        for d in (2, 1, 3):
            send_one(g2_copy(portion, d))

    drain(urecv, ur.at[0])
    img[1, plane_rows, :] = ub[0] + jnp.sum(urecv[...], axis=0)
    iz_copy = remote(
        img.at[1, plane_rows], img.at[0, plane_rows], izs.at[0], izr.at[0], opposite
    )
    send_one(iz_copy)

    def ix_copy(half, d):
        return remote(
            img.at[half, plane_rows],
            img.at[half, plane_rows],
            ixs.at[half],
            ixr.at[half],
            plane_peer(after(d)[1]),
        )

    def ix_bytes(half):
        return img.at[half, pl.ds(0, HALF - ROWS)]

    def ix_send(half):
        send(lambda d: ix_copy(half, d), PLANE, ix_bytes(half), ixs.at[half])

    def ix_receive(half):
        drain(ix_bytes(half), ixr.at[half])

    ix_send(1)

    for portion in range(2):
        for d in (1, 3, 2):
            g2_copy(portion, d).wait_recv()
        for d in (2, 1, 3):
            send_one(g1_copy(portion, d))

    drain(gp_bytes, gpr.at[0])
    ghalf[g_half, :] = jnp.sum(gall[...], axis=0)
    gh_copy = remote(
        ghalf.at[g_half], ghalf.at[g_half], ghs.at[0], ghr.at[0], sibling
    )
    send_one(gh_copy)
    gh_copy.wait_recv()

    left = [ghalf[...] for _ in range(3)]
    right = [(lane_at == row_at + k * RANK).astype(F32) for k in range(3)]
    def eliminate(j):
        for k in range(3):
            at = k * RANK + j
            pivot = left[k][j : j + 1, at : at + 1]
            column = left[k][:, at : at + 1] / pivot
            factor = jnp.where(row_at > j, column, 0.0)
            left[k] = left[k] - factor * left[k][j : j + 1, :]
            right[k] = right[k] - factor * right[k][j : j + 1, :]

    middle_step = RANK // 2
    for j in range(middle_step):
        eliminate(j)
    iz_copy.wait_recv()
    ix_send(0)
    for j in range(middle_step, RANK - 1):
        eliminate(j)
    inverse = []
    for k in range(3):
        diagonal = jnp.sum(
            jnp.where(lane_at == row_at + k * RANK, left[k], 0.0), axis=1, keepdims=True
        )
        inverse.append(right[k] / jnp.sqrt(diagonal))
    inverse.append(jnp.zeros((RANK, LANES), F32))
    inverse = jnp.concatenate(inverse, axis=0)

    for side_half in range(2):
        qb[side_half, QB_USED:QB, :] = jnp.zeros((QB - QB_USED, LANES), F32)
    for half in (1, 0):
        ix_receive(half)
        if half == 0:
            for portion in range(2):
                for d in (1, 3, 2):
                    g1_copy(portion, d).wait_recv()
            gc_copy = remote(
                pf.at[core], pf.at[core], gcs.at[0], gcr.at[0], sibling
            )
            send_one(gc_copy)
        images = mm_t(img[half], inverse, HIGH) * (1.0 / GROUPS)
        img_high, img_low = split(images.T)
        for k in range(3):
            rows = slice(k * RANK, (k + 1) * RANK)
            both = jnp.concatenate([img_high[rows], img_low[rows]], axis=0)
            first = mm(both, acts[k, half, 0])
            second = mm(img_high[rows], acts[k, half, 1])
            share = first[0:RANK] + first[RANK:] + second
            for tile in range(FFL // LANES):
                part = share[:, tile * LANES : (tile + 1) * LANES]
                for block, row, start, count in pieces(
                    tile * W + k * RANK, RANK, QB_USED
                ):
                    piece = part[start : start + count]
                    if half == 0:
                        piece = piece + qb[block, row : row + count, :]
                    qb[block, row : row + count, :] = piece

    qc_copy = remote(qb.at[1 - core], qcrecv, qcs.at[0], qcr.at[0], sibling)
    send_one(qc_copy)

    qc_copy.wait_recv()
    qh[...] = qb[core] + qcrecv[...]

    def zl_peer(index):
        return (index * 2 + core, mp)

    def q_rows(index):
        return pl.ds(pl.multiple_of(index * QS, 8), QS)

    across = lax.rem(zl + 4, ZLO)
    run_start = zl - lax.rem(zl, 4)

    def in_run(d):
        return run_start + lax.rem(zl + d, 4)

    def qr_copy(d, far):
        to = in_run(d)
        owner = lax.rem(to + 4, ZLO) if far else to
        return remote(
            qh.at[q_rows(owner)],
            qr.at[far, d - 1],
            qrs.at[far],
            qrr.at[far],
            zl_peer(to),
        )

    for far_chunk in (1, 0):
        for d in (2, 3, 1):
            qr_copy(d, far_chunk).start()

    q_own, q_across = q_rows(zl), q_rows(across)

    def qx_copy(far):
        return remote(
            qx.at[far],
            qy.at[1 - far],
            qrs.at[2 + far],
            qrr.at[3 - far],
            zl_peer(across),
        )

    for far_chunk, rows in ((1, q_across), (0, q_own)):
        drain(qr.at[far_chunk], qrr.at[far_chunk])
        qx[far_chunk] = qh[rows, :] + jnp.sum(qr[far_chunk], axis=0)
        qx_copy(far_chunk).start()

    gc_copy.wait_recv()

    for of_core in range(2):
        for chip in range(PLANE):
            for row, k, tile in tiles_of(of_core, chip)[1]:
                ptf[k * RANK : (k + 1) * RANK, tile * LANES : (tile + 1) * LANES] = pf[
                    of_core, chip // SIDE, chip % SIDE, row : row + RANK, :
                ]
    scaled = inverse[0:W, 0:W] * math.sqrt(D)

    def left_factor(tile, carry):
        at = pl.ds(pl.multiple_of(tile * 4 * LANES, LANES), 4 * LANES)
        p_out[:, at] = mm(scaled, ptf[:, at], HIGH)
        return carry

    lax.fori_loop(0, D // (4 * LANES), left_factor, 0)

    finish()

    def qg_copy(rows, kind, to):
        block = qf.at[core, rows]
        return remote(block, block, qgs.at[kind], qgr.at[kind], zl_peer(to))

    def run_rows(start):
        return qf.at[core, pl.ds(pl.multiple_of(start * QS, 8), 4 * QS)]

    def qd_copy(start, kind):
        block = run_rows(start)
        return remote(block, block, qds.at[kind], qdr.at[kind], sibling)

    for kind, rows in ((0, q_own), (1, q_across)):
        qx_copy(1 - kind).wait_recv()
        qf[core, rows, :] = qx[kind] + qy[kind]
        for d in (2, 3, 1):
            qg_copy(rows, kind, in_run(d)).start()
    run_bytes = qr.at[0]
    drain(run_bytes, qgr.at[0])
    send_one(qd_copy(run_start, 0))
    drain(run_bytes, qgr.at[1])
    send_one(qd_copy(4 - run_start, 1))
    for kind in range(2):
        drain(run_bytes, qrs.at[kind])
        qx_copy(kind).wait_send()
        drain(run_bytes, qgs.at[kind])
    for kind in range(2):
        qd_copy(run_start, kind).wait_recv()

    for tile in range(FFL // LANES):
        parts = [
            qf[half, row : row + count, :]
            for half, row, _, count in pieces(tile * W, W, QB_USED)
        ]
        whole = parts[0] if len(parts) == 1 else jnp.concatenate(parts, axis=0)
        q_out[:, tile * LANES : (tile + 1) * LANES] = whole

    finish()


def deliver(p_ref, q_ref, p_out, q_out, go):
    count = 6
    parts = [pl.ds(i * (W // count), W // count) for i in range(count)]
    copies = [
        pltpu.make_async_copy(p_ref.at[part], p_out.at[part], go.at[i])
        for i, part in enumerate(parts)
    ]
    copies.append(pltpu.make_async_copy(q_ref, q_out, go.at[count]))
    for copy in copies:
        copy.start()
    for copy in copies:
        copy.wait()


def on_device(inputs, out_grad, gate_pre, up_pre, hidden_grad, q_start):
    vmem = pl.BlockSpec(memory_space=pltpu.VMEM)
    far = pl.BlockSpec(memory_space=pl.ANY)
    buffers = [
        pltpu.VMEM((2, PLANE, ROWS, FFL), BF16),
        pltpu.VMEM((2, PLANE, ROWS, FFL), BF16),
        pltpu.VMEM((2, PLANE, ROWS, FFL), BF16),
        pltpu.VMEM((3, 2, 2, HALF, FFL), BF16),
        pltpu.VMEM((2 * LANES, FFL), BF16),
        pltpu.VMEM((2, HALF, LANES), F32),
        pltpu.VMEM((2, PLANE - 1, ROWS, LANES), F32),
        pltpu.VMEM((ROWS, LANES), F32),
        pltpu.VMEM((16, LANES), F32),
        pltpu.VMEM((2 * TILES, ROWS, LANES), F32),
        pltpu.VMEM((NEAR, 3, ROWS, LANES), F32),
        pltpu.VMEM((NEAR * ROWS, 3 * LANES), BF16),
        pltpu.VMEM((NEAR, ROWS, LANES), F32),
        pltpu.VMEM((W, 3 * LANES), F32),
        pltpu.VMEM((SHARE, LANES), F32),
        pltpu.VMEM((DEPTH - 1, 8, LANES), F32),
        pltpu.VMEM((SHARE, LANES), F32),
        pltpu.VMEM((LANES, 3 * LANES), F32),
        pltpu.VMEM((2 * LANES, 3 * LANES), BF16),
        pltpu.VMEM((NEAR, ROWS, LANES), F32),
        pltpu.VMEM((NEAR - 1, ROWS, LANES), F32),
        pltpu.VMEM((RANK, LANES), F32),
        pltpu.VMEM((RANK, LANES), F32),
        pltpu.VMEM((PLANE, 16, LANES), F32),
        pltpu.VMEM((RANK, LANES), F32),
        pltpu.VMEM((2, SIDE, SIDE, SHARE, LANES), F32),
        pltpu.VMEM((W, D), F32),
        pltpu.VMEM((2, HALF, LANES), F32),
        pltpu.VMEM((2, QB, LANES), F32),
        pltpu.VMEM((QB, LANES), F32),
        pltpu.VMEM((QB, LANES), F32),
        pltpu.VMEM((2, 3, QS, LANES), F32),
        pltpu.VMEM((2, QS, LANES), F32),
        pltpu.VMEM((2, QS, LANES), F32),
        pltpu.VMEM((2, QB, LANES), F32),
    ]
    counts = [12]
    counts += [2, 2, 1, 1]
    counts += [1, 2, 1, 1]
    counts += [1, 1, 1, 1]
    counts += [1, 1]
    counts += [1, 1, 1, 1, 1, 1]
    counts += [6, 6, 6, 6, 1, 1]
    counts += [1, 1, 2, 2]
    counts += [1, 1, 4, 4, 2, 2, 2, 2]
    flags = [pltpu.SemaphoreType.DMA((count,)) for count in counts]
    by_half = [
        array.reshape(PLANE, 2, ROWS, FFL) for array in (gate_pre, up_pre, hidden_grad)
    ]
    p_turned, q_turned = pl.pallas_call(
        kernel,
        out_shape=(pltpu.VMEM((W, D), F32), pltpu.VMEM((W, FFL), F32)),
        in_specs=[vmem, vmem, far, far, far, vmem],
        out_specs=(vmem, vmem),
        scratch_shapes=buffers + flags,
        compiler_params=pltpu.CompilerParams(
            collective_id=0, has_side_effects=True, vmem_limit_bytes=56 * 2**20
        ),
        name="power_step",
    )(inputs, out_grad, *by_half, q_start.T)
    shapes = (
        jax.ShapeDtypeStruct((W, D), F32),
        jax.ShapeDtypeStruct((W, FFL), F32),
    )
    p_turned, q_turned = pl.pallas_call(
        deliver,
        out_shape=shapes,
        in_specs=[vmem, vmem],
        out_specs=(far, far),
        scratch_shapes=[
            pltpu.SemaphoreType.DMA((7,)),
        ],
        name="deliver",
    )(
        pltpu.with_memory_space_constraint(p_turned, pltpu.VMEM),
        pltpu.with_memory_space_constraint(q_turned, pltpu.VMEM),
    )
    return p_turned.T, q_turned.T


def solution(mesh):
    in_specs = (
        P(("dp", "mp"), None),
        P(("dp", "mp"), None),
        P("dp", "mp"),
        P("dp", "mp"),
        P("dp", "mp"),
        P("mp", None),
    )
    out_specs = (P(), P("mp", None))
    return jax.shard_map(
        on_device, mesh=mesh, in_specs=in_specs, out_specs=out_specs, check_vma=False
    )
```
